768 devices in a mesh: seg: 64 (over x, y, core), sub: 12 (over z).
Axes of the slice: x: 4, y: 8, z: 12, core: 2. Of those that a mesh axis runs over, the one named last changes fastest.
Arguments:
- fields: float32 [7, 2048, 1536], P(None, 'seg', 'sub'), may hold values from -1.5 to 3, as said below
- region_levels: int32 [64, 12], replicated, may hold values from 0 to 2, as said below
Outputs:
- new_fields: float32 [7, 2048, 1536], P(None, 'seg', 'sub')
The draws below stay inside these ranges and needn't reach their ends.
Inputs may be any that keep to these rules, and one draw needn't show every extreme that they name: `region_levels`: root regions sharing a side or a corner differ by at most one level; some root region is at level 2. `fields`: component 0 (density) lies between 1 and 3; tile entries in a tile's unused room are not read.
All inputs are finite; a program needn't handle non-finite values.
Results may differ from the reference program's by a relative error of at most 0.0003.
Values sent between devices are 32-bit elements; how exact they have to be, the bound alone decides.
No kernel may reach another device: no remote copies, remote signals or barrier semaphores. Data moves between devices by JAX's collectives and lax.ppermute only.
A program may use at most 64 MiB of HBM per device.

```python
import math
from functools import partial
import jax
import jax.numpy as jnp
from jax import lax

GRID_Y = 2048
GRID_X = 1536
N_SEG = 64
N_SUB = 12


def draw_fields(key, part):
    key = jax.random.fold_in(key, 5)
    keys = jax.random.split(key, 7)
    grid_shape = (GRID_Y, GRID_X)
    density = jnp.exp(jax.random.uniform(keys[0], grid_shape, jnp.float32, 0.0, math.log(3.0)))
    speed_x = 0.25 * jax.random.truncated_normal(keys[1], -2.0, 2.0, grid_shape, jnp.float32)
    speed_y = 0.25 * jax.random.truncated_normal(keys[2], -2.0, 2.0, grid_shape, jnp.float32)
    speed_z = 0.25 * jax.random.truncated_normal(keys[3], -2.0, 2.0, grid_shape, jnp.float32)
    field_z = 0.3 * jax.random.truncated_normal(keys[4], -2.0, 2.0, grid_shape, jnp.float32)
    face_x = 0.3 * jax.random.truncated_normal(keys[5], -2.0, 2.0, grid_shape, jnp.float32)
    face_y = 0.3 * jax.random.truncated_normal(keys[6], -2.0, 2.0, grid_shape, jnp.float32)
    return jnp.stack([density, density * speed_x, density * speed_y, density * speed_z, field_z, face_x, face_y]).astype(jnp.float32)


def draw_region_levels(key, part):
    key = jax.random.fold_in(key, 11)
    keys = jax.random.split(key, 2)
    seed_count = max(N_SEG // 2, 1)
    start_row = jax.random.randint(keys[0], (), 0, N_SEG)
    start_col = jax.random.randint(keys[1], (), 0, N_SUB)
    counter = jnp.arange(seed_count, dtype=jnp.int32)
    seed_rows = (start_row + 2 * counter) % N_SEG
    seed_cols = (start_col + 5 * counter) % N_SUB
    row_gap = jnp.abs(jnp.arange(N_SEG, dtype=jnp.int32)[:, None] - seed_rows[None, :])
    row_gap = jnp.minimum(row_gap, N_SEG - row_gap)
    col_gap = jnp.abs(jnp.arange(N_SUB, dtype=jnp.int32)[:, None] - seed_cols[None, :])
    col_gap = jnp.minimum(col_gap, N_SUB - col_gap)
    distance = jnp.min(jnp.maximum(row_gap[:, None, :], col_gap[None, :, :]), axis=2)
    return (2 - jnp.minimum(distance, 2)).astype(jnp.int32)


def block_scale(rng, extent, cuts, smallest, high):
    gain, own = 1.0, jax.random.fold_in(rng, 6)
    for dim, parts in cuts:
        heights = jnp.exp(jax.random.uniform(jax.random.fold_in(own, dim), (parts,), jnp.float32, smallest / len(cuts), high / len(cuts)))
        gain = gain * jnp.repeat(heights, extent[dim] // parts).reshape([-1 if axis == dim else 1 for axis in range(len(extent))])
    return gain


def setup_inputs(seed: int = 0) -> dict:
    seeds = jax.random.split(jax.random.key(seed), 3)
    fields = draw_fields(jax.random.fold_in(seeds[2], 71), 0)
    region_levels = draw_region_levels(jax.random.fold_in(seeds[2], 71), 0)
    return dict(fields=fields, region_levels=region_levels)


SOUND_SQUARED = 1.0
STEP_SIZE = 0.08

def minmod(before_diff, after_diff):
    return 0.5 * (jnp.sign(before_diff) + jnp.sign(after_diff)) * jnp.minimum(jnp.abs(before_diff), jnp.abs(after_diff))

def riemann(left_state, right_state, normal):

    def pieces(values):
        density, speed_n, speed_t, speed_z, field_t, field_z = values
        field_square = normal * normal + field_t * field_t + field_z * field_z
        pressure = SOUND_SQUARED * density + 0.5 * field_square
        moment = density * speed_n
        fluxes = jnp.stack([moment, moment * speed_n + pressure - normal * normal, moment * speed_t - normal * field_t, moment * speed_z - normal * field_z, field_t * speed_n - normal * speed_t, field_z * speed_n - normal * speed_z])
        conserved = jnp.stack([density, moment, density * speed_t, density * speed_z, field_t, field_z])
        signal = jnp.abs(speed_n) + jnp.sqrt(SOUND_SQUARED + field_square / density)
        return (fluxes, conserved, signal)
    flux_left, cons_left, signal_left = pieces(left_state)
    flux_right, cons_right, signal_right = pieces(right_state)
    fastest = jnp.maximum(signal_left, signal_right)
    return 0.5 * (flux_left + flux_right) - 0.5 * fastest * (cons_right - cons_left)

def sweep_faces(primitives, normal):
    before_diff = primitives[:, :, 1:-1] - primitives[:, :, :-2]
    after_diff = primitives[:, :, 2:] - primitives[:, :, 1:-1]
    slopes = minmod(before_diff, after_diff)
    left_state = primitives[:, :, 1:-2] + 0.5 * slopes[:, :, :-1]
    right_state = primitives[:, :, 2:-1] - 0.5 * slopes[:, :, 1:]
    return riemann(left_state, right_state, normal[:, 2:-1])

def advance(ghosted, row_count, col_count, spacing):
    density = ghosted[0, :-1, :-1]
    speed_x = ghosted[1, :-1, :-1] / density
    speed_y = ghosted[2, :-1, :-1] / density
    speed_z = ghosted[3, :-1, :-1] / density
    field_z = ghosted[4, :-1, :-1]
    face_x = ghosted[5]
    face_y = ghosted[6]
    centre_x = 0.5 * (face_x[:-1, :-1] + face_x[:-1, 1:])
    centre_y = 0.5 * (face_y[:-1, :-1] + face_y[1:, :-1])
    along_x = sweep_faces(jnp.stack([density, speed_x, speed_y, speed_z, centre_y, field_z]), face_x[:-1, :-1])
    along_y = sweep_faces(jnp.stack([density, speed_y, speed_x, speed_z, centre_x, field_z]).transpose(0, 2, 1), face_y[:-1, :-1].T)
    step_ratio = STEP_SIZE / spacing
    flux_x = along_x[:, 3:row_count + 3, :]
    diff_x = flux_x[:, :, 2:col_count + 2] - flux_x[:, :, 1:col_count + 1]
    flux_y = along_y[:, 3:col_count + 3, :]
    diff_y = (flux_y[:, :, 2:row_count + 2] - flux_y[:, :, 1:row_count + 1]).transpose(0, 2, 1)
    change = jnp.stack([diff_x[0] + diff_y[0], diff_x[1] + diff_y[2], diff_x[2] + diff_y[1], diff_x[3] + diff_y[3], diff_x[5] + diff_y[5]])
    cell_update = ghosted[:5, 3:row_count + 3, 3:col_count + 3] - step_ratio * change
    edge_x = along_x[4, 2:row_count + 4, 1:col_count + 2]
    edge_y = along_y[4, 2:col_count + 4, 1:row_count + 2]
    edge_field = 0.25 * ((edge_y[1:] + edge_y[:-1]).T - (edge_x[1:] + edge_x[:-1]))
    return (cell_update, edge_field)

def halve_once(region_block):
    cell_part = 0.5 * (region_block[:5, 0::2, :] + region_block[:5, 1::2, :])
    cell_part = 0.5 * (cell_part[:, :, 0::2] + cell_part[:, :, 1::2])
    face_x = region_block[5, :, 0::2]
    face_x = 0.5 * (face_x[0::2] + face_x[1::2])
    face_y = region_block[6, 0::2, :]
    face_y = 0.5 * (face_y[:, 0::2] + face_y[:, 1::2])
    return jnp.concatenate([cell_part, face_x[None], face_y[None]], axis=0)

def coarsen(region_block, halvings):
    for repeat_count in range(halvings):
        region_block = halve_once(region_block)
    return region_block

def inject(region_tile, refine_level):
    factor = 4 >> refine_level
    row_count = region_tile.shape[1] // factor
    col_count = region_tile.shape[2] // factor
    part_used = region_tile[:, :row_count, :col_count]
    return jnp.repeat(jnp.repeat(part_used, factor, axis=1), factor, axis=2)

def publish_step(ghosted, refine_level, fine_rows, fine_cols):
    factor = 4 >> refine_level
    row_count = fine_rows // factor
    col_count = fine_cols // factor
    cell_update, edge_field = advance(ghosted, row_count, col_count, float(factor))
    cell_padded = jnp.zeros((5, fine_rows, fine_cols), jnp.float32).at[:, :row_count, :col_count].set(cell_update)
    published = jnp.zeros((fine_rows + 1, fine_cols + 1), jnp.float32).at[::factor, ::factor].set(edge_field)
    return (cell_padded, published)

def image_pass(window, refine_level, fine_rows, fine_cols):
    factor = 4 >> refine_level
    ghosted = coarsen(window, 2 - refine_level)
    margin = 12 // factor - 3
    ghosted = ghosted[:, margin:margin + fine_rows // factor + 6, margin:margin + fine_cols // factor + 6]
    return publish_step(ghosted, refine_level, fine_rows, fine_cols)

def corner(current, values_list, levels_list, refine_level):
    values = jnp.stack(values_list)
    levels = jnp.stack(levels_list)
    highest = jnp.max(levels)
    chosen = (levels == highest).astype(jnp.float32)
    average = jnp.sum(chosen * values) / jnp.sum(chosen)
    return jnp.where(highest > refine_level, average, current)

def correct(edge_field, halo_edges, near_levels, refine_level, factor, row_count, col_count):
    fine_rows = halo_edges.shape[0] - 3
    fine_cols = halo_edges.shape[1] - 3
    initial = edge_field
    bottom_line = halo_edges[0, 1:fine_cols + 2:factor]
    top_line = halo_edges[fine_rows + 2, 1:fine_cols + 2:factor]
    left_line = halo_edges[1:fine_rows + 2:factor, 0]
    right_line = halo_edges[1:fine_rows + 2:factor, fine_cols + 2]
    edge_field = edge_field.at[0, :].set(jnp.where(near_levels[0, 1] > refine_level, bottom_line, edge_field[0, :]))
    edge_field = edge_field.at[row_count, :].set(jnp.where(near_levels[2, 1] > refine_level, top_line, edge_field[row_count, :]))
    edge_field = edge_field.at[:, 0].set(jnp.where(near_levels[1, 0] > refine_level, left_line, edge_field[:, 0]))
    edge_field = edge_field.at[:, col_count].set(jnp.where(near_levels[1, 2] > refine_level, right_line, edge_field[:, col_count]))
    lower_left = corner(initial[0, 0], [halo_edges[0, 1], halo_edges[1, 0], halo_edges[0, 0]], [near_levels[0, 1], near_levels[1, 0], near_levels[0, 0]], refine_level)
    lower_right = corner(initial[0, col_count], [halo_edges[0, fine_cols + 1], halo_edges[1, fine_cols + 2], halo_edges[0, fine_cols + 2]], [near_levels[0, 1], near_levels[1, 2], near_levels[0, 2]], refine_level)
    upper_left = corner(initial[row_count, 0], [halo_edges[fine_rows + 2, 1], halo_edges[fine_rows + 1, 0], halo_edges[fine_rows + 2, 0]], [near_levels[2, 1], near_levels[1, 0], near_levels[2, 0]], refine_level)
    upper_right = corner(initial[row_count, col_count], [halo_edges[fine_rows + 2, fine_cols + 1], halo_edges[fine_rows + 1, fine_cols + 2], halo_edges[fine_rows + 2, fine_cols + 2]], [near_levels[2, 1], near_levels[1, 2], near_levels[2, 2]], refine_level)
    edge_field = edge_field.at[0, 0].set(lower_left)
    edge_field = edge_field.at[0, col_count].set(lower_right)
    edge_field = edge_field.at[row_count, 0].set(upper_left)
    edge_field = edge_field.at[row_count, col_count].set(upper_right)
    return edge_field

def faces_pass(cell_padded, published, halo_edges, current, start_fields, near_levels, refine_level, blending):
    fine_rows = current.shape[1]
    fine_cols = current.shape[2]
    factor = 4 >> refine_level
    row_count = fine_rows // factor
    col_count = fine_cols // factor
    edge_field = published[::factor, ::factor]
    edge_field = correct(edge_field, halo_edges, near_levels, refine_level, factor, row_count, col_count)
    step_ratio = STEP_SIZE / float(factor)
    face_x = current[5, :row_count, :col_count] - step_ratio * (edge_field[1:, :-1] - edge_field[:-1, :-1])
    face_y = current[6, :row_count, :col_count] + step_ratio * (edge_field[:-1, 1:] - edge_field[:-1, :-1])
    updated = jnp.concatenate([cell_padded[:, :row_count, :col_count], face_x[None], face_y[None]], axis=0)
    if blending:
        updated = 0.5 * (start_fields[:, :row_count, :col_count] + updated)
    return jnp.zeros((7, fine_rows, fine_cols), jnp.float32).at[:, :row_count, :col_count].set(updated)

def section(region_tiles, start_tiles, region_levels, blending):
    fine_rows = region_tiles.shape[3]
    fine_cols = region_tiles.shape[4]
    region_count = N_SEG * N_SUB
    injects = [partial(inject, refine_level=refine_level) for refine_level in range(3)]
    image_branches = [partial(image_pass, refine_level=refine_level, fine_rows=fine_rows, fine_cols=fine_cols) for refine_level in range(3)]
    face_branches = [partial(faces_pass, refine_level=refine_level, blending=blending) for refine_level in range(3)]

    def beside_all(region_index):
        seg_index = region_index // N_SUB
        sub_index = region_index % N_SUB
        rows_wanted = ((seg_index + jnp.arange(-1, 2, dtype=jnp.int32)) % N_SEG).astype(jnp.int32)
        cols_wanted = ((sub_index + jnp.arange(-1, 2, dtype=jnp.int32)) % N_SUB).astype(jnp.int32)
        return (seg_index, sub_index, rows_wanted, cols_wanted)

    def first_pass(region_index):
        seg_index, sub_index, rows_wanted, cols_wanted = beside_all(region_index)
        band_list = []
        for row_pos in range(3):
            strip_list = []
            for col_pos in range(3):
                neighbour_tile = region_tiles[rows_wanted[row_pos], cols_wanted[col_pos]]
                neighbour_level = region_levels[rows_wanted[row_pos], cols_wanted[col_pos]]
                strip_list.append(lax.switch(neighbour_level, injects, neighbour_tile))
            band_list.append(jnp.concatenate(strip_list, axis=2))
        assembled = jnp.concatenate(band_list, axis=1)
        window = assembled[:, fine_rows - 12:2 * fine_rows + 12, fine_cols - 12:2 * fine_cols + 12]
        return lax.switch(region_levels[seg_index, sub_index], image_branches, window)
    cell_all, publish_all = lax.map(first_pass, jnp.arange(region_count, dtype=jnp.int32))
    cell_all = cell_all.reshape(N_SEG, N_SUB, 5, fine_rows, fine_cols)
    publish_all = publish_all.reshape(N_SEG, N_SUB, fine_rows + 1, fine_cols + 1)

    def second_pass(region_index):
        seg_index, sub_index, rows_wanted, cols_wanted = beside_all(region_index)
        band_list = []
        for row_pos in range(3):
            strip_list = []
            for col_pos in range(3):
                strip_list.append(publish_all[rows_wanted[row_pos], cols_wanted[col_pos]])
            band_list.append(jnp.concatenate(strip_list, axis=1))
        assembled = jnp.concatenate(band_list, axis=0)
        halo_edges = assembled[fine_rows:2 * fine_rows + 3, fine_cols:2 * fine_cols + 3]
        near_levels = region_levels[rows_wanted][:, cols_wanted]
        return lax.switch(region_levels[seg_index, sub_index], face_branches, cell_all[seg_index, sub_index], publish_all[seg_index, sub_index], halo_edges, region_tiles[seg_index, sub_index], start_tiles[seg_index, sub_index], near_levels)
    result = lax.map(second_pass, jnp.arange(region_count, dtype=jnp.int32))
    return result.reshape(N_SEG, N_SUB, 7, fine_rows, fine_cols)

def reference(fields, region_levels):
    fine_rows = fields.shape[1] // N_SEG
    fine_cols = fields.shape[2] // N_SUB
    region_tiles = fields.reshape(7, N_SEG, fine_rows, N_SUB, fine_cols).transpose(1, 3, 0, 2, 4)
    midpoint = section(region_tiles, region_tiles, region_levels, False)
    final_tiles = section(midpoint, region_tiles, region_levels, True)
    return final_tiles.transpose(2, 0, 3, 1, 4).reshape(7, N_SEG * fine_rows, N_SUB * fine_cols)
```

```python
from functools import partial

import jax
import jax.numpy as jnp
from jax import lax
from jax.experimental import pallas as pl
from jax.experimental.pallas import tpu as pltpu
from jax.sharding import PartitionSpec as P

STEP_SIZE = 0.08
ROWS, COLS = 32, 128
F32 = jnp.float32
VMEM = pl.BlockSpec(memory_space=pltpu.VMEM)
SMEM = pl.BlockSpec(memory_space=pltpu.SMEM)

PAD = 8


def lane(rows):
    return lax.broadcasted_iota(jnp.int32, (rows, COLS), 1)


def gather_lanes(value, index):
    return jnp.take_along_axis(value, index, axis=1, mode="promise_in_bounds")


def near_level(levels_ref, row, col):
    seg_count, sub_count = levels_ref.shape
    s = lax.rem(lax.axis_index("seg") + (row + seg_count), seg_count)
    u = lax.rem(lax.axis_index("sub") + (col + sub_count), sub_count)
    return levels_ref[s, u]


def rows_kernel(levels_ref, fields_ref, low_ref, high_ref):
    start = 8 * (1 << near_level(levels_ref, 0, 0)) - 8
    for f in range(7):
        low_ref[f] = fields_ref[f, 0:8, :]
        high_ref[f] = fields_ref[f, pl.ds(pl.multiple_of(start, 8), 8), :]


def cols_kernel(levels_ref, fields_ref, below_ref, above_ref, out_ref):
    def pack(read, rows, level):
        p = lane(rows)
        first = 32 * (1 << level) - 8
        index = (p & 7) + jnp.where((p & 15) < 8, first, 0)
        packed = gather_lanes(read(0), index)
        for f in range(1, 7):
            packed = jnp.where((p >> 4) == f, gather_lanes(read(f), index), packed)
        return packed

    out_ref[0:8, :] = pack(lambda f: below_ref[f], 8, near_level(levels_ref, -1, 0))
    out_ref[8:40, :] = pack(lambda f: fields_ref[f], 32, near_level(levels_ref, 0, 0))
    out_ref[40:48, :] = pack(lambda f: above_ref[f], 8, near_level(levels_ref, 1, 0))


def minmod(a, b):
    return jnp.maximum(jnp.minimum(a, b), 0.0) + jnp.minimum(jnp.maximum(a, b), 0.0)


def side(state, normal):
    density, speed_n, speed_t, speed_z, field_t, field_z = state
    normal_square = normal * normal
    field_square = normal_square + field_t * field_t + field_z * field_z
    moment = density * speed_n
    fluxes = [
        moment,
        moment * speed_n + (density + 0.5 * field_square) - normal_square,
        moment * speed_t - normal * field_t,
        moment * speed_z - normal * field_z,
        field_t * speed_n - normal * speed_t,
        field_z * speed_n - normal * speed_z,
    ]
    conserved = [density, moment, density * speed_t, density * speed_z, field_t, field_z]
    signal = jnp.abs(speed_n) + jnp.sqrt(1.0 + field_square / density)
    return fluxes, conserved, signal


def riemann(left, right, normal):
    flux_left, cons_left, signal_left = side(left, normal)
    flux_right, cons_right, signal_right = side(right, normal)
    fastest = jnp.maximum(signal_left, signal_right)
    return [
        0.5 * ((a + b) - fastest * (d - c))
        for a, b, c, d in zip(flux_left, flux_right, cons_left, cons_right)
    ]


def main_kernel(
    levels_ref,
    fields_ref,
    below_ref,
    above_ref,
    left_ref,
    right_ref,
    out_ref,
    win,
    prim,
    lefty,
    diffx,
    fluxy,
    gx,
    edge,
    lev,
    corner,
    tmp,
):
    near = [[near_level(levels_ref, i, j) for j in (-1, 0, 1)] for i in (-1, 0, 1)]
    own_level = near[1][1]
    p32 = lane(32)
    p24 = lane(24)
    p16 = lane(16)
    p8 = lane(8)
    coarse32 = (p32 >= 72) & (p32 < 120)

    def by_cols(row, rows, kind):
        p = lane(rows)
        first, middle, last = near[row]
        if kind == 0:
            return jnp.full((rows, COLS), middle, jnp.int32)
        if kind == 1:
            return jnp.where(p < 64, last, first)
        inner = (p < 64) | ((p >= 80) & (p < 112))
        outer = ((p >= 64) & (p < 72)) | ((p >= 112) & (p < 120))
        return jnp.where(inner, middle, jnp.where(outer, last, first))

    for kind in range(2):
        lev[kind, 0:8, :] = by_cols(0, 8, kind)
        lev[kind, 8:40, :] = by_cols(1, 32, kind)
        lev[kind, 40:48, :] = by_cols(2, 8, kind)
    is_coarse = (p8 >= 72) & (p8 < 120)
    centre_row = by_cols(1, 8, 2)
    top_row = by_cols(2, 8, 2)
    lev[2, 0:8, :] = by_cols(0, 8, 2)
    lev[2, 8:16, :] = centre_row
    lev[2, 16:24, :] = jnp.where(is_coarse, top_row, centre_row)
    lev[2, 24:32, :] = top_row
    beside = lev[2, 0:32, :]
    beside = jnp.maximum(beside, pltpu.roll(beside, 1, 1))
    corner[...] = jnp.maximum(beside, pltpu.roll(beside, 1, 0))

    p48 = lane(48)
    strips = jnp.where((p48 & 15) < 8, left_ref[...], right_ref[...])
    strip = ((p8 >= 64) & (p8 < 80)) | (p8 >= 112)
    right_strip = ((p8 >= 64) & (p8 < 72)) | ((p8 >= 112) & (p8 < 120))
    strip_index = (p8 & 7) + jnp.where(right_strip, 8, 0)
    for f in range(7):
        win[f, 0, PAD : PAD + 8, :] = below_ref[f]
        win[f, 0, PAD + 8 : PAD + 40, :] = fields_ref[f]
        win[f, 0, PAD + 40 : PAD + 48, :] = above_ref[f]
        win[f, 1, PAD : PAD + 48, :] = pltpu.roll(strips, (120 - 16 * f) % 128, 1)
        index = strip_index + 16 * f
        packed = [gather_lanes(strips[r : r + 8], index) for r in (0, 8, 16, 40)]

        def joined(fine, coarse):
            return jnp.where(p8 < 72, fine, pltpu.roll(coarse, 80, 1))

        below, above = below_ref[f], above_ref[f]
        near_rows, next_rows = fields_ref[f, 0:8, :], fields_ref[f, 8:16, :]
        win[f, 2, PAD : PAD + 8, :] = jnp.where(strip, packed[0], joined(below, below))
        win[f, 2, PAD + 8 : PAD + 16, :] = jnp.where(
            strip, packed[1], joined(near_rows, near_rows)
        )
        win[f, 2, PAD + 16 : PAD + 24, :] = jnp.where(
            strip, jnp.where(is_coarse, packed[3], packed[2]), joined(next_rows, above)
        )
        win[f, 2, PAD + 24 : PAD + 32, :] = jnp.where(strip, packed[3], above)

    index_up_one = jnp.where(p32 < 72, 80 + (p32 >> 1), jnp.where(p32 >= 120, 16 + (p32 >> 1), p32))
    index_up_two = (p32 >> 1, 64 + (p32 >> 1))
    index_down_two = (2 * p24) & 127
    index_down_one = (2 * (p16 - 80)) & 127

    def doubled(value, first, count, slot):
        tmp[slot, 0:32, :] = value
        part = tmp[slot, pl.ds(first, count), :]
        tmp[slot + 1, pl.ds(0, count, stride=2), :] = part
        tmp[slot + 1, pl.ds(1, count, stride=2), :] = part
        return tmp[slot + 1, 0 : 2 * count, :]

    def rows_halved(ref, first, count, by_rows):
        initial = ref[pl.ds(first, count, stride=2), :]
        if not by_rows:
            return initial
        return 0.5 * (initial + ref[pl.ds(first + 1, count, stride=2), :])

    def cols_halved(value, by_cols):
        return 0.5 * (value + pltpu.roll(value, 127, 1)) if by_cols else value

    def down_two(ref0, ref1, first, by_rows, by_cols, slot):
        parts = [cols_halved(rows_halved(ref, first, 24, by_rows), by_cols) for ref in (ref0, ref1)]
        parts = [gather_lanes(part, index_down_two) for part in parts]
        tmp[slot, 4:28, :] = jnp.where(p24 < 64, parts[0], parts[1])
        return tmp[slot, 0:32, :]

    def down_one(ref, first, by_rows, by_cols, slot):
        part = cols_halved(rows_halved(ref, first, 16, by_rows), by_cols)
        tmp[slot, 4:20, :] = gather_lanes(part, index_down_one)
        return tmp[slot, 0:32, :]

    def share():
        level_b = lev[2, 0:32, :]
        fine_a = [lev[k, 0:48, :] == 2 for k in range(2)]
        for f in range(7):
            by_rows, by_cols = f != 6, f != 5
            value = win[f, 2, PAD : PAD + 32, :]
            injected = doubled(gather_lanes(value, index_up_one), 4, 16, 0)
            value = jnp.where((level_b == 0) & ~coarse32, injected, value)
            for k in range(2):
                injected = doubled(gather_lanes(value, index_up_two[k]), 4, 24, 2 + 2 * k)
                win[f, k, PAD : PAD + 48, :] = jnp.where(
                    fine_a[k], win[f, k, PAD : PAD + 48, :], injected
                )
            halved = down_two(win.at[f, 0], win.at[f, 1], PAD, by_rows, by_cols, 6)
            value = jnp.where((level_b == 2) & ~coarse32, halved, value)
            win[f, 2, PAD : PAD + 32, :] = value
            halved = down_one(win.at[f, 2], PAD, by_rows, by_cols, 7)
            win[f, 2, PAD : PAD + 32, :] = jnp.where((level_b >= 1) & coarse32, halved, value)

    def load(ref, fields, wide, row):
        if wide:
            return jnp.concatenate([ref[*fields, k, pl.ds(row, 8), :] for k in range(2)], axis=0)
        return ref[*fields, 2, pl.ds(row, 16), :]

    def store(ref, fields, wide, row, value):
        if wide:
            for k in range(2):
                ref[*fields, k, pl.ds(row, 8), :] = value[8 * k : 8 * k + 8]
        else:
            ref[*fields, 2, pl.ds(row, 16), :] = value

    def shifted(value, wide, back):
        moved = pltpu.roll(value, 1 if back else 127, 1)
        if not wide:
            return moved
        other = jnp.concatenate([moved[8:], moved[:8]], axis=0)
        return jnp.where(p16 == (0 if back else 127), other, moved)

    def over_chunks(body):
        for c in range(6):
            body(True, PAD + 8 * c)
        for c in range(2):
            body(False, PAD + 16 * c)

    def primitives(wide, row):
        inverse = 1.0 / load(win, (0,), wide, row)
        for i in range(3):
            store(prim, (i,), wide, row, load(win, (1 + i,), wide, row) * inverse)
        face_x = load(win, (5,), wide, row)
        store(prim, (3,), wide, row, 0.5 * (face_x + shifted(face_x, wide, False)))
        face_y = load(win, (6,), wide, row)
        store(prim, (4,), wide, row, 0.5 * (face_y + load(win, (6,), wide, row + 1)))

    RHO, VX, VY, VZ, CX, CY, BZ = (
        (win, 0),
        (prim, 0),
        (prim, 1),
        (prim, 2),
        (prim, 3),
        (prim, 4),
        (win, 4),
    )

    def sweeps(wide, row):
        def at(item, step=0):
            return load(item[0], (item[1],), wide, row + step)

        left, right = [], []
        for item in (RHO, VX, VY, VZ, CY, BZ):
            value = at(item)
            before = value - shifted(value, wide, True)
            slope = 0.5 * minmod(before, shifted(before, wide, False))
            left.append(shifted(value + slope, wide, True))
            right.append(value - slope)
        flux = riemann(left, right, at((win, 5)))
        for i, n in enumerate((0, 1, 2, 3, 5)):
            store(diffx, (i,), wide, row, shifted(flux[n], wide, False) - flux[n])
        flux_by = flux[4]
        store(gx, (), wide, row, flux_by)
        left, right = [], []
        for i, item in enumerate((RHO, VY, VX, VZ, CX, BZ)):
            value = at(item)
            slope = 0.5 * minmod(value - at(item, -1), at(item, 1) - value)
            store(lefty, (i,), wide, row, value + slope)
            left.append(load(lefty, (i,), wide, row - 1))
            right.append(value - slope)
        flux = riemann(left, right, at((win, 6)))
        for i, n in enumerate((0, 2, 1, 3, 5)):
            store(fluxy, (i,), wide, row, flux[n])
        flux_bx = flux[4]
        value = (flux_bx + shifted(flux_bx, wide, True)) - (flux_by + load(gx, (), wide, row - 1))
        store(edge, (), wide, row, 0.25 * value)

    ratio_b = jnp.where((p16 >= 72) & (p16 < 120), STEP_SIZE / 4, STEP_SIZE / 2)

    def correct():
        value = edge[2, PAD : PAD + 32, :]
        finest = corner[...]
        halved_two = down_two(edge.at[0], edge.at[1], PAD, False, False, 6)
        halved_one = down_one(edge.at[2], PAD, False, False, 7)
        value = jnp.where((finest == 2) & ~coarse32, halved_two, value)
        edge[2, PAD : PAD + 32, :] = jnp.where((finest >= 1) & coarse32, halved_one, value)

    def update(wide, row):
        ratio = STEP_SIZE if wide else ratio_b
        for i in range(5):
            change = load(diffx, (i,), wide, row) + (
                load(fluxy, (i,), wide, row + 1) - load(fluxy, (i,), wide, row)
            )
            store(win, (i,), wide, row, load(win, (i,), wide, row) - ratio * change)
        value = load(edge, (), wide, row)
        diff_x = load(edge, (), wide, row + 1) - value
        diff_y = shifted(value, wide, False) - value
        store(win, (5,), wide, row, load(win, (5,), wide, row) - ratio * diff_x)
        store(win, (6,), wide, row, load(win, (6,), wide, row) + ratio * diff_y)

    for _ in range(2):
        share()
        over_chunks(primitives)
        over_chunks(sweeps)
        correct()
        over_chunks(update)

    zero = jnp.zeros((8, COLS), F32)
    for f in range(7):
        for c in range(4):
            value = win[f, 0, PAD + 8 + 8 * c : PAD + 16 + 8 * c, :]
            if c < 2:
                medium = win[f, 2, PAD + 8 + 8 * c : PAD + 16 + 8 * c, :]
                coarse = pltpu.roll(medium, 48, 1) if c == 0 else zero
                lower = jnp.where(own_level == 1, medium, coarse)
                value = jnp.where(own_level == 2, value, lower)
            rows = 8 << own_level
            used = (8 * c < rows) & (p8 < (32 << own_level))
            blend = 0.5 * (fields_ref[f, 8 * c : 8 * c + 8, :] + value)
            out_ref[f, 8 * c : 8 * c + 8, :] = jnp.where(used, blend, 0.0)


def moved(value, axis, step):
    size = lax.axis_size(axis)
    return lax.ppermute(value, axis, [(i, (i + step) % size) for i in range(size)])


def on_device(fields, region_levels):
    shape = jax.ShapeDtypeStruct
    params = pltpu.CompilerParams(vmem_limit_bytes=32 * 1024 * 1024)
    rows = shape((7, 8, COLS), F32)
    low, high = pl.pallas_call(
        rows_kernel, out_shape=(rows, rows), in_specs=[SMEM, VMEM], out_specs=(VMEM, VMEM)
    )(region_levels, fields)
    below = moved(high, "seg", 1)
    above = moved(low, "seg", -1)
    packed = pl.pallas_call(
        cols_kernel,
        out_shape=shape((48, COLS), F32),
        in_specs=[SMEM, VMEM, VMEM, VMEM],
        out_specs=VMEM,
        compiler_params=params,
    )(region_levels, fields, below, above)
    left = moved(packed, "sub", 1)
    right = moved(packed, "sub", -1)

    def window(*lead):
        return pltpu.VMEM((*lead, 3, PAD + 56, COLS), F32)

    return pl.pallas_call(
        main_kernel,
        out_shape=shape(fields.shape, F32),
        in_specs=[SMEM, VMEM, VMEM, VMEM, VMEM, VMEM],
        out_specs=VMEM,
        scratch_shapes=[
            window(7),
            window(5),
            window(6),
            window(5),
            window(5),
            window(),
            window(),
            pltpu.VMEM((3, 48, COLS), jnp.int32),
            pltpu.VMEM((32, COLS), jnp.int32),
            pltpu.VMEM((8, 48, COLS), F32),
        ],
        compiler_params=params,
    )(region_levels, fields, below, above, left, right)


def solution(mesh):
    placed = (P(None, "seg", "sub"), P())
    return jax.shard_map(
        on_device, mesh=mesh, in_specs=placed, out_specs=P(None, "seg", "sub"), check_vma=False
    )
```

```python
from functools import partial

import jax
import jax.numpy as jnp
from jax import lax
from jax.experimental import pallas as pl
from jax.experimental.pallas import tpu as pltpu
from jax.sharding import PartitionSpec as P

STEP_SIZE = 0.08
ROWS, COLS = 32, 128
F32 = jnp.float32
VMEM = pl.BlockSpec(memory_space=pltpu.VMEM)

PAD = 8


def lane(rows):
    return lax.broadcasted_iota(jnp.int32, (rows, COLS), 1)


def gather_lanes(value, index):
    return jnp.take_along_axis(value, index, axis=1, mode="promise_in_bounds")


def near_rows(levels_ref, held_ref):
    seg_count, sub_count = levels_ref.shape
    sub = lax.axis_index("sub")
    for i in range(3):
        s = lax.rem(lax.axis_index("seg") + (i - 1 + seg_count), seg_count)
        held_ref[8 * i : 8 * i + 1, 0:sub_count] = levels_ref[pl.ds(s, 1), :]

    def level_of(i, offset):
        row = jnp.broadcast_to(held_ref[8 * i : 8 * i + 1, :], (8, COLS))
        u = sub + offset
        u = jnp.where(u < 0, u + sub_count, jnp.where(u >= sub_count, u - sub_count, u))
        return gather_lanes(row, u)

    return level_of


def last_rows(ref, f, level):
    return jnp.where(
        level == 2, ref[f, 24:32, :], jnp.where(level == 1, ref[f, 8:16, :], ref[f, 0:8, :])
    )


def cols_kernel(levels_ref, fields_ref, below_ref, above_ref, out_ref, held):
    level_of = near_rows(levels_ref, held)
    p = lane(8)

    def pack(read, level):
        first = jnp.where(level == 2, 120, jnp.where(level == 1, 56, 24))
        index = (p & 7) + jnp.where((p & 15) < 8, first, 0)
        packed = gather_lanes(read(0), index)
        for f in range(1, 7):
            packed = jnp.where((p >> 4) == f, gather_lanes(read(f), index), packed)
        return packed

    none = jnp.zeros((8, COLS), jnp.int32)
    level = level_of(0, none)
    out_ref[0:8, :] = pack(lambda f: last_rows(below_ref, f, level), level)
    own = level_of(1, none)
    for r in range(0, 32, 8):
        out_ref[8 + r : 16 + r, :] = pack(lambda f: fields_ref[f, r : r + 8, :], own)
    out_ref[40:48, :] = pack(lambda f: above_ref[f, 0:8, :], level_of(2, none))


def minmod(a, b):
    return jnp.maximum(jnp.minimum(a, b), 0.0) + jnp.minimum(jnp.maximum(a, b), 0.0)


def side(state, normal):
    density, speed_n, speed_t, speed_z, field_t, field_z = state
    normal_square = normal * normal
    field_square = normal_square + field_t * field_t + field_z * field_z
    moment = density * speed_n
    fluxes = [
        moment,
        moment * speed_n + (density + 0.5 * field_square) - normal_square,
        moment * speed_t - normal * field_t,
        moment * speed_z - normal * field_z,
        field_t * speed_n - normal * speed_t,
        field_z * speed_n - normal * speed_z,
    ]
    conserved = [density, moment, density * speed_t, density * speed_z, field_t, field_z]
    signal = jnp.abs(speed_n) + jnp.sqrt(1.0 + field_square / density)
    return fluxes, conserved, signal


def riemann(left, right, normal):
    flux_left, cons_left, signal_left = side(left, normal)
    flux_right, cons_right, signal_right = side(right, normal)
    fastest = jnp.maximum(signal_left, signal_right)
    return [
        0.5 * ((a + b) - fastest * (d - c))
        for a, b, c, d in zip(flux_left, flux_right, cons_left, cons_right)
    ]


def main_kernel(
    levels_ref,
    fields_ref,
    below_ref,
    above_ref,
    left_ref,
    right_ref,
    out_ref,
    win,
    prim,
    lefty,
    diffx,
    fluxy,
    gx,
    edge,
    lev,
    corner,
    tmp,
    held,
):
    level_of = near_rows(levels_ref, held)
    p32 = lane(32)
    p24 = lane(24)
    p16 = lane(16)
    p8 = lane(8)
    coarse32 = (p32 >= 72) & (p32 < 120)

    inner = (p8 < 64) | ((p8 >= 80) & (p8 < 112))
    outer = ((p8 >= 64) & (p8 < 72)) | ((p8 >= 112) & (p8 < 120))
    middle = jnp.zeros((8, COLS), jnp.int32)
    offsets = (middle, jnp.where(p8 < 64, 1, -1), jnp.where(inner, 0, jnp.where(outer, 1, -1)))
    is_coarse = (p8 >= 72) & (p8 < 120)
    for kind in range(3):
        below_row, centre_row, above_row = (level_of(i, offsets[kind]) for i in range(3))
        lev[kind, 0:8, :] = below_row
        lev[kind, 8:16, :] = centre_row
        if kind == 2:
            lev[kind, 16:24, :] = jnp.where(is_coarse, above_row, centre_row)
            lev[kind, 24:32, :] = above_row
        else:
            for r in (16, 24, 32):
                lev[kind, r : r + 8, :] = centre_row
            lev[kind, 40:48, :] = above_row
    own_level = lev[0, 8:16, :]
    below_level = lev[0, 0:8, :]
    beside = lev[2, 0:32, :]
    beside = jnp.maximum(beside, pltpu.roll(beside, 1, 1))
    corner[...] = jnp.maximum(beside, pltpu.roll(beside, 1, 0))

    p48 = lane(48)
    strips = jnp.where((p48 & 15) < 8, left_ref[...], right_ref[...])
    strip = ((p8 >= 64) & (p8 < 80)) | (p8 >= 112)
    right_strip = ((p8 >= 64) & (p8 < 72)) | ((p8 >= 112) & (p8 < 120))
    strip_index = (p8 & 7) + jnp.where(right_strip, 8, 0)
    for f in range(7):
        below, above = last_rows(below_ref, f, below_level), above_ref[f, 0:8, :]
        win[f, 0, PAD : PAD + 8, :] = below
        win[f, 0, PAD + 8 : PAD + 40, :] = fields_ref[f]
        win[f, 0, PAD + 40 : PAD + 48, :] = above
        win[f, 1, PAD : PAD + 48, :] = pltpu.roll(strips, (120 - 16 * f) % 128, 1)
        index = strip_index + 16 * f
        packed = [gather_lanes(strips[r : r + 8], index) for r in (0, 8, 16, 40)]

        def joined(fine, coarse):
            return jnp.where(p8 < 72, fine, pltpu.roll(coarse, 80, 1))

        initial, second = fields_ref[f, 0:8, :], fields_ref[f, 8:16, :]
        win[f, 2, PAD : PAD + 8, :] = jnp.where(strip, packed[0], joined(below, below))
        win[f, 2, PAD + 8 : PAD + 16, :] = jnp.where(
            strip, packed[1], joined(initial, initial)
        )
        win[f, 2, PAD + 16 : PAD + 24, :] = jnp.where(
            strip, jnp.where(is_coarse, packed[3], packed[2]), joined(second, above)
        )
        win[f, 2, PAD + 24 : PAD + 32, :] = jnp.where(strip, packed[3], above)

    index_up_one = jnp.where(p32 < 72, 80 + (p32 >> 1), jnp.where(p32 >= 120, 16 + (p32 >> 1), p32))
    index_up_two = (p32 >> 1, 64 + (p32 >> 1))
    index_down_two = (2 * p24) & 127
    index_down_one = (2 * (p16 - 80)) & 127

    def doubled(value, first, count, slot):
        tmp[slot, 0:32, :] = value
        part = tmp[slot, pl.ds(first, count), :]
        tmp[slot + 1, pl.ds(0, count, stride=2), :] = part
        tmp[slot + 1, pl.ds(1, count, stride=2), :] = part
        return tmp[slot + 1, 0 : 2 * count, :]

    def rows_halved(ref, first, count, by_rows):
        initial = ref[pl.ds(first, count, stride=2), :]
        if not by_rows:
            return initial
        return 0.5 * (initial + ref[pl.ds(first + 1, count, stride=2), :])

    def cols_halved(value, by_cols):
        return 0.5 * (value + pltpu.roll(value, 127, 1)) if by_cols else value

    def down_two(ref0, ref1, first, by_rows, by_cols, slot):
        parts = [cols_halved(rows_halved(ref, first, 24, by_rows), by_cols) for ref in (ref0, ref1)]
        parts = [gather_lanes(part, index_down_two) for part in parts]
        tmp[slot, 4:28, :] = jnp.where(p24 < 64, parts[0], parts[1])
        return tmp[slot, 0:32, :]

    def down_one(ref, first, by_rows, by_cols, slot):
        part = cols_halved(rows_halved(ref, first, 16, by_rows), by_cols)
        tmp[slot, 4:20, :] = gather_lanes(part, index_down_one)
        return tmp[slot, 0:32, :]

    def share():
        level_b = lev[2, 0:32, :]
        fine_a = [lev[k, 0:48, :] == 2 for k in range(2)]
        for f in range(7):
            by_rows, by_cols = f != 6, f != 5
            value = win[f, 2, PAD : PAD + 32, :]
            injected = doubled(gather_lanes(value, index_up_one), 4, 16, 0)
            value = jnp.where((level_b == 0) & ~coarse32, injected, value)
            for k in range(2):
                injected = doubled(gather_lanes(value, index_up_two[k]), 4, 24, 2 + 2 * k)
                win[f, k, PAD : PAD + 48, :] = jnp.where(
                    fine_a[k], win[f, k, PAD : PAD + 48, :], injected
                )
            halved = down_two(win.at[f, 0], win.at[f, 1], PAD, by_rows, by_cols, 6)
            value = jnp.where((level_b == 2) & ~coarse32, halved, value)
            win[f, 2, PAD : PAD + 32, :] = value
            halved = down_one(win.at[f, 2], PAD, by_rows, by_cols, 7)
            win[f, 2, PAD : PAD + 32, :] = jnp.where((level_b >= 1) & coarse32, halved, value)

    def load(ref, fields, wide, row):
        if wide:
            return jnp.concatenate([ref[*fields, k, pl.ds(row, 8), :] for k in range(2)], axis=0)
        return ref[*fields, 2, pl.ds(row, 16), :]

    def store(ref, fields, wide, row, value):
        if wide:
            for k in range(2):
                ref[*fields, k, pl.ds(row, 8), :] = value[8 * k : 8 * k + 8]
        else:
            ref[*fields, 2, pl.ds(row, 16), :] = value

    def shifted(value, wide, back):
        moved = pltpu.roll(value, 1 if back else 127, 1)
        if not wide:
            return moved
        other = jnp.concatenate([moved[8:], moved[:8]], axis=0)
        return jnp.where(p16 == (0 if back else 127), other, moved)

    def over_chunks(body):
        for c in range(6):
            body(True, PAD + 8 * c)
        for c in range(2):
            body(False, PAD + 16 * c)

    def primitives(wide, row):
        inverse = 1.0 / load(win, (0,), wide, row)
        for i in range(3):
            store(prim, (i,), wide, row, load(win, (1 + i,), wide, row) * inverse)
        face_x = load(win, (5,), wide, row)
        store(prim, (3,), wide, row, 0.5 * (face_x + shifted(face_x, wide, False)))
        face_y = load(win, (6,), wide, row)
        store(prim, (4,), wide, row, 0.5 * (face_y + load(win, (6,), wide, row + 1)))

    RHO, VX, VY, VZ, CX, CY, BZ = (
        (win, 0),
        (prim, 0),
        (prim, 1),
        (prim, 2),
        (prim, 3),
        (prim, 4),
        (win, 4),
    )

    def sweeps(wide, row):
        def at(item, step=0):
            return load(item[0], (item[1],), wide, row + step)

        left, right = [], []
        for item in (RHO, VX, VY, VZ, CY, BZ):
            value = at(item)
            before = value - shifted(value, wide, True)
            slope = 0.5 * minmod(before, shifted(before, wide, False))
            left.append(shifted(value + slope, wide, True))
            right.append(value - slope)
        flux = riemann(left, right, at((win, 5)))
        for i, n in enumerate((0, 1, 2, 3, 5)):
            store(diffx, (i,), wide, row, shifted(flux[n], wide, False) - flux[n])
        flux_by = flux[4]
        store(gx, (), wide, row, flux_by)
        left, right = [], []
        for i, item in enumerate((RHO, VY, VX, VZ, CX, BZ)):
            value = at(item)
            slope = 0.5 * minmod(value - at(item, -1), at(item, 1) - value)
            store(lefty, (i,), wide, row, value + slope)
            left.append(load(lefty, (i,), wide, row - 1))
            right.append(value - slope)
        flux = riemann(left, right, at((win, 6)))
        for i, n in enumerate((0, 2, 1, 3, 5)):
            store(fluxy, (i,), wide, row, flux[n])
        flux_bx = flux[4]
        value = (flux_bx + shifted(flux_bx, wide, True)) - (flux_by + load(gx, (), wide, row - 1))
        store(edge, (), wide, row, 0.25 * value)

    ratio_b = jnp.where((p16 >= 72) & (p16 < 120), STEP_SIZE / 4, STEP_SIZE / 2)

    def correct():
        value = edge[2, PAD : PAD + 32, :]
        finest = corner[...]
        halved_two = down_two(edge.at[0], edge.at[1], PAD, False, False, 6)
        halved_one = down_one(edge.at[2], PAD, False, False, 7)
        value = jnp.where((finest == 2) & ~coarse32, halved_two, value)
        edge[2, PAD : PAD + 32, :] = jnp.where((finest >= 1) & coarse32, halved_one, value)

    def update(wide, row):
        ratio = STEP_SIZE if wide else ratio_b
        for i in range(5):
            change = load(diffx, (i,), wide, row) + (
                load(fluxy, (i,), wide, row + 1) - load(fluxy, (i,), wide, row)
            )
            store(win, (i,), wide, row, load(win, (i,), wide, row) - ratio * change)
        value = load(edge, (), wide, row)
        diff_x = load(edge, (), wide, row + 1) - value
        diff_y = shifted(value, wide, False) - value
        store(win, (5,), wide, row, load(win, (5,), wide, row) - ratio * diff_x)
        store(win, (6,), wide, row, load(win, (6,), wide, row) + ratio * diff_y)

    for _ in range(2):
        share()
        over_chunks(primitives)
        over_chunks(sweeps)
        correct()
        over_chunks(update)

    zero = jnp.zeros((8, COLS), F32)
    for f in range(7):
        for c in range(4):
            value = win[f, 0, PAD + 8 + 8 * c : PAD + 16 + 8 * c, :]
            if c < 2:
                medium = win[f, 2, PAD + 8 + 8 * c : PAD + 16 + 8 * c, :]
                coarse = pltpu.roll(medium, 48, 1) if c == 0 else zero
                lower = jnp.where(own_level == 1, medium, coarse)
                value = jnp.where(own_level == 2, value, lower)
            used = p8 < jnp.where(own_level == 2, 128, jnp.where(own_level == 1, 64, 32))
            used = used & (own_level >= (0, 1, 2, 2)[c])
            blend = 0.5 * (fields_ref[f, 8 * c : 8 * c + 8, :] + value)
            out_ref[f, 8 * c : 8 * c + 8, :] = jnp.where(used, blend, 0.0)


def moved(value, axis, step):
    size = lax.axis_size(axis)
    return lax.ppermute(value, axis, [(i, (i + step) % size) for i in range(size)])


def on_device(fields, region_levels):
    shape = jax.ShapeDtypeStruct
    params = pltpu.CompilerParams(vmem_limit_bytes=32 * 1024 * 1024)
    below = moved(fields, "seg", 1)
    above = moved(fields, "seg", -1)
    packed = pl.pallas_call(
        cols_kernel,
        out_shape=shape((48, COLS), F32),
        in_specs=[VMEM] * 4,
        out_specs=VMEM,
        scratch_shapes=[pltpu.VMEM((24, COLS), jnp.int32)],
        compiler_params=params,
    )(region_levels, fields, below, above)
    right = moved(packed, "sub", -1)
    left = moved(packed, "sub", 1)

    def window(*lead):
        return pltpu.VMEM((*lead, 3, PAD + 56, COLS), F32)

    return pl.pallas_call(
        main_kernel,
        out_shape=shape(fields.shape, F32),
        in_specs=[VMEM] * 6,
        out_specs=VMEM,
        scratch_shapes=[
            window(7),
            window(5),
            window(6),
            window(5),
            window(5),
            window(),
            window(),
            pltpu.VMEM((3, 48, COLS), jnp.int32),
            pltpu.VMEM((32, COLS), jnp.int32),
            pltpu.VMEM((8, 48, COLS), F32),
            pltpu.VMEM((24, COLS), jnp.int32),
        ],
        compiler_params=params,
    )(region_levels, fields, below, above, left, right)


def solution(mesh):
    placed = (P(None, "seg", "sub"), P())
    return jax.shard_map(
        on_device, mesh=mesh, in_specs=placed, out_specs=P(None, "seg", "sub"), check_vma=False
    )
```

```python
from functools import partial

import jax
import jax.numpy as jnp
from jax import lax
from jax.experimental import pallas as pl
from jax.experimental.pallas import tpu as pltpu
from jax.sharding import PartitionSpec as P

STEP_SIZE = 0.08
ROWS, COLS = 32, 128
F32 = jnp.float32
VMEM = pl.BlockSpec(memory_space=pltpu.VMEM)

PAD = 8
TPAD = 16
MID, SIDE = PAD + 48, PAD + 80


def lane(rows):
    return lax.broadcasted_iota(jnp.int32, (rows, COLS), 1)


def gather_lanes(value, index):
    return jnp.take_along_axis(value, index, axis=1, mode="promise_in_bounds")


def near_rows(levels_ref, held_ref):
    seg_count, sub_count = levels_ref.shape
    sub = lax.axis_index("sub")
    for i in range(3):
        s = lax.rem(lax.axis_index("seg") + (i - 1 + seg_count), seg_count)
        held_ref[8 * i : 8 * i + 1, 0:sub_count] = levels_ref[pl.ds(s, 1), :]

    def level_of(i, offset):
        row = jnp.broadcast_to(held_ref[8 * i : 8 * i + 1, :], (8, COLS))
        u = sub + offset
        u = jnp.where(u < 0, u + sub_count, jnp.where(u >= sub_count, u - sub_count, u))
        return gather_lanes(row, u)

    return level_of


def last_rows(ref, f, level):
    return jnp.where(
        level == 2, ref[f, 24:32, :], jnp.where(level == 1, ref[f, 8:16, :], ref[f, 0:8, :])
    )


def cols_kernel(levels_ref, fields_ref, below_ref, above_ref, out_ref, held):
    level_of = near_rows(levels_ref, held)
    p = lane(8)

    def pack(read, level):
        first = jnp.where(level == 2, 120, jnp.where(level == 1, 56, 24))
        index = (p & 7) + jnp.where((p & 15) < 8, first, 0)
        packed = gather_lanes(read(0), index)
        for f in range(1, 7):
            packed = jnp.where((p >> 4) == f, gather_lanes(read(f), index), packed)
        return packed

    none = jnp.zeros((8, COLS), jnp.int32)
    level = level_of(0, none)
    out_ref[0:8, :] = pack(lambda f: last_rows(below_ref, f, level), level)
    own = level_of(1, none)
    for r in range(0, 32, 8):
        out_ref[8 + r : 16 + r, :] = pack(lambda f: fields_ref[f, r : r + 8, :], own)
    out_ref[40:48, :] = pack(lambda f: above_ref[f, 0:8, :], level_of(2, none))


def minmod(a, b):
    return jnp.maximum(jnp.minimum(a, b), 0.0) + jnp.minimum(jnp.maximum(a, b), 0.0)


def side(state, normal):
    density, speed_n, speed_t, speed_z, field_t, field_z = state
    normal_square = normal * normal
    field_square = normal_square + field_t * field_t + field_z * field_z
    moment = density * speed_n
    fluxes = [
        moment,
        moment * speed_n + (density + 0.5 * field_square) - normal_square,
        moment * speed_t - normal * field_t,
        moment * speed_z - normal * field_z,
        field_t * speed_n - normal * speed_t,
        field_z * speed_n - normal * speed_z,
    ]
    conserved = [density, moment, density * speed_t, density * speed_z, field_t, field_z]
    signal = jnp.abs(speed_n) + jnp.sqrt(1.0 + field_square / density)
    return fluxes, conserved, signal


def riemann(left, right, normal):
    flux_left, cons_left, signal_left = side(left, normal)
    flux_right, cons_right, signal_right = side(right, normal)
    fastest = jnp.maximum(signal_left, signal_right)
    return [
        0.5 * ((a + b) - fastest * (d - c))
        for a, b, c, d in zip(flux_left, flux_right, cons_left, cons_right)
    ]


def main_kernel(
    levels_ref,
    fields_ref,
    below_ref,
    above_ref,
    right_ref,
    left_ref,
    out_ref,
    win,
    prim,
    lefty,
    fluxy,
    gx,
    diffx,
    edge,
    turned,
    leftx,
    fluxx,
    lev,
    corner,
    tmp,
    held,
):
    level_of = near_rows(levels_ref, held)
    p32, p24, p16, p8 = lane(32), lane(24), lane(16), lane(8)
    coarse32 = (p32 >= 72) & (p32 < 120)

    inner = (p8 < 64) | ((p8 >= 80) & (p8 < 112))
    outer = ((p8 >= 64) & (p8 < 72)) | ((p8 >= 112) & (p8 < 120))
    middle = jnp.zeros((8, COLS), jnp.int32)
    offsets = (middle, jnp.where(inner, 0, jnp.where(outer, 1, -1)), jnp.where(p8 < 64, 1, -1))
    is_coarse = (p8 >= 72) & (p8 < 120)
    for kind, first in enumerate((0, 48, 80)):
        below_row, centre_row, above_row = (level_of(i, offsets[kind]) for i in range(3))
        lev[first : first + 8, :] = below_row
        lev[first + 8 : first + 16, :] = centre_row
        if kind == 1:
            lev[first + 16 : first + 24, :] = jnp.where(is_coarse, above_row, centre_row)
            lev[first + 24 : first + 32, :] = above_row
        else:
            for r in (16, 24, 32):
                lev[first + r : first + r + 8, :] = centre_row
            lev[first + 40 : first + 48, :] = above_row
    own_level = lev[8:16, :]
    below_level = lev[0:8, :]
    beside = lev[48:80, :]
    beside = jnp.maximum(beside, pltpu.roll(beside, 1, 1))
    corner[...] = jnp.maximum(beside, pltpu.roll(beside, 1, 0))

    p48 = lane(48)
    strips = jnp.where((p48 & 15) < 8, left_ref[...], right_ref[...])
    strip = ((p8 >= 64) & (p8 < 80)) | (p8 >= 112)
    strip_index = (p8 & 7) + jnp.where(outer, 8, 0)
    for f in range(7):
        below, above = last_rows(below_ref, f, below_level), above_ref[f, 0:8, :]
        win[f, PAD : PAD + 8, :] = below
        win[f, PAD + 8 : PAD + 40, :] = fields_ref[f]
        win[f, PAD + 40 : PAD + 48, :] = above
        win[f, SIDE : SIDE + 48, :] = pltpu.roll(strips, (120 - 16 * f) % 128, 1)
        index = strip_index + 16 * f
        packed = [gather_lanes(strips[r : r + 8], index) for r in (0, 8, 16, 40)]

        def joined(fine, coarse):
            return jnp.where(p8 < 72, fine, pltpu.roll(coarse, 80, 1))

        initial, second = fields_ref[f, 0:8, :], fields_ref[f, 8:16, :]
        win[f, MID : MID + 8, :] = jnp.where(strip, packed[0], joined(below, below))
        win[f, MID + 8 : MID + 16, :] = jnp.where(strip, packed[1], joined(initial, initial))
        win[f, MID + 16 : MID + 24, :] = jnp.where(
            strip, jnp.where(is_coarse, packed[3], packed[2]), joined(second, above)
        )
        win[f, MID + 24 : MID + 32, :] = jnp.where(strip, packed[3], above)

    index_up_one = jnp.where(p32 < 72, 80 + (p32 >> 1), jnp.where(p32 >= 120, 16 + (p32 >> 1), p32))
    index_up_two = (p32 >> 1, 64 + (p32 >> 1))
    index_down_two = (2 * p24) & 127
    index_down_one = (2 * (p16 - 80)) & 127

    def doubled(value, first, count, slot):
        tmp[slot, 0:32, :] = value
        part = tmp[slot, pl.ds(first, count), :]
        tmp[slot + 1, pl.ds(0, count, stride=2), :] = part
        tmp[slot + 1, pl.ds(1, count, stride=2), :] = part
        return tmp[slot + 1, 0 : 2 * count, :]

    def rows_halved(ref, first, count, by_rows):
        initial = ref[pl.ds(first, count, stride=2), :]
        if not by_rows:
            return initial
        return 0.5 * (initial + ref[pl.ds(first + 1, count, stride=2), :])

    def cols_halved(value, by_cols):
        return 0.5 * (value + pltpu.roll(value, 127, 1)) if by_cols else value

    def down_two(ref, by_rows, by_cols, slot):
        parts = [
            cols_halved(rows_halved(ref, first, 24, by_rows), by_cols) for first in (PAD, SIDE)
        ]
        parts = [gather_lanes(part, index_down_two) for part in parts]
        tmp[slot, 4:28, :] = jnp.where(p24 < 64, parts[0], parts[1])
        return tmp[slot, 0:32, :]

    def down_one(ref, by_rows, by_cols, slot):
        part = cols_halved(rows_halved(ref, MID, 16, by_rows), by_cols)
        tmp[slot, 4:20, :] = gather_lanes(part, index_down_one)
        return tmp[slot, 0:32, :]

    def share():
        level_b = lev[48:80, :]
        for f in range(7):
            by_rows, by_cols = f != 6, f != 5
            value = win[f, MID : MID + 32, :]
            injected = doubled(gather_lanes(value, index_up_one), 4, 16, 0)
            value = jnp.where((level_b == 0) & ~coarse32, injected, value)
            for k, first in enumerate((0, 80)):
                injected = doubled(gather_lanes(value, index_up_two[k]), 4, 24, 2 + 2 * k)
                held_rows = slice(PAD + first, PAD + first + 48)
                win[f, held_rows, :] = jnp.where(
                    lev[first : first + 48, :] == 2, win[f, held_rows, :], injected
                )
            halved = down_two(win.at[f], by_rows, by_cols, 6)
            value = jnp.where((level_b == 2) & ~coarse32, halved, value)
            win[f, MID : MID + 32, :] = value
            halved = down_one(win.at[f], by_rows, by_cols, 7)
            win[f, MID : MID + 32, :] = jnp.where((level_b >= 1) & coarse32, halved, value)

    def swapped(value):
        outside = jnp.where(p8 < 48, pltpu.roll(value, 48, 1), pltpu.roll(value, 80, 1))
        return jnp.where((p8 >= 48) & (p8 < 80), value, outside)

    def turn(slot, value):
        value = value.T
        turned[slot, TPAD : TPAD + 128, :] = value
        turned[slot, TPAD - 8 : TPAD, :] = swapped(value[120:128])
        turned[slot, TPAD + 128 : TPAD + 136, :] = swapped(value[0:8])

    chunks = [PAD + 16 * c for c in range(8)]

    def primitives():
        for row in chunks:
            rows = slice(row, row + 16)
            inverse = 1.0 / win[0, rows, :]
            for i in range(3):
                prim[i, rows, :] = win[1 + i, rows, :] * inverse
            prim[3, rows, :] = 0.5 * (win[6, rows, :] + win[6, row + 1 : row + 17, :])
        sources = [(win, 0), (prim, 0), (prim, 1), (prim, 2), (prim, 3), (win, 4), (win, 5)]
        for slot, (ref, i) in enumerate(sources):
            turn(slot, ref[i, PAD : PAD + 128, :])
        face_x = turned.at[6]
        prim[4, PAD : PAD + 128, :] = (
            0.5 * (face_x[TPAD : TPAD + 128, :] + face_x[TPAD + 1 : TPAD + 129, :])
        ).T

    def sweep(items, lefts, row, count, normal):
        def at(item, step):
            ref, i = item
            return ref[i, row + step : row + step + count, :]

        left, right = [], []
        for i, item in enumerate(items):
            value = at(item, 0)
            slope = 0.5 * minmod(value - at(item, -1), at(item, 1) - value)
            lefts[i, row : row + count, :] = value + slope
            if normal is not None:
                left.append(lefts[i, row - 1 : row - 1 + count, :])
                right.append(value - slope)
        if normal is None:
            return None
        return riemann(left, right, at(normal, 0))

    def sweep_x():
        items = [(turned, i) for i in range(6)]
        sweep(items, leftx, TPAD - 8, 8, None)
        for row in [TPAD + 16 * c for c in range(9)]:
            count = 8 if row == TPAD + 128 else 16
            flux = sweep(items, leftx, row, count, (turned, 6))
            for i, value in enumerate(flux):
                fluxx[i, row : row + count, :] = value
        for i, n in enumerate((0, 1, 2, 3, 5)):
            value = fluxx[n, TPAD + 1 : TPAD + 129, :] - fluxx[n, TPAD : TPAD + 128, :]
            diffx[i, PAD : PAD + 128, :] = value.T
        gx[PAD : PAD + 128, :] = fluxx[4, TPAD : TPAD + 128, :].T

    def sweep_y():
        items = [(win, 0), (prim, 1), (prim, 0), (prim, 2), (prim, 4), (win, 4)]
        for row in chunks:
            flux = sweep(items, lefty, row, 16, (win, 6))
            for i, n in enumerate((0, 2, 1, 3, 5, 4)):
                fluxy[i, row : row + 16, :] = flux[n]

    def beside_cols(ref, row, back):
        parts = [ref[r : r + 8, :] for r in row]
        parts = [pltpu.roll(part, 1 if back else 127, 1) for part in parts]
        edge_lane = p8 == (0 if back else 127)
        return [
            jnp.where(edge_lane, parts[1], parts[0]),
            jnp.where(edge_lane, parts[0], parts[1]),
        ] + parts[2:]

    row_sets = [
        (PAD + 8 * c, SIDE + 8 * c) + ((MID + 8 * c,) if c < 4 else ()) for c in range(6)
    ]

    def edges():
        for rows in row_sets:
            shifted = beside_cols(fluxy.at[5], rows, True)
            for row, other in zip(rows, shifted):
                value = (fluxy[5, row : row + 8, :] + other) - (
                    gx[row : row + 8, :] + gx[row - 1 : row + 7, :]
                )
                edge[row : row + 8, :] = 0.25 * value

    def correct():
        value = edge[MID : MID + 32, :]
        finest = corner[...]
        halved_two = down_two(edge, False, False, 6)
        halved_one = down_one(edge, False, False, 7)
        value = jnp.where((finest == 2) & ~coarse32, halved_two, value)
        edge[MID : MID + 32, :] = jnp.where((finest >= 1) & coarse32, halved_one, value)

    def update():
        for rows in row_sets:
            shifted = beside_cols(edge, rows, False)
            for k, (row, other) in enumerate(zip(rows, shifted)):
                ratio = STEP_SIZE
                if k == 2:
                    ratio = jnp.where(is_coarse, STEP_SIZE / 4, STEP_SIZE / 2)
                part = slice(row, row + 8)
                for i in range(5):
                    change = diffx[i, part, :] + (fluxy[i, row + 1 : row + 9, :] - fluxy[i, part, :])
                    win[i, part, :] = win[i, part, :] - ratio * change
                value = edge[part, :]
                diff_x = edge[row + 1 : row + 9, :] - value
                win[5, part, :] = win[5, part, :] - ratio * diff_x
                win[6, part, :] = win[6, part, :] + ratio * (other - value)

    for _ in range(2):
        share()
        primitives()
        sweep_x()
        sweep_y()
        edges()
        correct()
        update()

    zero = jnp.zeros((8, COLS), F32)
    for f in range(7):
        for c in range(4):
            value = win[f, PAD + 8 + 8 * c : PAD + 16 + 8 * c, :]
            if c < 2:
                medium = win[f, MID + 8 + 8 * c : MID + 16 + 8 * c, :]
                coarse = pltpu.roll(medium, 48, 1) if c == 0 else zero
                lower = jnp.where(own_level == 1, medium, coarse)
                value = jnp.where(own_level == 2, value, lower)
            used = p8 < jnp.where(own_level == 2, 128, jnp.where(own_level == 1, 64, 32))
            used = used & (own_level >= (0, 1, 2, 2)[c])
            blend = 0.5 * (fields_ref[f, 8 * c : 8 * c + 8, :] + value)
            out_ref[f, 8 * c : 8 * c + 8, :] = jnp.where(used, blend, 0.0)


def moved(value, axis, step):
    size = lax.axis_size(axis)
    return lax.ppermute(value, axis, [(i, (i + step) % size) for i in range(size)])


def on_device(fields, region_levels):
    shape = jax.ShapeDtypeStruct
    params = pltpu.CompilerParams(vmem_limit_bytes=32 * 1024 * 1024)
    below = moved(fields, "seg", 1)
    above = moved(fields, "seg", -1)
    packed = pl.pallas_call(
        cols_kernel,
        out_shape=shape((48, COLS), F32),
        in_specs=[VMEM] * 4,
        out_specs=VMEM,
        scratch_shapes=[pltpu.VMEM((24, COLS), jnp.int32)],
        compiler_params=params,
    )(region_levels, fields, below, above)
    right = moved(packed, "sub", -1)
    left = moved(packed, "sub", 1)

    def window(*lead):
        return pltpu.VMEM((*lead, PAD + 136, COLS), F32)

    def across(*lead):
        return pltpu.VMEM((*lead, TPAD + 144, COLS), F32)

    return pl.pallas_call(
        main_kernel,
        out_shape=shape(fields.shape, F32),
        in_specs=[VMEM] * 6,
        out_specs=VMEM,
        scratch_shapes=[
            window(7),
            window(5),
            window(6),
            window(6),
            window(),
            window(5),
            window(),
            across(7),
            across(6),
            across(6),
            pltpu.VMEM((128, COLS), jnp.int32),
            pltpu.VMEM((32, COLS), jnp.int32),
            pltpu.VMEM((8, 48, COLS), F32),
            pltpu.VMEM((24, COLS), jnp.int32),
        ],
        compiler_params=params,
    )(region_levels, fields, below, above, right, left)


def solution(mesh):
    placed = (P(None, "seg", "sub"), P())
    return jax.shard_map(
        on_device, mesh=mesh, in_specs=placed, out_specs=P(None, "seg", "sub"), check_vma=False
    )
```

```python
from functools import partial

import jax
import jax.numpy as jnp
from jax import lax
from jax.experimental import pallas as pl
from jax.experimental.pallas import tpu as pltpu
from jax.sharding import PartitionSpec as P

STEP_SIZE = 0.08
ROWS, COLS = 32, 128
F32 = jnp.float32
VMEM = pl.BlockSpec(memory_space=pltpu.VMEM)

PAD = 8
TPAD = 16
MID, SIDE = PAD + 48, PAD + 80


def lane(rows):
    return lax.broadcasted_iota(jnp.int32, (rows, COLS), 1)


def gather_lanes(value, index):
    return jnp.take_along_axis(value, index, axis=1, mode="promise_in_bounds")


def near_rows(levels_ref, held_ref):
    seg_count, sub_count = levels_ref.shape
    sub = lax.axis_index("sub")
    for i in range(3):
        s = lax.rem(lax.axis_index("seg") + (i - 1 + seg_count), seg_count)
        held_ref[8 * i : 8 * i + 1, 0:sub_count] = levels_ref[pl.ds(s, 1), :]

    def level_of(i, offset):
        row = jnp.broadcast_to(held_ref[8 * i : 8 * i + 1, :], (8, COLS))
        u = sub + offset
        u = jnp.where(u < 0, u + sub_count, jnp.where(u >= sub_count, u - sub_count, u))
        return gather_lanes(row, u)

    return level_of


def last_rows(ref, f, level):
    return jnp.where(
        level == 2, ref[f, 24:32, :], jnp.where(level == 1, ref[f, 8:16, :], ref[f, 0:8, :])
    )


def packed_cols(read, level):
    p = lane(8)
    first = jnp.where(level == 2, 120, jnp.where(level == 1, 56, 24))
    index = (p & 7) + jnp.where((p & 15) < 8, first, 0)
    packed = gather_lanes(read(0), index)
    for f in range(1, 7):
        packed = jnp.where((p >> 4) == f, gather_lanes(read(f), index), packed)
    return packed


def own_kernel(levels_ref, fields_ref, lev, corner, cols_ref, held):
    level_of = near_rows(levels_ref, held)
    p8 = lane(8)
    inner = (p8 < 64) | ((p8 >= 80) & (p8 < 112))
    outer = ((p8 >= 64) & (p8 < 72)) | ((p8 >= 112) & (p8 < 120))
    middle = jnp.zeros((8, COLS), jnp.int32)
    offsets = (middle, jnp.where(inner, 0, jnp.where(outer, 1, -1)), jnp.where(p8 < 64, 1, -1))
    is_coarse = (p8 >= 72) & (p8 < 120)
    for kind, first in enumerate((0, 48, 80)):
        below_row, centre_row, above_row = (level_of(i, offsets[kind]) for i in range(3))
        lev[first : first + 8, :] = below_row
        lev[first + 8 : first + 16, :] = centre_row
        if kind == 1:
            lev[first + 16 : first + 24, :] = jnp.where(is_coarse, above_row, centre_row)
            lev[first + 24 : first + 32, :] = above_row
        else:
            for r in (16, 24, 32):
                lev[first + r : first + r + 8, :] = centre_row
            lev[first + 40 : first + 48, :] = above_row
    beside = lev[48:80, :]
    beside = jnp.maximum(beside, pltpu.roll(beside, 1, 1))
    corner[...] = jnp.maximum(beside, pltpu.roll(beside, 1, 0))
    own = lev[8:16, :]
    for r in range(0, 32, 8):
        cols_ref[r : r + 8, :] = packed_cols(lambda f: fields_ref[f, r : r + 8, :], own)


def cols_kernel(lev, cols_ref, far_ref, close_ref, out_ref, below_ref, above_ref):
    even = jnp.full((8, COLS), lax.rem(lax.axis_index("seg"), 2)) == 0
    below_level, above_level = lev[0:8, :], lev[40:48, :]
    for f in range(7):
        far, close = (last_rows(ref, f, below_level) for ref in (far_ref, close_ref))
        below_ref[f] = jnp.where(even, far, close)
        above_ref[f] = jnp.where(even, close_ref[f, 0:8, :], far_ref[f, 0:8, :])
    out_ref[0:8, :] = packed_cols(lambda f: below_ref[f], below_level)
    out_ref[8:40, :] = cols_ref[...]
    out_ref[40:48, :] = packed_cols(lambda f: above_ref[f], above_level)


def minmod(a, b):
    return jnp.maximum(jnp.minimum(a, b), 0.0) + jnp.minimum(jnp.maximum(a, b), 0.0)


def side(state, normal):
    density, speed_n, speed_t, speed_z, field_t, field_z = state
    normal_square = normal * normal
    field_square = normal_square + field_t * field_t + field_z * field_z
    moment = density * speed_n
    fluxes = [
        moment,
        moment * speed_n + (density + 0.5 * field_square) - normal_square,
        moment * speed_t - normal * field_t,
        moment * speed_z - normal * field_z,
        field_t * speed_n - normal * speed_t,
        field_z * speed_n - normal * speed_z,
    ]
    conserved = [density, moment, density * speed_t, density * speed_z, field_t, field_z]
    signal = jnp.abs(speed_n) + jnp.sqrt(1.0 + field_square / density)
    return fluxes, conserved, signal


def riemann(left, right, normal):
    flux_left, cons_left, signal_left = side(left, normal)
    flux_right, cons_right, signal_right = side(right, normal)
    fastest = jnp.maximum(signal_left, signal_right)
    return [
        0.5 * ((a + b) - fastest * (d - c))
        for a, b, c, d in zip(flux_left, flux_right, cons_left, cons_right)
    ]


def main_kernel(
    lev,
    corner,
    fields_ref,
    below_ref,
    above_ref,
    right_ref,
    left_ref,
    out_ref,
    win,
    prim,
    lefty,
    fluxy,
    gx,
    diffx,
    edge,
    turned,
    leftx,
    fluxx,
    tmp,
):
    p32, p24, p16, p8 = lane(32), lane(24), lane(16), lane(8)
    coarse32 = (p32 >= 72) & (p32 < 120)

    is_coarse = (p8 >= 72) & (p8 < 120)
    outer = ((p8 >= 64) & (p8 < 72)) | ((p8 >= 112) & (p8 < 120))
    own_level = lev[8:16, :]

    p48 = lane(48)
    strips = jnp.where((p48 & 15) < 8, left_ref[...], right_ref[...])
    strip = ((p8 >= 64) & (p8 < 80)) | (p8 >= 112)
    strip_index = (p8 & 7) + jnp.where(outer, 8, 0)
    for f in range(7):
        below, above = below_ref[f], above_ref[f]
        win[f, PAD : PAD + 8, :] = below
        win[f, PAD + 8 : PAD + 40, :] = fields_ref[f]
        win[f, PAD + 40 : PAD + 48, :] = above
        win[f, SIDE : SIDE + 48, :] = pltpu.roll(strips, (120 - 16 * f) % 128, 1)
        index = strip_index + 16 * f
        packed = [gather_lanes(strips[r : r + 8], index) for r in (0, 8, 16, 40)]

        def joined(fine, coarse):
            return jnp.where(p8 < 72, fine, pltpu.roll(coarse, 80, 1))

        initial, second = fields_ref[f, 0:8, :], fields_ref[f, 8:16, :]
        win[f, MID : MID + 8, :] = jnp.where(strip, packed[0], joined(below, below))
        win[f, MID + 8 : MID + 16, :] = jnp.where(strip, packed[1], joined(initial, initial))
        win[f, MID + 16 : MID + 24, :] = jnp.where(
            strip, jnp.where(is_coarse, packed[3], packed[2]), joined(second, above)
        )
        win[f, MID + 24 : MID + 32, :] = jnp.where(strip, packed[3], above)

    index_up_one = jnp.where(p32 < 72, 80 + (p32 >> 1), jnp.where(p32 >= 120, 16 + (p32 >> 1), p32))
    index_up_two = (p32 >> 1, 64 + (p32 >> 1))
    index_down_two = (2 * p24) & 127
    index_down_one = (2 * (p16 - 80)) & 127

    def doubled(value, first, count, slot):
        tmp[slot, 0:32, :] = value
        part = tmp[slot, pl.ds(first, count), :]
        tmp[slot + 1, pl.ds(0, count, stride=2), :] = part
        tmp[slot + 1, pl.ds(1, count, stride=2), :] = part
        return tmp[slot + 1, 0 : 2 * count, :]

    def rows_halved(ref, first, count, by_rows):
        initial = ref[pl.ds(first, count, stride=2), :]
        if not by_rows:
            return initial
        return 0.5 * (initial + ref[pl.ds(first + 1, count, stride=2), :])

    def cols_halved(value, by_cols):
        return 0.5 * (value + pltpu.roll(value, 127, 1)) if by_cols else value

    def down_two(ref, by_rows, by_cols, slot):
        parts = [
            cols_halved(rows_halved(ref, first, 24, by_rows), by_cols) for first in (PAD, SIDE)
        ]
        parts = [gather_lanes(part, index_down_two) for part in parts]
        tmp[slot, 4:28, :] = jnp.where(p24 < 64, parts[0], parts[1])
        return tmp[slot, 0:32, :]

    def down_one(ref, by_rows, by_cols, slot):
        part = cols_halved(rows_halved(ref, MID, 16, by_rows), by_cols)
        tmp[slot, 4:20, :] = gather_lanes(part, index_down_one)
        return tmp[slot, 0:32, :]

    def share():
        level_b = lev[48:80, :]
        for f in range(7):
            by_rows, by_cols = f != 6, f != 5
            value = win[f, MID : MID + 32, :]
            injected = doubled(gather_lanes(value, index_up_one), 4, 16, 0)
            value = jnp.where((level_b == 0) & ~coarse32, injected, value)
            for k, first in enumerate((0, 80)):
                injected = doubled(gather_lanes(value, index_up_two[k]), 4, 24, 2 + 2 * k)
                held_rows = slice(PAD + first, PAD + first + 48)
                win[f, held_rows, :] = jnp.where(
                    lev[first : first + 48, :] == 2, win[f, held_rows, :], injected
                )
            halved = down_two(win.at[f], by_rows, by_cols, 6)
            value = jnp.where((level_b == 2) & ~coarse32, halved, value)
            win[f, MID : MID + 32, :] = value
            halved = down_one(win.at[f], by_rows, by_cols, 7)
            win[f, MID : MID + 32, :] = jnp.where((level_b >= 1) & coarse32, halved, value)

    def swapped(value):
        outside = jnp.where(p8 < 48, pltpu.roll(value, 48, 1), pltpu.roll(value, 80, 1))
        return jnp.where((p8 >= 48) & (p8 < 80), value, outside)

    def turn(slot, value):
        value = value.T
        turned[slot, TPAD : TPAD + 128, :] = value
        turned[slot, TPAD - 8 : TPAD, :] = swapped(value[120:128])
        turned[slot, TPAD + 128 : TPAD + 136, :] = swapped(value[0:8])

    chunks = [PAD + 16 * c for c in range(8)]

    def primitives():
        for row in chunks:
            rows = slice(row, row + 16)
            inverse = 1.0 / win[0, rows, :]
            for i in range(3):
                prim[i, rows, :] = win[1 + i, rows, :] * inverse
            prim[3, rows, :] = 0.5 * (win[6, rows, :] + win[6, row + 1 : row + 17, :])
        sources = [(win, 0), (prim, 0), (prim, 1), (prim, 2), (prim, 3), (win, 4), (win, 5)]
        for slot, (ref, i) in enumerate(sources):
            turn(slot, ref[i, PAD : PAD + 128, :])
        face_x = turned.at[6]
        prim[4, PAD : PAD + 128, :] = (
            0.5 * (face_x[TPAD : TPAD + 128, :] + face_x[TPAD + 1 : TPAD + 129, :])
        ).T

    def sweep(items, lefts, row, count, normal):
        def at(item, step):
            ref, i = item
            return ref[i, row + step : row + step + count, :]

        left, right = [], []
        for i, item in enumerate(items):
            value = at(item, 0)
            slope = 0.5 * minmod(value - at(item, -1), at(item, 1) - value)
            lefts[i, row : row + count, :] = value + slope
            if normal is not None:
                left.append(lefts[i, row - 1 : row - 1 + count, :])
                right.append(value - slope)
        if normal is None:
            return None
        return riemann(left, right, at(normal, 0))

    def sweep_x():
        items = [(turned, i) for i in range(6)]
        sweep(items, leftx, TPAD - 8, 8, None)
        for row in [TPAD + 16 * c for c in range(9)]:
            count = 8 if row == TPAD + 128 else 16
            flux = sweep(items, leftx, row, count, (turned, 6))
            for i, value in enumerate(flux):
                fluxx[i, row : row + count, :] = value
        for i, n in enumerate((0, 1, 2, 3, 5)):
            value = fluxx[n, TPAD + 1 : TPAD + 129, :] - fluxx[n, TPAD : TPAD + 128, :]
            diffx[i, PAD : PAD + 128, :] = value.T
        gx[PAD : PAD + 128, :] = fluxx[4, TPAD : TPAD + 128, :].T

    def sweep_y():
        items = [(win, 0), (prim, 1), (prim, 0), (prim, 2), (prim, 4), (win, 4)]
        for row in chunks:
            flux = sweep(items, lefty, row, 16, (win, 6))
            for i, n in enumerate((0, 2, 1, 3, 5, 4)):
                fluxy[i, row : row + 16, :] = flux[n]

    def beside_cols(ref, row, back):
        parts = [ref[r : r + 8, :] for r in row]
        parts = [pltpu.roll(part, 1 if back else 127, 1) for part in parts]
        edge_lane = p8 == (0 if back else 127)
        return [
            jnp.where(edge_lane, parts[1], parts[0]),
            jnp.where(edge_lane, parts[0], parts[1]),
        ] + parts[2:]

    row_sets = [
        (PAD + 8 * c, SIDE + 8 * c) + ((MID + 8 * c,) if c < 4 else ()) for c in range(6)
    ]

    def edges():
        for rows in row_sets:
            shifted = beside_cols(fluxy.at[5], rows, True)
            for row, other in zip(rows, shifted):
                value = (fluxy[5, row : row + 8, :] + other) - (
                    gx[row : row + 8, :] + gx[row - 1 : row + 7, :]
                )
                edge[row : row + 8, :] = 0.25 * value

    def correct():
        value = edge[MID : MID + 32, :]
        finest = corner[...]
        halved_two = down_two(edge, False, False, 6)
        halved_one = down_one(edge, False, False, 7)
        value = jnp.where((finest == 2) & ~coarse32, halved_two, value)
        edge[MID : MID + 32, :] = jnp.where((finest >= 1) & coarse32, halved_one, value)

    def update():
        for rows in row_sets:
            shifted = beside_cols(edge, rows, False)
            for k, (row, other) in enumerate(zip(rows, shifted)):
                ratio = STEP_SIZE
                if k == 2:
                    ratio = jnp.where(is_coarse, STEP_SIZE / 4, STEP_SIZE / 2)
                part = slice(row, row + 8)
                for i in range(5):
                    change = diffx[i, part, :] + (fluxy[i, row + 1 : row + 9, :] - fluxy[i, part, :])
                    win[i, part, :] = win[i, part, :] - ratio * change
                value = edge[part, :]
                diff_x = edge[row + 1 : row + 9, :] - value
                win[5, part, :] = win[5, part, :] - ratio * diff_x
                win[6, part, :] = win[6, part, :] + ratio * (other - value)

    for _ in range(2):
        share()
        primitives()
        sweep_x()
        sweep_y()
        edges()
        correct()
        update()

    zero = jnp.zeros((8, COLS), F32)
    for f in range(7):
        for c in range(4):
            value = win[f, PAD + 8 + 8 * c : PAD + 16 + 8 * c, :]
            if c < 2:
                medium = win[f, MID + 8 + 8 * c : MID + 16 + 8 * c, :]
                coarse = pltpu.roll(medium, 48, 1) if c == 0 else zero
                lower = jnp.where(own_level == 1, medium, coarse)
                value = jnp.where(own_level == 2, value, lower)
            used = p8 < jnp.where(own_level == 2, 128, jnp.where(own_level == 1, 64, 32))
            used = used & (own_level >= (0, 1, 2, 2)[c])
            blend = 0.5 * (fields_ref[f, 8 * c : 8 * c + 8, :] + value)
            out_ref[f, 8 * c : 8 * c + 8, :] = jnp.where(used, blend, 0.0)


def moved(value, axis, step):
    size = lax.axis_size(axis)
    return lax.ppermute(value, axis, [(i, (i + step) % size) for i in range(size)])


def swapped_pairs(value, axis, first):
    size = lax.axis_size(axis)
    pairs = [(i, (i + 1) % size) for i in range(first, size, 2)]
    return lax.ppermute(value, axis, pairs + [(j, i) for i, j in pairs])


def on_device(fields, region_levels):
    shape = jax.ShapeDtypeStruct
    params = pltpu.CompilerParams(vmem_limit_bytes=32 * 1024 * 1024)
    far = swapped_pairs(fields, "seg", 1)
    close = swapped_pairs(fields, "seg", 0)
    lev, corner, cols = pl.pallas_call(
        own_kernel,
        out_shape=(
            shape((128, COLS), jnp.int32),
            shape((32, COLS), jnp.int32),
            shape((32, COLS), F32),
        ),
        in_specs=[VMEM] * 2,
        out_specs=(VMEM,) * 3,
        scratch_shapes=[pltpu.VMEM((24, COLS), jnp.int32)],
        compiler_params=params,
    )(region_levels, fields)
    rows = shape((7, 8, COLS), F32)
    packed, below, above = pl.pallas_call(
        cols_kernel,
        out_shape=(shape((48, COLS), F32), rows, rows),
        in_specs=[VMEM] * 4,
        out_specs=(VMEM,) * 3,
        compiler_params=params,
    )(lev, cols, far, close)
    right = moved(packed, "sub", -1)
    left = moved(packed, "sub", 1)

    def window(*lead):
        return pltpu.VMEM((*lead, PAD + 136, COLS), F32)

    def across(*lead):
        return pltpu.VMEM((*lead, TPAD + 144, COLS), F32)

    return pl.pallas_call(
        main_kernel,
        out_shape=shape(fields.shape, F32),
        in_specs=[VMEM] * 7,
        out_specs=VMEM,
        scratch_shapes=[
            window(7),
            window(5),
            window(6),
            window(6),
            window(),
            window(5),
            window(),
            across(7),
            across(6),
            across(6),
            pltpu.VMEM((8, 48, COLS), F32),
        ],
        compiler_params=params,
    )(lev, corner, fields, below, above, right, left)


def solution(mesh):
    placed = (P(None, "seg", "sub"), P())
    return jax.shard_map(
        on_device, mesh=mesh, in_specs=placed, out_specs=P(None, "seg", "sub"), check_vma=False
    )
```

```python
from functools import partial

import jax
import jax.numpy as jnp
from jax import lax
from jax.experimental import pallas as pl
from jax.experimental.pallas import tpu as pltpu
from jax.sharding import PartitionSpec as P

STEP_SIZE = 0.08
ROWS, COLS = 32, 128
F32 = jnp.float32
VMEM = pl.BlockSpec(memory_space=pltpu.VMEM)
HBM = pl.BlockSpec(memory_space=pltpu.HBM)

PAD = 8
TPAD = 16
MID, SIDE = PAD + 48, PAD + 80


def lane(rows):
    return lax.broadcasted_iota(jnp.int32, (rows, COLS), 1)


def gather_lanes(value, index):
    return jnp.take_along_axis(value, index, axis=1, mode="promise_in_bounds")


def near_rows(levels_ref, held_ref):
    sub_count, seg_count = levels_ref.shape
    for j in range(3):
        u = lax.rem(lax.axis_index("sub") + (j - 1 + sub_count), sub_count)
        held_ref[8 * j : 8 * j + 1, 0:seg_count] = levels_ref[pl.ds(u, 1), :]
    table = []
    for i in range(3):
        s = lax.rem(lax.axis_index("seg") + (i - 1 + seg_count), seg_count)
        s = jnp.full((8, COLS), s, jnp.int32)
        rows = [jnp.broadcast_to(held_ref[8 * j : 8 * j + 1, :], (8, COLS)) for j in range(3)]
        table.append([gather_lanes(row, s) for row in rows])

    def level_of(i, offset):
        first, middle, last = table[i]
        return jnp.where(offset < 0, first, jnp.where(offset > 0, last, middle))

    return level_of


def last_rows(ref, f, level):
    return jnp.where(
        level == 2, ref[f, 24:32, :], jnp.where(level == 1, ref[f, 8:16, :], ref[f, 0:8, :])
    )


def packed_cols(read, level):
    p = lane(8)
    first = jnp.where(level == 2, 120, jnp.where(level == 1, 56, 24))
    index = (p & 7) + jnp.where((p & 15) < 8, first, 0)
    packed = gather_lanes(read(0), index)
    for f in range(1, 7):
        packed = jnp.where((p >> 4) == f, gather_lanes(read(f), index), packed)
    return packed


def own_kernel(levels_hbm, fields_hbm, lev, lev_strips, corner, cols_ref, levels_ref, fields_ref, held, sems):
    copies = [
        pltpu.make_async_copy(levels_hbm, levels_ref, sems.at[0]),
        pltpu.make_async_copy(fields_hbm, fields_ref, sems.at[1]),
    ]
    for copy in copies:
        copy.start()
    copies[0].wait()
    level_of = near_rows(levels_ref, held)
    p8 = lane(8)
    inner = (p8 < 64) | ((p8 >= 80) & (p8 < 112))
    outer = ((p8 >= 64) & (p8 < 72)) | ((p8 >= 112) & (p8 < 120))
    middle = jnp.zeros((8, COLS), jnp.int32)
    offsets = (middle, jnp.where(inner, 0, jnp.where(outer, 1, -1)), jnp.where(p8 < 64, 1, -1))
    is_coarse = (p8 >= 72) & (p8 < 120)
    for kind, first in enumerate((0, 48, 80)):
        below_row, centre_row, above_row = (level_of(i, offsets[kind]) for i in range(3))
        lev[first : first + 8, :] = below_row
        lev[first + 8 : first + 16, :] = centre_row
        if kind == 1:
            lev[first + 16 : first + 24, :] = jnp.where(is_coarse, above_row, centre_row)
            lev[first + 24 : first + 32, :] = above_row
        else:
            for r in (16, 24, 32):
                lev[first + r : first + r + 8, :] = centre_row
            lev[first + 40 : first + 48, :] = above_row
    offset = jnp.where((p8 & 15) < 8, -1, 1)
    below_row, centre_row, above_row = (level_of(i, offset) for i in range(3))
    for first, count in ((0, 6), (48, 4), (80, 3)):
        for r in range(count):
            row = below_row if r == 0 else above_row if r == count - 1 else centre_row
            lev_strips[first + 8 * r : first + 8 * r + 8, :] = row
    beside = lev[48:80, :]
    beside = jnp.maximum(beside, pltpu.roll(beside, 1, 1))
    corner[...] = jnp.maximum(beside, pltpu.roll(beside, 1, 0))
    own = lev[8:16, :]
    copies[1].wait()
    for r in range(0, 32, 8):
        cols_ref[r : r + 8, :] = packed_cols(lambda f: fields_ref[f, r : r + 8, :], own)


def cols_kernel(lev, cols_ref, close_ref, far_ref, out_ref, below_ref, above_ref):
    even = jnp.full((8, COLS), lax.rem(lax.axis_index("seg"), 2)) == 0
    below_level, above_level = lev[0:8, :], lev[40:48, :]
    for f in range(7):
        far, close = (last_rows(ref, f, below_level) for ref in (far_ref, close_ref))
        below_ref[f] = jnp.where(even, far, close)
        above_ref[f] = jnp.where(even, close_ref[f, 0:8, :], far_ref[f, 0:8, :])
    out_ref[0:8, :] = packed_cols(lambda f: below_ref[f], below_level)
    out_ref[8:40, :] = cols_ref[...]
    out_ref[40:48, :] = packed_cols(lambda f: above_ref[f], above_level)


def minmod(a, b):
    return jnp.maximum(jnp.minimum(a, b), 0.0) + jnp.minimum(jnp.maximum(a, b), 0.0)


def side(state, normal):
    density, speed_n, speed_t, speed_z, field_t, field_z = state
    normal_square = normal * normal
    field_square = normal_square + field_t * field_t + field_z * field_z
    moment = density * speed_n
    fluxes = [
        moment,
        moment * speed_n + (density + 0.5 * field_square) - normal_square,
        moment * speed_t - normal * field_t,
        moment * speed_z - normal * field_z,
        field_t * speed_n - normal * speed_t,
        field_z * speed_n - normal * speed_z,
    ]
    conserved = [density, moment, density * speed_t, density * speed_z, field_t, field_z]
    signal = jnp.abs(speed_n) + jnp.sqrt(1.0 + field_square / density)
    return fluxes, conserved, signal


def riemann(left, right, normal):
    flux_left, cons_left, signal_left = side(left, normal)
    flux_right, cons_right, signal_right = side(right, normal)
    fastest = jnp.maximum(signal_left, signal_right)
    return [
        0.5 * ((a + b) - fastest * (d - c))
        for a, b, c, d in zip(flux_left, flux_right, cons_left, cons_right)
    ]


def doubled(part, tmp):
    count = part.shape[0]
    tmp[pl.ds(0, count, stride=2), :] = part
    tmp[pl.ds(1, count, stride=2), :] = part
    return tmp[0 : 2 * count, :]


def rows_halved(ref, first, count, by_rows):
    initial = ref[pl.ds(first, count, stride=2), :]
    if not by_rows:
        return initial
    return 0.5 * (initial + ref[pl.ds(first + 1, count, stride=2), :])


def cols_halved(value, by_cols):
    return 0.5 * (value + pltpu.roll(value, 127, 1)) if by_cols else value


def down_two(ref, firsts, by_rows, by_cols, tmp):
    p = lane(24)
    parts = [cols_halved(rows_halved(ref, first, 24, by_rows), by_cols) for first in firsts]
    parts = [gather_lanes(part, (2 * p) & 127) for part in parts]
    tmp[4:28, :] = parts[0] if len(parts) == 1 else jnp.where(p < 64, parts[0], parts[1])
    return tmp[0:32, :]


def down_one(ref, first, by_rows, by_cols, tmp):
    part = cols_halved(rows_halved(ref, first, 16, by_rows), by_cols)
    tmp[4:20, :] = gather_lanes(part, (2 * (lane(16) - 80)) & 127)
    return tmp[0:32, :]


def share_levels(win, lev, tmp, base, blocks):
    p32, p24, p16 = lane(32), lane(24), lane(16)
    coarse32 = (p32 >= 72) & (p32 < 120)
    mid = base + 48
    level_b = lev[48:80, :]
    up_one = jnp.where(p16 < 72, 80 + (p16 >> 1), jnp.where(p16 >= 120, 16 + (p16 >> 1), p16))
    up_two = (p24 >> 1, 64 + (p24 >> 1))
    for f in range(7):
        by_rows, by_cols = f != 6, f != 5
        slots = [tmp.at[8 * f + k] for k in range(5)]
        injected = doubled(gather_lanes(win[f, mid + 4 : mid + 20, :], up_one), slots[0])
        value = jnp.where((level_b == 0) & ~coarse32, injected, win[f, mid : mid + 32, :])
        win[f, mid : mid + 32, :] = value
        part = win[f, mid + 4 : mid + 28, :]
        for k, first in enumerate(blocks):
            injected = doubled(gather_lanes(part, up_two[k]), slots[1 + k])
            rows = slice(base + first, base + first + 48)
            win[f, rows, :] = jnp.where(lev[first : first + 48, :] == 2, win[f, rows, :], injected)
        firsts = [base + first for first in blocks]
        halved = down_two(win.at[f], firsts, by_rows, by_cols, slots[3])
        value = jnp.where((level_b == 2) & ~coarse32, halved, value)
        win[f, mid : mid + 32, :] = value
        halved = down_one(win.at[f], mid, by_rows, by_cols, slots[4])
        win[f, mid : mid + 32, :] = jnp.where((level_b >= 1) & coarse32, halved, value)


def rows_kernel(lev, fields_ref, below_ref, above_ref, win, tmp):
    p8 = lane(8)
    is_coarse = (p8 >= 72) & (p8 < 120)

    def joined(fine, coarse):
        return jnp.where(is_coarse, pltpu.roll(coarse, 80, 1), fine)

    for f in range(7):
        below, above = below_ref[f], above_ref[f]
        initial, second = fields_ref[f, 0:8, :], fields_ref[f, 8:16, :]
        win[f, 0:8, :] = below
        win[f, 8:40, :] = fields_ref[f]
        win[f, 40:48, :] = above
        win[f, 48:56, :] = joined(below, below)
        win[f, 56:64, :] = joined(initial, initial)
        win[f, 64:72, :] = joined(second, above)
        win[f, 72:80, :] = above
    share_levels(win, lev, tmp, 0, (0,))


def share_strips(strips, lev_strips, held, tmp):
    p = lane(24)
    k = p & 15
    up = (p - k) + jnp.where(k < 8, 4 + (k >> 1), 8 + ((k - 8) >> 1))
    down = (p - k) + ((2 * k - 8) & 15)
    held[0:48, :] = strips
    held[48:72, :] = strips[0:24]
    held[72:80, :] = strips[40:48]
    held[80:96, :] = strips[0:16]
    held[96:104, :] = strips[40:48]
    level_one = lev_strips[48:80, :]

    def halved(first, count):
        initial = held[pl.ds(first, count, stride=2), :]
        mean = 0.5 * (initial + held[pl.ds(first + 1, count, stride=2), :])
        f = lane(count) >> 4
        value = jnp.where(f == 6, initial, mean)
        value = jnp.where(f == 5, value, 0.5 * (value + pltpu.roll(value, 127, 1)))
        return gather_lanes(value, down[0:count])

    injected = doubled(gather_lanes(held[84:100, :], up[0:16]), tmp.at[0])
    value = jnp.where(level_one == 0, injected, held[48:80, :])
    held[48:80, :] = value
    injected = doubled(gather_lanes(held[52:76, :], up), tmp.at[1])
    held[0:48, :] = jnp.where(lev_strips[0:48, :] == 2, held[0:48, :], injected)
    tmp[2, 4:28, :] = halved(0, 24)
    held[48:80, :] = jnp.where(level_one == 2, tmp[2, 0:32, :], value)
    tmp[3, 4:20, :] = halved(48, 16)
    held[80:104, :] = jnp.where(lev_strips[80:104, :] >= 1, tmp[3, 0:24, :], held[80:104, :])


def main_kernel(
    lev,
    lev_strips,
    corner,
    fields_ref,
    own_ref,
    right_ref,
    left_ref,
    out_ref,
    win,
    prim,
    lefty,
    fluxy,
    gx,
    diffx,
    edge,
    turned,
    leftx,
    fluxx,
    held,
    tmp,
):
    p32, p8 = lane(32), lane(8)
    coarse32 = (p32 >= 72) & (p32 < 120)
    is_coarse = (p8 >= 72) & (p8 < 120)
    own_level = lev[8:16, :]

    p48 = lane(48)
    strips = jnp.where((p48 & 15) < 8, left_ref[...], right_ref[...])
    share_strips(strips, lev_strips, held, tmp)
    strip_one = ((p32 >= 64) & (p32 < 72)) | (p32 >= 120)
    strip_none = ((p32 >= 72) & (p32 < 80)) | ((p32 >= 112) & (p32 < 120))
    right_side = ((p32 >= 64) & (p32 < 72)) | ((p32 >= 112) & (p32 < 120))
    strip_index = (p32 & 7) + jnp.where(right_side, 8, 0)
    for f in range(7):
        index = strip_index + 16 * f
        win[f, PAD : PAD + 48, :] = own_ref[f, 0:48, :]
        win[f, SIDE : SIDE + 48, :] = pltpu.roll(held[0:48, :], (120 - 16 * f) % 128, 1)
        fine = gather_lanes(held[48:80, :], index)
        win[f, MID : MID + 32, :] = jnp.where(strip_one, fine, own_ref[f, 48:80, :])
        coarse = gather_lanes(held[80:104, :], index[0:24])
        win[f, MID : MID + 24, :] = jnp.where(
            strip_none[0:24], coarse, win[f, MID : MID + 24, :]
        )

    def swapped(value):
        outside = jnp.where(p8 < 48, pltpu.roll(value, 48, 1), pltpu.roll(value, 80, 1))
        return jnp.where((p8 >= 48) & (p8 < 80), value, outside)

    def turn(slot, value):
        value = value.T
        turned[slot, TPAD : TPAD + 128, :] = value
        turned[slot, TPAD - 8 : TPAD, :] = swapped(value[120:128])
        turned[slot, TPAD + 128 : TPAD + 136, :] = swapped(value[0:8])

    chunks = [PAD + 16 * c for c in range(8)]

    def primitives():
        for row in chunks:
            rows = slice(row, row + 16)
            inverse = 1.0 / win[0, rows, :]
            for i in range(3):
                prim[i, rows, :] = win[1 + i, rows, :] * inverse
            prim[3, rows, :] = 0.5 * (win[6, rows, :] + win[6, row + 1 : row + 17, :])
        sources = [(win, 0), (prim, 0), (prim, 1), (prim, 2), (prim, 3), (win, 4), (win, 5)]
        for slot, (ref, i) in enumerate(sources):
            turn(slot, ref[i, PAD : PAD + 128, :])
        face_x = turned.at[6]
        prim[4, PAD : PAD + 128, :] = (
            0.5 * (face_x[TPAD : TPAD + 128, :] + face_x[TPAD + 1 : TPAD + 129, :])
        ).T

    def sweep(items, lefts, row, count, normal):
        def at(item, step):
            ref, i = item
            return ref[i, row + step : row + step + count, :]

        left, right = [], []
        for i, item in enumerate(items):
            value = at(item, 0)
            slope = 0.5 * minmod(value - at(item, -1), at(item, 1) - value)
            lefts[i, row : row + count, :] = value + slope
            if normal is not None:
                left.append(lefts[i, row - 1 : row - 1 + count, :])
                right.append(value - slope)
        if normal is None:
            return None
        return riemann(left, right, at(normal, 0))

    def sweep_x():
        items = [(turned, i) for i in range(6)]
        sweep(items, leftx, TPAD - 8, 8, None)
        for row in [TPAD + 16 * c for c in range(9)]:
            count = 8 if row == TPAD + 128 else 16
            flux = sweep(items, leftx, row, count, (turned, 6))
            for i, value in enumerate(flux):
                fluxx[i, row : row + count, :] = value
        for i, n in enumerate((0, 1, 2, 3, 5)):
            value = fluxx[n, TPAD + 1 : TPAD + 129, :] - fluxx[n, TPAD : TPAD + 128, :]
            diffx[i, PAD : PAD + 128, :] = value.T
        gx[PAD : PAD + 128, :] = fluxx[4, TPAD : TPAD + 128, :].T

    def sweep_y():
        items = [(win, 0), (prim, 1), (prim, 0), (prim, 2), (prim, 4), (win, 4)]
        for row in chunks:
            flux = sweep(items, lefty, row, 16, (win, 6))
            for i, n in enumerate((0, 2, 1, 3, 5, 4)):
                fluxy[i, row : row + 16, :] = flux[n]

    def beside_cols(ref, row, back):
        parts = [ref[r : r + 8, :] for r in row]
        parts = [pltpu.roll(part, 1 if back else 127, 1) for part in parts]
        edge_lane = p8 == (0 if back else 127)
        return [
            jnp.where(edge_lane, parts[1], parts[0]),
            jnp.where(edge_lane, parts[0], parts[1]),
        ] + parts[2:]

    row_sets = [
        (PAD + 8 * c, SIDE + 8 * c) + ((MID + 8 * c,) if c < 4 else ()) for c in range(6)
    ]

    def edges():
        for rows in row_sets:
            shifted = beside_cols(fluxy.at[5], rows, True)
            for row, other in zip(rows, shifted):
                value = (fluxy[5, row : row + 8, :] + other) - (
                    gx[row : row + 8, :] + gx[row - 1 : row + 7, :]
                )
                edge[row : row + 8, :] = 0.25 * value

    def correct():
        value = edge[MID : MID + 32, :]
        finest = corner[...]
        halved_two = down_two(edge, (PAD, SIDE), False, False, tmp.at[0])
        halved_one = down_one(edge, MID, False, False, tmp.at[1])
        value = jnp.where((finest == 2) & ~coarse32, halved_two, value)
        edge[MID : MID + 32, :] = jnp.where((finest >= 1) & coarse32, halved_one, value)

    def update():
        for rows in row_sets:
            shifted = beside_cols(edge, rows, False)
            for k, (row, other) in enumerate(zip(rows, shifted)):
                ratio = STEP_SIZE
                if k == 2:
                    ratio = jnp.where(is_coarse, STEP_SIZE / 4, STEP_SIZE / 2)
                part = slice(row, row + 8)
                for i in range(5):
                    change = diffx[i, part, :] + (fluxy[i, row + 1 : row + 9, :] - fluxy[i, part, :])
                    win[i, part, :] = win[i, part, :] - ratio * change
                value = edge[part, :]
                diff_x = edge[row + 1 : row + 9, :] - value
                win[5, part, :] = win[5, part, :] - ratio * diff_x
                win[6, part, :] = win[6, part, :] + ratio * (other - value)

    for section in range(2):
        if section == 1:
            share_levels(win, lev, tmp, PAD, (0, 80))
        primitives()
        sweep_x()
        sweep_y()
        edges()
        correct()
        update()

    zero = jnp.zeros((8, COLS), F32)
    for f in range(7):
        for c in range(4):
            value = win[f, PAD + 8 + 8 * c : PAD + 16 + 8 * c, :]
            if c < 2:
                medium = win[f, MID + 8 + 8 * c : MID + 16 + 8 * c, :]
                coarse = pltpu.roll(medium, 48, 1) if c == 0 else zero
                lower = jnp.where(own_level == 1, medium, coarse)
                value = jnp.where(own_level == 2, value, lower)
            used = p8 < jnp.where(own_level == 2, 128, jnp.where(own_level == 1, 64, 32))
            used = used & (own_level >= (0, 1, 2, 2)[c])
            blend = 0.5 * (fields_ref[f, 8 * c : 8 * c + 8, :] + value)
            out_ref[f, 8 * c : 8 * c + 8, :] = jnp.where(used, blend, 0.0)


def moved(value, axis, step):
    size = lax.axis_size(axis)
    return lax.ppermute(value, axis, [(i, (i + step) % size) for i in range(size)])


def swapped_pairs(value, axis, first):
    size = lax.axis_size(axis)
    pairs = [(i, (i + 1) % size) for i in range(first, size, 2)]
    return lax.ppermute(value, axis, pairs + [(j, i) for i, j in pairs])


def on_device(fields, region_levels):
    shape = jax.ShapeDtypeStruct
    params = pltpu.CompilerParams(vmem_limit_bytes=32 * 1024 * 1024)
    far = swapped_pairs(fields, "seg", 1)
    close = swapped_pairs(fields, "seg", 0)
    lev, lev_strips, corner, cols = pl.pallas_call(
        own_kernel,
        out_shape=(
            shape((128, COLS), jnp.int32),
            shape((104, COLS), jnp.int32),
            shape((32, COLS), jnp.int32),
            shape((32, COLS), F32),
        ),
        in_specs=[HBM] * 2,
        out_specs=(VMEM,) * 4,
        scratch_shapes=[
            pltpu.VMEM(region_levels.shape[::-1], jnp.int32),
            pltpu.VMEM(fields.shape, F32),
            pltpu.VMEM((24, COLS), jnp.int32),
            pltpu.SemaphoreType.DMA((2,)),
        ],
        compiler_params=params,
    )(*(pltpu.with_memory_space_constraint(x, pltpu.HBM) for x in (region_levels.T, fields)))
    rows = shape((7, 8, COLS), F32)
    packed, below, above = pl.pallas_call(
        cols_kernel,
        out_shape=(shape((48, COLS), F32), rows, rows),
        in_specs=[VMEM] * 4,
        out_specs=(VMEM,) * 3,
        compiler_params=params,
    )(lev, cols, close, far)
    right = moved(packed, "sub", -1)
    left = moved(packed, "sub", 1)
    own = pl.pallas_call(
        rows_kernel,
        out_shape=shape((7, 128, COLS), F32),
        in_specs=[VMEM] * 4,
        out_specs=VMEM,
        scratch_shapes=[pltpu.VMEM((56, 48, COLS), F32)],
        compiler_params=params,
    )(lev, fields, below, above)

    def window(*lead):
        return pltpu.VMEM((*lead, PAD + 136, COLS), F32)

    def across(*lead):
        return pltpu.VMEM((*lead, TPAD + 144, COLS), F32)

    return pl.pallas_call(
        main_kernel,
        out_shape=shape(fields.shape, F32),
        in_specs=[VMEM] * 7,
        out_specs=VMEM,
        scratch_shapes=[
            window(7),
            window(5),
            window(6),
            window(6),
            window(),
            window(5),
            window(),
            across(7),
            across(6),
            across(6),
            pltpu.VMEM((104, COLS), F32),
            pltpu.VMEM((56, 48, COLS), F32),
        ],
        compiler_params=params,
    )(lev, lev_strips, corner, fields, own, right, left)


def solution(mesh):
    placed = (P(None, "seg", "sub"), P())
    return jax.shard_map(
        on_device, mesh=mesh, in_specs=placed, out_specs=P(None, "seg", "sub"), check_vma=False
    )
```

```python
from functools import partial

import jax
import jax.numpy as jnp
from jax import lax
from jax.experimental import pallas as pl
from jax.experimental.pallas import tpu as pltpu
from jax.sharding import PartitionSpec as P

STEP_SIZE = 0.08
ROWS, COLS = 32, 128
F32 = jnp.float32
VMEM = pl.BlockSpec(memory_space=pltpu.VMEM)
HBM = pl.BlockSpec(memory_space=pltpu.HBM)

PAD = 8
TPAD = 16
MID, SIDE = PAD + 48, PAD + 80


def lane(rows):
    return lax.broadcasted_iota(jnp.int32, (rows, COLS), 1)


def gather_lanes(value, index):
    return jnp.take_along_axis(value, index, axis=1, mode="promise_in_bounds")


def near_rows(levels_ref, held_ref):
    sub_count, seg_count = levels_ref.shape
    for j in range(3):
        u = lax.rem(lax.axis_index("sub") + (j - 1 + sub_count), sub_count)
        held_ref[8 * j : 8 * j + 1, 0:seg_count] = levels_ref[pl.ds(u, 1), :]
    table = []
    for i in range(3):
        s = lax.rem(lax.axis_index("seg") + (i - 1 + seg_count), seg_count)
        s = jnp.full((8, COLS), s, jnp.int32)
        rows = [jnp.broadcast_to(held_ref[8 * j : 8 * j + 1, :], (8, COLS)) for j in range(3)]
        table.append([gather_lanes(row, s) for row in rows])

    def level_of(i, offset):
        first, middle, last = table[i]
        return jnp.where(offset < 0, first, jnp.where(offset > 0, last, middle))

    return level_of


def last_rows(ref, f, level):
    return jnp.where(
        level == 2, ref[f, 24:32, :], jnp.where(level == 1, ref[f, 8:16, :], ref[f, 0:8, :])
    )


def packed_cols(read, level):
    p = lane(8)
    first = jnp.where(level == 2, 120, jnp.where(level == 1, 56, 24))
    index = (p & 7) + jnp.where((p & 15) < 8, first, 0)
    packed = gather_lanes(read(0), index)
    for f in range(1, 7):
        packed = jnp.where((p >> 4) == f, gather_lanes(read(f), index), packed)
    return packed


def own_kernel(levels_hbm, fields_hbm, lev, lev_strips, corner, cols_ref, levels_ref, fields_ref, held, sems):
    copies = [
        pltpu.make_async_copy(levels_hbm, levels_ref, sems.at[0]),
        pltpu.make_async_copy(fields_hbm, fields_ref, sems.at[1]),
    ]
    for copy in copies:
        copy.start()
    copies[0].wait()
    level_of = near_rows(levels_ref, held)
    p8 = lane(8)
    inner = (p8 < 64) | ((p8 >= 80) & (p8 < 112))
    outer = ((p8 >= 64) & (p8 < 72)) | ((p8 >= 112) & (p8 < 120))
    middle = jnp.zeros((8, COLS), jnp.int32)
    offsets = (middle, jnp.where(inner, 0, jnp.where(outer, 1, -1)), jnp.where(p8 < 64, 1, -1))
    is_coarse = (p8 >= 72) & (p8 < 120)
    for kind, first in enumerate((0, 48, 80)):
        below_row, centre_row, above_row = (level_of(i, offsets[kind]) for i in range(3))
        lev[first : first + 8, :] = below_row
        lev[first + 8 : first + 16, :] = centre_row
        if kind == 1:
            lev[first + 16 : first + 24, :] = jnp.where(is_coarse, above_row, centre_row)
            lev[first + 24 : first + 32, :] = above_row
        else:
            for r in (16, 24, 32):
                lev[first + r : first + r + 8, :] = centre_row
            lev[first + 40 : first + 48, :] = above_row
    offset = jnp.where((p8 & 15) < 8, -1, 1)
    below_row, centre_row, above_row = (level_of(i, offset) for i in range(3))
    for first, count in ((0, 6), (48, 4), (80, 3)):
        for r in range(count):
            row = below_row if r == 0 else above_row if r == count - 1 else centre_row
            lev_strips[first + 8 * r : first + 8 * r + 8, :] = row
    beside = lev[48:80, :]
    beside = jnp.maximum(beside, pltpu.roll(beside, 1, 1))
    corner[0] = jnp.maximum(beside, pltpu.roll(beside, 1, 0))
    corner[1] = pltpu.roll(corner[0], 127, 1)
    own = lev[8:16, :]
    copies[1].wait()
    for r in range(0, 32, 8):
        cols_ref[r : r + 8, :] = packed_cols(lambda f: fields_ref[f, r : r + 8, :], own)


def cols_kernel(lev, cols_ref, close_ref, far_ref, out_ref, below_ref, above_ref):
    even = jnp.full((8, COLS), lax.rem(lax.axis_index("seg"), 2)) == 0
    below_level, above_level = lev[0:8, :], lev[40:48, :]
    for f in range(7):
        far, close = (last_rows(ref, f, below_level) for ref in (far_ref, close_ref))
        below_ref[f] = jnp.where(even, far, close)
        above_ref[f] = jnp.where(even, close_ref[f, 0:8, :], far_ref[f, 0:8, :])
    out_ref[0:8, :] = packed_cols(lambda f: below_ref[f], below_level)
    out_ref[8:40, :] = cols_ref[...]
    out_ref[40:48, :] = packed_cols(lambda f: above_ref[f], above_level)


def minmod(a, b):
    return jnp.minimum(jnp.maximum(b, jnp.minimum(a, 0.0)), jnp.maximum(a, 0.0))


def riemann(left, right, normal):
    rho_l, vn_l, vt_l, vz_l, bt_l, bz_l = left
    rho_r, vn_r, vt_r, vz_r, bt_r, bz_r = right
    normal_square = normal * normal

    def signal(density, speed, square):
        total = density + (square + normal_square)
        return jnp.abs(speed) + jnp.abs(total) * lax.rsqrt(density * total)

    square_l = bt_l * bt_l + bz_l * bz_l
    square_r = bt_r * bt_r + bz_r * bz_r
    fastest = jnp.maximum(signal(rho_l, vn_l, square_l), signal(rho_r, vn_r, square_r))
    mn_l, mt_l, mz_l = rho_l * vn_l, rho_l * vt_l, rho_l * vz_l
    mn_r, mt_r, mz_r = rho_r * vn_r, rho_r * vt_r, rho_r * vz_r

    def carried(value_l, value_r, pull):
        return (value_l * vn_l + value_r * vn_r - pull) - fastest * (value_r - value_l)

    pressure = (rho_l + rho_r) + 0.5 * (square_l + square_r)
    return [
        (mn_l + mn_r) - fastest * (rho_r - rho_l),
        carried(mn_l, mn_r, normal_square - pressure),
        carried(mt_l, mt_r, normal * (bt_l + bt_r)),
        carried(mz_l, mz_r, normal * (bz_l + bz_r)),
        carried(bt_l, bt_r, normal * (vt_l + vt_r)),
        carried(bz_l, bz_r, normal * (vz_l + vz_r)),
    ]


def doubled(part):
    low = lax.broadcasted_iota(jnp.int32, (8, COLS), 0) >> 1
    rows = []
    for r in range(0, part.shape[0], 8):
        for index in (low, low + 4):
            rows.append(
                jnp.take_along_axis(part[r : r + 8], index, axis=0, mode="promise_in_bounds")
            )
    return jnp.concatenate(rows, axis=0)


def rows_halved(ref, first, by_rows):
    initial = ref[pl.ds(first - 8, 32, stride=2), :]
    if not by_rows:
        return initial
    return 0.5 * (initial + ref[pl.ds(first - 7, 32, stride=2), :])


def paired_lanes(value, index, by_cols):
    initial = gather_lanes(value, index)
    return 0.5 * (initial + gather_lanes(value, index + 1)) if by_cols else initial


def down_two(ref, firsts, by_rows, by_cols, step=0):
    p = lane(32) + step
    index = (2 * p) & 127
    parts = [paired_lanes(rows_halved(ref, first, by_rows), index, by_cols) for first in firsts]
    return parts[0] if len(parts) == 1 else jnp.where((p & 127) < 64, parts[0], parts[1])


def down_one(ref, first, by_rows, by_cols, step=0):
    return paired_lanes(
        rows_halved(ref, first, by_rows), (2 * (lane(32) + step - 80)) & 127, by_cols
    )


def share_levels(win, out, lev, blocks, fields):
    p32, p24, p16 = lane(32), lane(24), lane(16)
    coarse32 = (p32 >= 72) & (p32 < 120)
    level_b = lev[48:80, :]
    up_one = jnp.where(p16 < 72, 80 + (p16 >> 1), jnp.where(p16 >= 120, 16 + (p16 >> 1), p16))
    up_two = (p24 >> 1, 64 + (p24 >> 1))
    for f in fields:
        by_rows, by_cols = f != 6, f != 5
        value = win[f, MID : MID + 32, :]
        up = doubled(gather_lanes(win[f, MID + 4 : MID + 20, :], up_one))
        part = win[f, MID + 4 : MID + 28, :]
        ups = [doubled(gather_lanes(part, up_two[k])) for k in range(len(blocks))]
        down = down_two(win.at[f], [PAD + first for first in blocks], by_rows, by_cols)
        last = down_one(win.at[f], MID, by_rows, by_cols)
        medium = jnp.where(level_b == 0, up, jnp.where(level_b == 2, down, value))
        coarse = jnp.where(level_b >= 1, last, value)
        for first, injected in zip(blocks, ups):
            rows = slice(PAD + first, PAD + first + 48)
            out[f, rows, :] = jnp.where(lev[first : first + 48, :] == 2, win[f, rows, :], injected)
        out[f, MID : MID + 32, :] = jnp.where(coarse32, coarse, medium)


def rows_kernel(lev, fields_ref, below_ref, above_ref, out_ref, win):
    p8 = lane(8)
    is_coarse = (p8 >= 72) & (p8 < 120)

    def joined(fine, coarse):
        return jnp.where(is_coarse, pltpu.roll(coarse, 80, 1), fine)

    for f in range(7):
        below, above = below_ref[f], above_ref[f]
        initial, second = fields_ref[f, 0:8, :], fields_ref[f, 8:16, :]
        win[f, PAD : PAD + 8, :] = below
        win[f, PAD + 8 : PAD + 40, :] = fields_ref[f]
        win[f, PAD + 40 : PAD + 48, :] = above
        win[f, MID : MID + 8, :] = joined(below, below)
        win[f, MID + 8 : MID + 16, :] = joined(initial, initial)
        win[f, MID + 16 : MID + 24, :] = joined(second, above)
        win[f, MID + 24 : MID + 32, :] = above
    share_levels(win, out_ref, lev, (0,), range(7))


def share_strips(strips, lev_strips, held):
    p = lane(32)
    k = p & 15
    up = (p - k) + jnp.where(k < 8, 4 + (k >> 1), 8 + ((k - 8) >> 1))
    down = (p - k) + ((2 * k - 8) & 15)
    held[8:56, :] = strips
    held[56:80, :] = strips[0:24]
    held[80:88, :] = strips[40:48]
    held[88:104, :] = strips[0:16]
    held[104:112, :] = strips[40:48]

    def halved(first, count):
        initial = held[pl.ds(first - 8, count, stride=2), :]
        mean = 0.5 * (initial + held[pl.ds(first - 7, count, stride=2), :])
        f = lane(count) >> 4
        value = jnp.where(f == 6, initial, mean)
        even, odd = (gather_lanes(value, down[0:count] + k) for k in range(2))
        return jnp.where(f == 5, even, 0.5 * (even + odd))

    levels = [lev_strips[first : first + count, :] for first, count in ((0, 48), (48, 32), (80, 24))]
    up_one = doubled(gather_lanes(held[92:108, :], up[0:16]))
    up_two = doubled(gather_lanes(held[60:84, :], up[0:24]))
    down_to_one, down_to_none = halved(8, 32), halved(56, 24)
    fine = jnp.where(levels[0] == 2, held[8:56, :], up_two)
    medium = jnp.where(levels[1] == 2, down_to_one, held[56:88, :])
    medium = jnp.where(levels[1] == 0, up_one, medium)
    coarse = jnp.where(levels[2] >= 1, down_to_none, held[88:112, :])
    return fine, medium, coarse


def main_kernel(
    lev,
    lev_strips,
    corner,
    fields_ref,
    own_ref,
    right_ref,
    left_ref,
    out_ref,
    win,
    base,
    prim,
    lefty,
    fluxy,
    gx,
    diffx,
    edge,
    fixed,
    turned,
    leftx,
    fluxx,
    held,
    result,
    sems,
):
    p32, p8 = lane(32), lane(8)
    is_coarse = (p8 >= 72) & (p8 < 120)
    own_level = lev[8:16, :]

    p48 = lane(48)
    strips = jnp.where((p48 & 15) < 8, left_ref[...], right_ref[...])
    fine, medium, coarse = share_strips(strips, lev_strips, held)
    strip_one = ((p32 >= 64) & (p32 < 72)) | (p32 >= 120)
    strip_none = ((p32 >= 72) & (p32 < 80)) | ((p32 >= 112) & (p32 < 120))
    right_side = ((p32 >= 64) & (p32 < 72)) | ((p32 >= 112) & (p32 < 120))
    strip_index = (p32 & 7) + jnp.where(right_side, 8, 0)
    for f in range(7):
        index = strip_index + 16 * f
        base[f, PAD : PAD + 48, :] = own_ref[f, PAD : PAD + 48, :]
        base[f, SIDE : SIDE + 48, :] = pltpu.roll(fine, (120 - 16 * f) % 128, 1)
        value = jnp.where(strip_one, gather_lanes(medium, index), own_ref[f, MID : MID + 32, :])
        base[f, MID + 24 : MID + 32, :] = value[24:32]
        base[f, MID : MID + 24, :] = jnp.where(
            strip_none[0:24], gather_lanes(coarse, index[0:24]), value[0:24]
        )

    def swapped(value):
        outside = jnp.where(p8 < 48, pltpu.roll(value, 48, 1), pltpu.roll(value, 80, 1))
        return jnp.where((p8 >= 48) & (p8 < 80), value, outside)

    def turn(slot, value):
        value = value.T
        turned[slot, TPAD : TPAD + 128, :] = value
        turned[slot, TPAD - 8 : TPAD, :] = swapped(value[120:128])
        turned[slot, TPAD + 128 : TPAD + 136, :] = swapped(value[0:8])

    chunks = [PAD + 16 * c for c in range(8)]

    def primitives():
        for row in chunks:
            rows = slice(row, row + 16)
            inverse = 1.0 / base[0, rows, :]
            for i in range(3):
                prim[i, rows, :] = base[1 + i, rows, :] * inverse
            prim[3, rows, :] = 0.5 * (base[6, rows, :] + base[6, row + 1 : row + 17, :])
        for rows in row_sets:
            faces = [base[5, row : row + 8, :] for row in rows]
            for row, face, other in zip(rows, faces, beside_cols(faces, False)):
                prim[4, row : row + 8, :] = 0.5 * (face + other)
        sources = [(base, 0), (prim, 0), (prim, 1), (prim, 2), (prim, 3), (base, 4), (base, 5)]
        for slot, (ref, i) in enumerate(sources):
            turn(slot, ref[i, PAD : PAD + 128, :])

    def sweep(items, lefts, row, count, normal):
        def at(item, step):
            ref, i = item
            return ref[i, row + step : row + step + count, :]

        left, right = [], []
        for i, item in enumerate(items):
            value = at(item, 0)
            slope = 0.5 * minmod(value - at(item, -1), at(item, 1) - value)
            lefts[i, row : row + count, :] = value + slope
            if normal is not None:
                left.append(lefts[i, row - 1 : row - 1 + count, :])
                right.append(value - slope)
        if normal is None:
            return None
        return riemann(left, right, at(normal, 0))

    def sweep_x():
        items = [(turned, i) for i in range(6)]
        sweep(items, leftx, TPAD - 8, 8, None)
        for row in [TPAD + 16 * c for c in range(9)]:
            count = 8 if row == TPAD + 128 else 16
            flux = sweep(items, leftx, row, count, (turned, 6))
            for i, value in enumerate(flux):
                fluxx[i, row : row + count, :] = value
        gx[PAD : PAD + 128, :] = fluxx[4, TPAD : TPAD + 128, :].T
        for i, n in enumerate((0, 1, 2, 3, 5)):
            value = fluxx[n, TPAD + 1 : TPAD + 129, :] - fluxx[n, TPAD : TPAD + 128, :]
            diffx[i, PAD : PAD + 128, :] = value.T

    def sweep_y():
        items = [(base, 0), (prim, 1), (prim, 0), (prim, 2), (prim, 4), (base, 4)]
        for row in chunks:
            flux = sweep(items, lefty, row, 16, (base, 6))
            for i, n in enumerate((0, 2, 1, 3, 5, 4)):
                fluxy[i, row : row + 16, :] = flux[n]

    def beside_cols(parts, back):
        parts = [pltpu.roll(part, 1 if back else 127, 1) for part in parts]
        edge_lane = p8 == (0 if back else 127)
        return [
            jnp.where(edge_lane, parts[1], parts[0]),
            jnp.where(edge_lane, parts[0], parts[1]),
        ] + parts[2:]

    row_sets = [
        (PAD + 8 * c, SIDE + 8 * c) + ((MID + 8 * c,) if c < 4 else ()) for c in range(6)
    ]

    def edges():
        for rows in row_sets:
            shifted = beside_cols([fluxy[5, row : row + 8, :] for row in rows], True)
            for row, other in zip(rows, shifted):
                value = (fluxy[5, row : row + 8, :] + other) - (
                    gx[row : row + 8, :] + gx[row - 1 : row + 7, :]
                )
                edge[row : row + 8, :] = 0.125 * value

    def correct():
        value = edge[MID : MID + 32, :]
        values = (value, pltpu.roll(value, 127, 1))
        for step in range(2):
            finest = corner[step]
            coarse = (p32 + step >= 72) & (p32 + step < 120)
            halved_two = down_two(edge, (PAD, SIDE), False, False, step)
            halved_one = down_one(edge, MID, False, False, step)
            value = jnp.where((finest == 2) & ~coarse, halved_two, values[step])
            fixed[step, 0:32, :] = jnp.where((finest >= 1) & coarse, halved_one, value)

    def update_cells(i):
        for rows in row_sets:
            for k, row in enumerate(rows):
                part = slice(row, row + 8)
                change = diffx[i, part, :] + (fluxy[i, row + 1 : row + 9, :] - fluxy[i, part, :])
                win[i, part, :] = base[i, part, :] - 0.5 * ratios[k] * change

    def update_faces():
        for rows in row_sets:
            values = [edge[row : row + 8, :] for row in rows[:2]]
            above = [edge[row + 1 : row + 9, :] for row in rows[:2]]
            others = beside_cols(values, False)
            for row in rows[2:]:
                first = row - MID
                values.append(fixed[0, first : first + 8, :])
                above.append(fixed[0, first + 1 : first + 9, :])
                others.append(fixed[1, first : first + 8, :])
            for row, ratio, value, up, other in zip(rows, ratios, values, above, others):
                part = slice(row, row + 8)
                win[5, part, :] = base[5, part, :] - ratio * (up - value)
                win[6, part, :] = base[6, part, :] + ratio * (other - value)

    ratios = (STEP_SIZE, STEP_SIZE, jnp.where(is_coarse, STEP_SIZE / 4, STEP_SIZE / 2))

    def shared(fields):
        share_levels(win, base, lev, (0, 80), fields)

    def finish(fields):
        zero = jnp.zeros((8, COLS), F32)
        for f in fields:
            for c in range(4):
                value = win[f, PAD + 8 + 8 * c : PAD + 16 + 8 * c, :]
                if c < 2:
                    medium = win[f, MID + 8 + 8 * c : MID + 16 + 8 * c, :]
                    coarse = pltpu.roll(medium, 48, 1) if c == 0 else zero
                    lower = jnp.where(own_level == 1, medium, coarse)
                    value = jnp.where(own_level == 2, value, lower)
                used = p8 < jnp.where(own_level == 2, 128, jnp.where(own_level == 1, 64, 32))
                used = used & (own_level >= (0, 1, 2, 2)[c])
                blend = 0.5 * (fields_ref[f, 8 * c : 8 * c + 8, :] + value)
                result[f, 8 * c : 8 * c + 8, :] = jnp.where(used, blend, 0.0)
            pltpu.make_async_copy(result.at[f], out_ref.at[f], sems.at[f]).start()

    for section in range(2):
        then = (shared, finish)[section]
        primitives()
        sweep_x()
        sweep_y()
        edges()
        update_cells(0)
        then((0,))
        correct()
        for i in range(1, 5):
            update_cells(i)
            then((i,))
            if i == 2:
                update_faces()
        then((5, 6))
    for f in range(7):
        pltpu.make_async_copy(result.at[f], out_ref.at[f], sems.at[f]).wait()


def moved(value, axis, step):
    size = lax.axis_size(axis)
    return lax.ppermute(value, axis, [(i, (i + step) % size) for i in range(size)])


def swapped_pairs(value, axis, first):
    size = lax.axis_size(axis)
    pairs = [(i, (i + 1) % size) for i in range(first, size, 2)]
    return lax.ppermute(value, axis, pairs + [(j, i) for i, j in pairs])


def on_device(fields, region_levels):
    shape = jax.ShapeDtypeStruct
    params = pltpu.CompilerParams(vmem_limit_bytes=32 * 1024 * 1024)
    far = swapped_pairs(fields, "seg", 1)
    close = swapped_pairs(fields, "seg", 0)
    lev, lev_strips, corner, cols = pl.pallas_call(
        own_kernel,
        out_shape=(
            shape((128, COLS), jnp.int32),
            shape((104, COLS), jnp.int32),
            shape((2, 32, COLS), jnp.int32),
            shape((32, COLS), F32),
        ),
        in_specs=[HBM] * 2,
        out_specs=(VMEM,) * 4,
        scratch_shapes=[
            pltpu.VMEM(region_levels.shape[::-1], jnp.int32),
            pltpu.VMEM(fields.shape, F32),
            pltpu.VMEM((24, COLS), jnp.int32),
            pltpu.SemaphoreType.DMA((2,)),
        ],
        compiler_params=params,
    )(*(pltpu.with_memory_space_constraint(x, pltpu.HBM) for x in (region_levels.T, fields)))
    rows = shape((7, 8, COLS), F32)
    packed, below, above = pl.pallas_call(
        cols_kernel,
        out_shape=(shape((48, COLS), F32), rows, rows),
        in_specs=[VMEM] * 4,
        out_specs=(VMEM,) * 3,
        compiler_params=params,
    )(lev, cols, close, far)
    right = moved(packed, "sub", -1)
    left = moved(packed, "sub", 1)
    own = pl.pallas_call(
        rows_kernel,
        out_shape=shape((7, PAD + 136, COLS), F32),
        in_specs=[VMEM] * 4,
        out_specs=VMEM,
        scratch_shapes=[pltpu.VMEM((7, PAD + 136, COLS), F32)],
        compiler_params=params,
    )(lev, fields, below, above)

    def window(*lead):
        return pltpu.VMEM((*lead, PAD + 136, COLS), F32)

    def across(*lead):
        return pltpu.VMEM((*lead, TPAD + 144, COLS), F32)

    return pl.pallas_call(
        main_kernel,
        out_shape=shape(fields.shape, F32),
        in_specs=[VMEM] * 7,
        out_specs=HBM,
        scratch_shapes=[
            window(7),
            window(7),
            window(5),
            window(6),
            window(6),
            window(),
            window(5),
            window(),
            pltpu.VMEM((2, 40, COLS), F32),
            across(7),
            across(6),
            across(6),
            pltpu.VMEM((112, COLS), F32),
            pltpu.VMEM(fields.shape, F32),
            pltpu.SemaphoreType.DMA((7,)),
        ],
        compiler_params=params,
    )(lev, lev_strips, corner, fields, own, right, left)


def solution(mesh):
    placed = (P(None, "seg", "sub"), P())
    return jax.shard_map(
        on_device, mesh=mesh, in_specs=placed, out_specs=P(None, "seg", "sub"), check_vma=False
    )
```

```python
from functools import partial

import jax
import jax.numpy as jnp
from jax import lax
from jax.experimental import pallas as pl
from jax.experimental.pallas import tpu as pltpu
from jax.sharding import PartitionSpec as P

STEP_SIZE = 0.08
ROWS, COLS = 32, 128
F32 = jnp.float32
VMEM = pl.BlockSpec(memory_space=pltpu.VMEM)
HBM = pl.BlockSpec(memory_space=pltpu.HBM)

PAD = 8
TPAD = 16
MID, SIDE = PAD + 48, PAD + 80


def lane(rows):
    return lax.broadcasted_iota(jnp.int32, (rows, COLS), 1)


def gather_lanes(value, index):
    return jnp.take_along_axis(value, index, axis=1, mode="promise_in_bounds")


def near_rows(levels_ref, held_ref):
    sub_count, seg_count = levels_ref.shape
    for j in range(3):
        u = lax.rem(lax.axis_index("sub") + (j - 1 + sub_count), sub_count)
        held_ref[8 * j : 8 * j + 1, 0:seg_count] = levels_ref[pl.ds(u, 1), :]
    table = []
    for i in range(3):
        s = lax.rem(lax.axis_index("seg") + (i - 1 + seg_count), seg_count)
        s = jnp.full((8, COLS), s, jnp.int32)
        rows = [jnp.broadcast_to(held_ref[8 * j : 8 * j + 1, :], (8, COLS)) for j in range(3)]
        table.append([gather_lanes(row, s) for row in rows])

    def level_of(i, offset):
        first, middle, last = table[i]
        return jnp.where(offset < 0, first, jnp.where(offset > 0, last, middle))

    return level_of


def last_rows(ref, f, level):
    return jnp.where(
        level == 2, ref[f, 24:32, :], jnp.where(level == 1, ref[f, 8:16, :], ref[f, 0:8, :])
    )


def packed_cols(read, level):
    p = lane(8)
    first = jnp.where(level == 2, 120, jnp.where(level == 1, 56, 24))
    index = (p & 7) + jnp.where((p & 15) < 8, first, 0)
    packed = gather_lanes(read(0), index)
    for f in range(1, 7):
        packed = jnp.where((p >> 4) == f, gather_lanes(read(f), index), packed)
    return packed


def own_kernel(levels_hbm, fields_hbm, lev, lev_strips, corner, cols_ref, levels_ref, fields_ref, held, sems):
    copies = [
        pltpu.make_async_copy(levels_hbm, levels_ref, sems.at[0]),
        pltpu.make_async_copy(fields_hbm, fields_ref, sems.at[1]),
    ]
    for copy in copies:
        copy.start()
    copies[0].wait()
    level_of = near_rows(levels_ref, held)
    p8 = lane(8)
    inner = (p8 < 64) | ((p8 >= 80) & (p8 < 112))
    outer = ((p8 >= 64) & (p8 < 72)) | ((p8 >= 112) & (p8 < 120))
    middle = jnp.zeros((8, COLS), jnp.int32)
    offsets = (middle, jnp.where(inner, 0, jnp.where(outer, 1, -1)), jnp.where(p8 < 64, 1, -1))
    is_coarse = (p8 >= 72) & (p8 < 120)
    for kind, first in enumerate((0, 48, 80)):
        below_row, centre_row, above_row = (level_of(i, offsets[kind]) for i in range(3))
        lev[first : first + 8, :] = below_row
        lev[first + 8 : first + 16, :] = centre_row
        if kind == 1:
            lev[first + 16 : first + 24, :] = jnp.where(is_coarse, above_row, centre_row)
            lev[first + 24 : first + 32, :] = above_row
        else:
            for r in (16, 24, 32):
                lev[first + r : first + r + 8, :] = centre_row
            lev[first + 40 : first + 48, :] = above_row
    offset = jnp.where((p8 & 15) < 8, -1, 1)
    below_row, centre_row, above_row = (level_of(i, offset) for i in range(3))
    for first, count in ((0, 6), (48, 4), (80, 3)):
        for r in range(count):
            row = below_row if r == 0 else above_row if r == count - 1 else centre_row
            lev_strips[first + 8 * r : first + 8 * r + 8, :] = row
    beside = lev[48:80, :]
    beside = jnp.maximum(beside, pltpu.roll(beside, 1, 1))
    corner[0] = jnp.maximum(beside, pltpu.roll(beside, 1, 0))
    corner[1] = pltpu.roll(corner[0], 127, 1)
    own = lev[8:16, :]
    copies[1].wait()
    for r in range(0, 32, 8):
        cols_ref[r : r + 8, :] = packed_cols(lambda f: fields_ref[f, r : r + 8, :], own)


def cols_kernel(lev, cols_ref, wrap_ref, close_ref, far_ref, out_ref, below_ref, above_ref):
    seg, last = lax.axis_index("seg"), lax.axis_size("seg") - 1
    even = jnp.full((8, COLS), lax.rem(seg, 2)) == 0
    ends = jnp.full((8, COLS), lax.rem(seg, last)) == 0
    below_level, above_level = lev[0:8, :], lev[40:48, :]
    for f in range(7):
        far, wrap, close = (last_rows(r, f, below_level) for r in (far_ref, wrap_ref, close_ref))
        below_ref[f] = jnp.where(even, jnp.where(ends, wrap, far), close)
        far = jnp.where(ends, wrap_ref[f, 0:8, :], far_ref[f, 0:8, :])
        above_ref[f] = jnp.where(even, close_ref[f, 0:8, :], far)
    out_ref[0:8, :] = packed_cols(lambda f: below_ref[f], below_level)
    out_ref[8:40, :] = cols_ref[...]
    out_ref[40:48, :] = packed_cols(lambda f: above_ref[f], above_level)


def minmod(a, b):
    return jnp.minimum(jnp.maximum(b, jnp.minimum(a, 0.0)), jnp.maximum(a, 0.0))


def riemann(left, right, normal):
    rho_l, vn_l, vt_l, vz_l, bt_l, bz_l = left
    rho_r, vn_r, vt_r, vz_r, bt_r, bz_r = right
    normal_square = normal * normal

    def signal(density, speed, square):
        total = density + (square + normal_square)
        return jnp.abs(speed) + jnp.abs(total) * lax.rsqrt(density * total)

    square_l = bt_l * bt_l + bz_l * bz_l
    square_r = bt_r * bt_r + bz_r * bz_r
    fastest = jnp.maximum(signal(rho_l, vn_l, square_l), signal(rho_r, vn_r, square_r))
    ahead, back = vn_l + fastest, vn_r - fastest
    mass_l, mass_r = rho_l * ahead, rho_r * back
    pressure = (rho_l + rho_r) + 0.5 * (square_l + square_r)
    return [
        mass_l + mass_r,
        (mass_l * vn_l + mass_r * vn_r) + (pressure - normal_square),
        (mass_l * vt_l + mass_r * vt_r) - normal * (bt_l + bt_r),
        (mass_l * vz_l + mass_r * vz_r) - normal * (bz_l + bz_r),
        (bt_l * ahead + bt_r * back) - normal * (vt_l + vt_r),
        (bz_l * ahead + bz_r * back) - normal * (vz_l + vz_r),
    ]


def doubled(part):
    low = lax.broadcasted_iota(jnp.int32, (8, COLS), 0) >> 1
    rows = []
    for r in range(0, part.shape[0], 8):
        for index in (low, low + 4):
            rows.append(
                jnp.take_along_axis(part[r : r + 8], index, axis=0, mode="promise_in_bounds")
            )
    return jnp.concatenate(rows, axis=0)


def rows_halved(ref, first, by_rows):
    initial = ref[pl.ds(first - 8, 32, stride=2), :]
    if not by_rows:
        return initial
    return 0.5 * (initial + ref[pl.ds(first - 7, 32, stride=2), :])


def paired_lanes(value, index, by_cols):
    initial = gather_lanes(value, index)
    return 0.5 * (initial + gather_lanes(value, index + 1)) if by_cols else initial


def down_two(ref, firsts, by_rows, by_cols, step=0):
    p = lane(32) + step
    index = (2 * p) & 127
    parts = [paired_lanes(rows_halved(ref, first, by_rows), index, by_cols) for first in firsts]
    return parts[0] if len(parts) == 1 else jnp.where((p & 127) < 64, parts[0], parts[1])


def down_one(ref, first, by_rows, by_cols, step=0):
    return paired_lanes(
        rows_halved(ref, first, by_rows), (2 * (lane(32) + step - 80)) & 127, by_cols
    )


def share_levels(win, out, lev, blocks, fields):
    p32, p24, p16 = lane(32), lane(24), lane(16)
    coarse32 = (p32 >= 72) & (p32 < 120)
    level_b = lev[48:80, :]
    up_one = jnp.where(p16 < 72, 80 + (p16 >> 1), jnp.where(p16 >= 120, 16 + (p16 >> 1), p16))
    up_two = (p24 >> 1, 64 + (p24 >> 1))
    for f in fields:
        by_rows, by_cols = f != 6, f != 5
        value = win[f, MID : MID + 32, :]
        up = doubled(gather_lanes(win[f, MID + 4 : MID + 20, :], up_one))
        part = win[f, MID + 4 : MID + 28, :]
        ups = [doubled(gather_lanes(part, up_two[k])) for k in range(len(blocks))]
        down = down_two(win.at[f], [PAD + first for first in blocks], by_rows, by_cols)
        last = down_one(win.at[f], MID, by_rows, by_cols)
        medium = jnp.where(level_b == 0, up, jnp.where(level_b == 2, down, value))
        coarse = jnp.where(level_b >= 1, last, value)
        for first, injected in zip(blocks, ups):
            rows = slice(PAD + first, PAD + first + 48)
            out[f, rows, :] = jnp.where(lev[first : first + 48, :] == 2, win[f, rows, :], injected)
        out[f, MID : MID + 32, :] = jnp.where(coarse32, coarse, medium)


def rows_kernel(lev, fields_ref, below_ref, above_ref, out_ref, win):
    p8 = lane(8)
    is_coarse = (p8 >= 72) & (p8 < 120)

    def joined(fine, coarse):
        return jnp.where(is_coarse, pltpu.roll(coarse, 80, 1), fine)

    for f in range(7):
        below, above = below_ref[f], above_ref[f]
        initial, second = fields_ref[f, 0:8, :], fields_ref[f, 8:16, :]
        win[f, PAD : PAD + 8, :] = below
        win[f, PAD + 8 : PAD + 40, :] = fields_ref[f]
        win[f, PAD + 40 : PAD + 48, :] = above
        win[f, MID : MID + 8, :] = joined(below, below)
        win[f, MID + 8 : MID + 16, :] = joined(initial, initial)
        win[f, MID + 16 : MID + 24, :] = joined(second, above)
        win[f, MID + 24 : MID + 32, :] = above
    share_levels(win, out_ref, lev, (0,), range(7))


def share_strips(strips, lev_strips, held):
    p = lane(32)
    k = p & 15
    up = (p - k) + jnp.where(k < 8, 4 + (k >> 1), 8 + ((k - 8) >> 1))
    down = (p - k) + ((2 * k - 8) & 15)
    held[8:56, :] = strips
    held[56:80, :] = strips[0:24]
    held[80:88, :] = strips[40:48]
    held[88:104, :] = strips[0:16]
    held[104:112, :] = strips[40:48]

    def halved(first, count):
        initial = held[pl.ds(first - 8, count, stride=2), :]
        mean = 0.5 * (initial + held[pl.ds(first - 7, count, stride=2), :])
        f = lane(count) >> 4
        value = jnp.where(f == 6, initial, mean)
        even, odd = (gather_lanes(value, down[0:count] + k) for k in range(2))
        return jnp.where(f == 5, even, 0.5 * (even + odd))

    levels = [lev_strips[first : first + count, :] for first, count in ((0, 48), (48, 32), (80, 24))]
    up_one = doubled(gather_lanes(held[92:108, :], up[0:16]))
    up_two = doubled(gather_lanes(held[60:84, :], up[0:24]))
    down_to_one, down_to_none = halved(8, 32), halved(56, 24)
    fine = jnp.where(levels[0] == 2, held[8:56, :], up_two)
    medium = jnp.where(levels[1] == 2, down_to_one, held[56:88, :])
    medium = jnp.where(levels[1] == 0, up_one, medium)
    coarse = jnp.where(levels[2] >= 1, down_to_none, held[88:112, :])
    return fine, medium, coarse


def main_kernel(
    lev,
    lev_strips,
    corner,
    fields_ref,
    own_ref,
    right_ref,
    left_ref,
    out_ref,
    win,
    base,
    prim,
    lefty,
    fluxy,
    gx,
    diffx,
    edge,
    fixed,
    turned,
    leftx,
    fluxx,
    held,
    result,
    sems,
):
    p32, p8 = lane(32), lane(8)
    is_coarse = (p8 >= 72) & (p8 < 120)
    own_level = lev[8:16, :]

    p48 = lane(48)
    strips = jnp.where((p48 & 15) < 8, left_ref[...], right_ref[...])
    fine, medium, coarse = share_strips(strips, lev_strips, held)
    strip_one = ((p32 >= 64) & (p32 < 72)) | (p32 >= 120)
    strip_none = ((p32 >= 72) & (p32 < 80)) | ((p32 >= 112) & (p32 < 120))
    right_side = ((p32 >= 64) & (p32 < 72)) | ((p32 >= 112) & (p32 < 120))
    strip_index = (p32 & 7) + jnp.where(right_side, 8, 0)
    for f in range(7):
        index = strip_index + 16 * f
        base[f, PAD : PAD + 48, :] = own_ref[f, PAD : PAD + 48, :]
        base[f, SIDE : SIDE + 48, :] = pltpu.roll(fine, (120 - 16 * f) % 128, 1)
        value = jnp.where(strip_one, gather_lanes(medium, index), own_ref[f, MID : MID + 32, :])
        base[f, MID + 24 : MID + 32, :] = value[24:32]
        base[f, MID : MID + 24, :] = jnp.where(
            strip_none[0:24], gather_lanes(coarse, index[0:24]), value[0:24]
        )

    def swapped(value):
        outside = jnp.where(p8 < 48, pltpu.roll(value, 48, 1), pltpu.roll(value, 80, 1))
        return jnp.where((p8 >= 48) & (p8 < 80), value, outside)

    def turn(slot, value):
        value = value.T
        turned[slot, TPAD : TPAD + 128, :] = value
        turned[slot, TPAD - 8 : TPAD, :] = swapped(value[120:128])
        turned[slot, TPAD + 128 : TPAD + 136, :] = swapped(value[0:8])

    chunks = [PAD + 16 * c for c in range(8)]

    def primitives():
        for row in chunks:
            rows = slice(row, row + 16)
            inverse = 1.0 / base[0, rows, :]
            for i in range(3):
                prim[i, rows, :] = base[1 + i, rows, :] * inverse
            prim[3, rows, :] = 0.5 * (base[6, rows, :] + base[6, row + 1 : row + 17, :])
        for rows in row_sets:
            faces = [base[5, row : row + 8, :] for row in rows]
            for row, face, other in zip(rows, faces, beside_cols(faces, False)):
                prim[4, row : row + 8, :] = 0.5 * (face + other)
        sources = [(base, 0), (prim, 0), (prim, 1), (prim, 2), (prim, 3), (base, 4), (base, 5)]
        for slot, (ref, i) in enumerate(sources):
            turn(slot, ref[i, PAD : PAD + 128, :])

    def sweep(items, lefts, row, count, normal):
        def at(item, step):
            ref, i = item
            return ref[i, row + step : row + step + count, :]

        left, right = [], []
        for i, item in enumerate(items):
            value = at(item, 0)
            slope = 0.5 * minmod(value - at(item, -1), at(item, 1) - value)
            lefts[i, row : row + count, :] = value + slope
            if normal is not None:
                left.append(lefts[i, row - 1 : row - 1 + count, :])
                right.append(value - slope)
        if normal is None:
            return None
        return riemann(left, right, at(normal, 0))

    def sweep_x():
        items = [(turned, i) for i in range(6)]
        sweep(items, leftx, TPAD - 8, 8, None)
        for row in [TPAD + 16 * c for c in range(9)]:
            count = 8 if row == TPAD + 128 else 16
            flux = sweep(items, leftx, row, count, (turned, 6))
            for i, value in enumerate(flux):
                fluxx[i, row : row + count, :] = value
        gx[PAD : PAD + 128, :] = fluxx[4, TPAD : TPAD + 128, :].T
        for i, n in enumerate((0, 1, 2, 3, 5)):
            value = fluxx[n, TPAD + 1 : TPAD + 129, :] - fluxx[n, TPAD : TPAD + 128, :]
            diffx[i, PAD : PAD + 128, :] = value.T

    def sweep_y():
        items = [(base, 0), (prim, 1), (prim, 0), (prim, 2), (prim, 4), (base, 4)]
        for row in chunks:
            flux = sweep(items, lefty, row, 16, (base, 6))
            for i, n in enumerate((0, 2, 1, 3, 5, 4)):
                fluxy[i, row : row + 16, :] = flux[n]

    def beside_cols(parts, back):
        parts = [pltpu.roll(part, 1 if back else 127, 1) for part in parts]
        edge_lane = p8 == (0 if back else 127)
        return [
            jnp.where(edge_lane, parts[1], parts[0]),
            jnp.where(edge_lane, parts[0], parts[1]),
        ] + parts[2:]

    row_sets = [
        (PAD + 8 * c, SIDE + 8 * c) + ((MID + 8 * c,) if c < 4 else ()) for c in range(6)
    ]

    def edges():
        for rows in row_sets:
            shifted = beside_cols([fluxy[5, row : row + 8, :] for row in rows], True)
            for row, other in zip(rows, shifted):
                value = (fluxy[5, row : row + 8, :] + other) - (
                    gx[row : row + 8, :] + gx[row - 1 : row + 7, :]
                )
                edge[row : row + 8, :] = 0.125 * value

    def correct():
        value = edge[MID : MID + 32, :]
        values = (value, pltpu.roll(value, 127, 1))
        for step in range(2):
            finest = corner[step]
            coarse = (p32 + step >= 72) & (p32 + step < 120)
            halved_two = down_two(edge, (PAD, SIDE), False, False, step)
            halved_one = down_one(edge, MID, False, False, step)
            value = jnp.where((finest == 2) & ~coarse, halved_two, values[step])
            fixed[step, 0:32, :] = jnp.where((finest >= 1) & coarse, halved_one, value)

    def update_cells(i):
        for rows in row_sets:
            for k, row in enumerate(rows):
                part = slice(row, row + 8)
                change = diffx[i, part, :] + (fluxy[i, row + 1 : row + 9, :] - fluxy[i, part, :])
                win[i, part, :] = base[i, part, :] - 0.5 * ratios[k] * change

    def update_faces():
        for rows in row_sets:
            values = [edge[row : row + 8, :] for row in rows[:2]]
            above = [edge[row + 1 : row + 9, :] for row in rows[:2]]
            others = beside_cols(values, False)
            for row in rows[2:]:
                first = row - MID
                values.append(fixed[0, first : first + 8, :])
                above.append(fixed[0, first + 1 : first + 9, :])
                others.append(fixed[1, first : first + 8, :])
            for row, ratio, value, up, other in zip(rows, ratios, values, above, others):
                part = slice(row, row + 8)
                win[5, part, :] = base[5, part, :] - ratio * (up - value)
                win[6, part, :] = base[6, part, :] + ratio * (other - value)

    ratios = (STEP_SIZE, STEP_SIZE, jnp.where(is_coarse, STEP_SIZE / 4, STEP_SIZE / 2))

    def shared(fields):
        share_levels(win, base, lev, (0, 80), fields)

    def finish(fields):
        zero = jnp.zeros((8, COLS), F32)
        for f in fields:
            for c in range(4):
                value = win[f, PAD + 8 + 8 * c : PAD + 16 + 8 * c, :]
                if c < 2:
                    medium = win[f, MID + 8 + 8 * c : MID + 16 + 8 * c, :]
                    coarse = pltpu.roll(medium, 48, 1) if c == 0 else zero
                    lower = jnp.where(own_level == 1, medium, coarse)
                    value = jnp.where(own_level == 2, value, lower)
                used = p8 < jnp.where(own_level == 2, 128, jnp.where(own_level == 1, 64, 32))
                used = used & (own_level >= (0, 1, 2, 2)[c])
                blend = 0.5 * (fields_ref[f, 8 * c : 8 * c + 8, :] + value)
                result[f, 8 * c : 8 * c + 8, :] = jnp.where(used, blend, 0.0)
            pltpu.make_async_copy(result.at[f], out_ref.at[f], sems.at[f]).start()

    for section in range(2):
        then = (shared, finish)[section]
        primitives()
        sweep_x()
        sweep_y()
        edges()
        update_cells(0)
        then((0,))
        correct()
        for i in range(1, 5):
            update_cells(i)
            then((i,))
            if i == 2:
                update_faces()
        then((5, 6))
    for f in range(7):
        pltpu.make_async_copy(result.at[f], out_ref.at[f], sems.at[f]).wait()


def moved(value, axis, step):
    size = lax.axis_size(axis)
    return lax.ppermute(value, axis, [(i, (i + step) % size) for i in range(size)])


def swapped_pairs(value, axis, first, stop):
    size = lax.axis_size(axis)
    pairs = [(i, (i + 1) % size) for i in range(first, stop, 2)]
    return lax.ppermute(value, axis, pairs + [(j, i) for i, j in pairs])


def on_device(fields, region_levels):
    shape = jax.ShapeDtypeStruct
    params = pltpu.CompilerParams(vmem_limit_bytes=32 * 1024 * 1024)
    size = lax.axis_size("seg")
    wrap = swapped_pairs(fields, "seg", size - 1, size)
    close = swapped_pairs(fields, "seg", 0, size)
    far = swapped_pairs(fields, "seg", 1, size - 1)
    lev, lev_strips, corner, cols = pl.pallas_call(
        own_kernel,
        out_shape=(
            shape((128, COLS), jnp.int32),
            shape((104, COLS), jnp.int32),
            shape((2, 32, COLS), jnp.int32),
            shape((32, COLS), F32),
        ),
        in_specs=[HBM] * 2,
        out_specs=(VMEM,) * 4,
        scratch_shapes=[
            pltpu.VMEM(region_levels.shape[::-1], jnp.int32),
            pltpu.VMEM(fields.shape, F32),
            pltpu.VMEM((24, COLS), jnp.int32),
            pltpu.SemaphoreType.DMA((2,)),
        ],
        compiler_params=params,
    )(*(pltpu.with_memory_space_constraint(x, pltpu.HBM) for x in (region_levels.T, fields)))
    rows = shape((7, 8, COLS), F32)
    packed, below, above = pl.pallas_call(
        cols_kernel,
        out_shape=(shape((48, COLS), F32), rows, rows),
        in_specs=[VMEM] * 5,
        out_specs=(VMEM,) * 3,
        compiler_params=params,
    )(lev, cols, wrap, close, far)
    right = moved(packed, "sub", -1)
    left = moved(packed, "sub", 1)
    own = pl.pallas_call(
        rows_kernel,
        out_shape=shape((7, PAD + 136, COLS), F32),
        in_specs=[VMEM] * 4,
        out_specs=VMEM,
        scratch_shapes=[pltpu.VMEM((7, PAD + 136, COLS), F32)],
        compiler_params=params,
    )(lev, fields, below, above)

    def window(*lead):
        return pltpu.VMEM((*lead, PAD + 136, COLS), F32)

    def across(*lead):
        return pltpu.VMEM((*lead, TPAD + 144, COLS), F32)

    return pl.pallas_call(
        main_kernel,
        out_shape=shape(fields.shape, F32),
        in_specs=[VMEM] * 7,
        out_specs=HBM,
        scratch_shapes=[
            window(7),
            window(7),
            window(5),
            window(6),
            window(6),
            window(),
            window(5),
            window(),
            pltpu.VMEM((2, 40, COLS), F32),
            across(7),
            across(6),
            across(6),
            pltpu.VMEM((112, COLS), F32),
            pltpu.VMEM(fields.shape, F32),
            pltpu.SemaphoreType.DMA((7,)),
        ],
        compiler_params=params,
    )(lev, lev_strips, corner, fields, own, right, left)


def solution(mesh):
    placed = (P(None, "seg", "sub"), P())
    return jax.shard_map(
        on_device, mesh=mesh, in_specs=placed, out_specs=P(None, "seg", "sub"), check_vma=False
    )
```

```python
from functools import partial

import jax
import jax.numpy as jnp
from jax import lax
from jax.experimental import pallas as pl
from jax.experimental.pallas import tpu as pltpu
from jax.sharding import PartitionSpec as P

STEP_SIZE = 0.08
ROWS, COLS = 32, 128
F32 = jnp.float32
VMEM = pl.BlockSpec(memory_space=pltpu.VMEM)
HBM = pl.BlockSpec(memory_space=pltpu.HBM)

PAD = 8
TPAD = 16
MID, SIDE = PAD + 48, PAD + 80


def lane(rows):
    return lax.broadcasted_iota(jnp.int32, (rows, COLS), 1)


def gather_lanes(value, index):
    return jnp.take_along_axis(value, index, axis=1, mode="promise_in_bounds")


def near_rows(levels_ref, held_ref):
    sub_count, seg_count = levels_ref.shape
    for j in range(3):
        u = lax.rem(lax.axis_index("sub") + (j - 1 + sub_count), sub_count)
        held_ref[8 * j : 8 * j + 1, 0:seg_count] = levels_ref[pl.ds(u, 1), :]
    table = []
    for i in range(3):
        s = lax.rem(lax.axis_index("seg") + (i - 1 + seg_count), seg_count)
        s = jnp.full((8, COLS), s, jnp.int32)
        rows = [jnp.broadcast_to(held_ref[8 * j : 8 * j + 1, :], (8, COLS)) for j in range(3)]
        table.append([gather_lanes(row, s) for row in rows])

    def level_of(i, offset):
        first, middle, last = table[i]
        return jnp.where(offset < 0, first, jnp.where(offset > 0, last, middle))

    return level_of


def last_rows(ref, f, level):
    return jnp.where(
        level == 2, ref[f, 24:32, :], jnp.where(level == 1, ref[f, 8:16, :], ref[f, 0:8, :])
    )


def packed_cols(read, level):
    p = lane(8)
    first = jnp.where(level == 2, 120, jnp.where(level == 1, 56, 24))
    index = (p & 7) + jnp.where((p & 15) < 8, first, 0)
    packed = gather_lanes(read(0), index)
    for f in range(1, 7):
        packed = jnp.where((p >> 4) == f, gather_lanes(read(f), index), packed)
    return packed


def own_kernel(levels_hbm, fields_hbm, lev, lev_strips, corner, cols_ref, levels_ref, fields_ref, held, sems):
    copies = [
        pltpu.make_async_copy(levels_hbm, levels_ref, sems.at[0]),
        pltpu.make_async_copy(fields_hbm, fields_ref, sems.at[1]),
    ]
    for copy in copies:
        copy.start()
    copies[0].wait()
    level_of = near_rows(levels_ref, held)
    p8 = lane(8)
    inner = (p8 < 64) | ((p8 >= 80) & (p8 < 112))
    outer = ((p8 >= 64) & (p8 < 72)) | ((p8 >= 112) & (p8 < 120))
    middle = jnp.zeros((8, COLS), jnp.int32)
    offsets = (middle, jnp.where(inner, 0, jnp.where(outer, 1, -1)), jnp.where(p8 < 64, 1, -1))
    is_coarse = (p8 >= 72) & (p8 < 120)
    for kind, first in enumerate((0, 48, 80)):
        below_row, centre_row, above_row = (level_of(i, offsets[kind]) for i in range(3))
        lev[first : first + 8, :] = below_row
        lev[first + 8 : first + 16, :] = centre_row
        if kind == 1:
            lev[first + 16 : first + 24, :] = jnp.where(is_coarse, above_row, centre_row)
            lev[first + 24 : first + 32, :] = above_row
        else:
            for r in (16, 24, 32):
                lev[first + r : first + r + 8, :] = centre_row
            lev[first + 40 : first + 48, :] = above_row
    offset = jnp.where((p8 & 15) < 8, -1, 1)
    below_row, centre_row, above_row = (level_of(i, offset) for i in range(3))
    for first, count in ((0, 6), (48, 4), (80, 3)):
        for r in range(count):
            row = below_row if r == 0 else above_row if r == count - 1 else centre_row
            lev_strips[first + 8 * r : first + 8 * r + 8, :] = row
    beside = lev[48:80, :]
    beside = jnp.maximum(beside, pltpu.roll(beside, 1, 1))
    corner[0] = jnp.maximum(beside, pltpu.roll(beside, 1, 0))
    corner[1] = pltpu.roll(corner[0], 127, 1)
    own = lev[8:16, :]
    copies[1].wait()
    for r in range(0, 32, 8):
        cols_ref[r : r + 8, :] = packed_cols(lambda f: fields_ref[f, r : r + 8, :], own)


def cols_kernel(lev, cols_ref, close_ref, far_ref, first_ref, out_ref, below_ref, above_ref):
    seg = lax.axis_index("seg")
    even = jnp.full((8, COLS), lax.rem(seg, 2)) == 0
    early = jnp.full((8, COLS), seg) < 2
    below_level, above_level = lev[0:8, :], lev[40:48, :]
    for f in range(7):
        far, close, first = (last_rows(r, f, below_level) for r in (far_ref, close_ref, first_ref))
        below_ref[f] = jnp.where(even, far, jnp.where(early, first, close))
        close = jnp.where(early, first_ref[f, 0:8, :], close_ref[f, 0:8, :])
        above_ref[f] = jnp.where(even, close, far_ref[f, 0:8, :])
    out_ref[0:8, :] = packed_cols(lambda f: below_ref[f], below_level)
    out_ref[8:40, :] = cols_ref[...]
    out_ref[40:48, :] = packed_cols(lambda f: above_ref[f], above_level)


def minmod(a, b):
    return jnp.minimum(jnp.maximum(b, jnp.minimum(a, 0.0)), jnp.maximum(a, 0.0))


def riemann(left, right, normal):
    rho_l, vn_l, vt_l, vz_l, bt_l, bz_l = left
    rho_r, vn_r, vt_r, vz_r, bt_r, bz_r = right
    normal_square = normal * normal

    def signal(density, speed, square):
        total = density + (square + normal_square)
        return jnp.abs(speed) + jnp.abs(total) * lax.rsqrt(density * total)

    square_l = bt_l * bt_l + bz_l * bz_l
    square_r = bt_r * bt_r + bz_r * bz_r
    fastest = jnp.maximum(signal(rho_l, vn_l, square_l), signal(rho_r, vn_r, square_r))
    ahead, back = vn_l + fastest, vn_r - fastest
    mass_l, mass_r = rho_l * ahead, rho_r * back
    pressure = (rho_l + rho_r) + 0.5 * (square_l + square_r)
    return [
        mass_l + mass_r,
        (mass_l * vn_l + mass_r * vn_r) + (pressure - normal_square),
        (mass_l * vt_l + mass_r * vt_r) - normal * (bt_l + bt_r),
        (mass_l * vz_l + mass_r * vz_r) - normal * (bz_l + bz_r),
        (bt_l * ahead + bt_r * back) - normal * (vt_l + vt_r),
        (bz_l * ahead + bz_r * back) - normal * (vz_l + vz_r),
    ]


def doubled(part):
    low = lax.broadcasted_iota(jnp.int32, (8, COLS), 0) >> 1
    rows = []
    for r in range(0, part.shape[0], 8):
        for index in (low, low + 4):
            rows.append(
                jnp.take_along_axis(part[r : r + 8], index, axis=0, mode="promise_in_bounds")
            )
    return jnp.concatenate(rows, axis=0)


def rows_halved(ref, first, by_rows):
    initial = ref[pl.ds(first - 8, 32, stride=2), :]
    if not by_rows:
        return initial
    return 0.5 * (initial + ref[pl.ds(first - 7, 32, stride=2), :])


def paired_lanes(value, index, by_cols):
    initial = gather_lanes(value, index)
    return 0.5 * (initial + gather_lanes(value, index + 1)) if by_cols else initial


def down_two(ref, firsts, by_rows, by_cols, step=0):
    p = lane(32) + step
    index = (2 * p) & 127
    parts = [paired_lanes(rows_halved(ref, first, by_rows), index, by_cols) for first in firsts]
    return parts[0] if len(parts) == 1 else jnp.where((p & 127) < 64, parts[0], parts[1])


def down_one(ref, first, by_rows, by_cols, step=0):
    return paired_lanes(
        rows_halved(ref, first, by_rows), (2 * (lane(32) + step - 80)) & 127, by_cols
    )


def share_levels(win, out, lev, blocks, fields):
    p32, p24, p16 = lane(32), lane(24), lane(16)
    coarse32 = (p32 >= 72) & (p32 < 120)
    level_b = lev[48:80, :]
    up_one = jnp.where(p16 < 72, 80 + (p16 >> 1), jnp.where(p16 >= 120, 16 + (p16 >> 1), p16))
    up_two = (p24 >> 1, 64 + (p24 >> 1))
    for f in fields:
        by_rows, by_cols = f != 6, f != 5
        value = win[f, MID : MID + 32, :]
        up = doubled(gather_lanes(win[f, MID + 4 : MID + 20, :], up_one))
        part = win[f, MID + 4 : MID + 28, :]
        ups = [doubled(gather_lanes(part, up_two[k])) for k in range(len(blocks))]
        down = down_two(win.at[f], [PAD + first for first in blocks], by_rows, by_cols)
        last = down_one(win.at[f], MID, by_rows, by_cols)
        medium = jnp.where(level_b == 0, up, jnp.where(level_b == 2, down, value))
        coarse = jnp.where(level_b >= 1, last, value)
        for first, injected in zip(blocks, ups):
            rows = slice(PAD + first, PAD + first + 48)
            out[f, rows, :] = jnp.where(lev[first : first + 48, :] == 2, win[f, rows, :], injected)
        out[f, MID : MID + 32, :] = jnp.where(coarse32, coarse, medium)


def rows_kernel(lev, fields_ref, below_ref, above_ref, out_ref, win):
    p8 = lane(8)
    is_coarse = (p8 >= 72) & (p8 < 120)

    def joined(fine, coarse):
        return jnp.where(is_coarse, pltpu.roll(coarse, 80, 1), fine)

    for f in range(7):
        below, above = below_ref[f], above_ref[f]
        initial, second = fields_ref[f, 0:8, :], fields_ref[f, 8:16, :]
        win[f, PAD : PAD + 8, :] = below
        win[f, PAD + 8 : PAD + 40, :] = fields_ref[f]
        win[f, PAD + 40 : PAD + 48, :] = above
        win[f, MID : MID + 8, :] = joined(below, below)
        win[f, MID + 8 : MID + 16, :] = joined(initial, initial)
        win[f, MID + 16 : MID + 24, :] = joined(second, above)
        win[f, MID + 24 : MID + 32, :] = above
    share_levels(win, out_ref, lev, (0,), range(7))


def share_strips(strips, lev_strips, held):
    p = lane(32)
    k = p & 15
    up = (p - k) + jnp.where(k < 8, 4 + (k >> 1), 8 + ((k - 8) >> 1))
    down = (p - k) + ((2 * k - 8) & 15)
    held[8:56, :] = strips
    held[56:80, :] = strips[0:24]
    held[80:88, :] = strips[40:48]
    held[88:104, :] = strips[0:16]
    held[104:112, :] = strips[40:48]

    def halved(first, count):
        initial = held[pl.ds(first - 8, count, stride=2), :]
        mean = 0.5 * (initial + held[pl.ds(first - 7, count, stride=2), :])
        f = lane(count) >> 4
        value = jnp.where(f == 6, initial, mean)
        even, odd = (gather_lanes(value, down[0:count] + k) for k in range(2))
        return jnp.where(f == 5, even, 0.5 * (even + odd))

    levels = [lev_strips[first : first + count, :] for first, count in ((0, 48), (48, 32), (80, 24))]
    up_one = doubled(gather_lanes(held[92:108, :], up[0:16]))
    up_two = doubled(gather_lanes(held[60:84, :], up[0:24]))
    down_to_one, down_to_none = halved(8, 32), halved(56, 24)
    fine = jnp.where(levels[0] == 2, held[8:56, :], up_two)
    medium = jnp.where(levels[1] == 2, down_to_one, held[56:88, :])
    medium = jnp.where(levels[1] == 0, up_one, medium)
    coarse = jnp.where(levels[2] >= 1, down_to_none, held[88:112, :])
    return fine, medium, coarse


def main_kernel(
    lev,
    lev_strips,
    corner,
    fields_ref,
    own_ref,
    right_ref,
    left_ref,
    out_ref,
    win,
    base,
    prim,
    lefty,
    fluxy,
    gx,
    diffx,
    edge,
    fixed,
    turned,
    leftx,
    fluxx,
    held,
    result,
    sems,
):
    p32, p8 = lane(32), lane(8)
    is_coarse = (p8 >= 72) & (p8 < 120)
    own_level = lev[8:16, :]

    p48 = lane(48)
    strips = jnp.where((p48 & 15) < 8, left_ref[...], right_ref[...])
    fine, medium, coarse = share_strips(strips, lev_strips, held)
    strip_one = ((p32 >= 64) & (p32 < 72)) | (p32 >= 120)
    strip_none = ((p32 >= 72) & (p32 < 80)) | ((p32 >= 112) & (p32 < 120))
    right_side = ((p32 >= 64) & (p32 < 72)) | ((p32 >= 112) & (p32 < 120))
    strip_index = (p32 & 7) + jnp.where(right_side, 8, 0)
    for f in range(7):
        index = strip_index + 16 * f
        base[f, PAD : PAD + 48, :] = own_ref[f, PAD : PAD + 48, :]
        base[f, SIDE : SIDE + 48, :] = pltpu.roll(fine, (120 - 16 * f) % 128, 1)
        value = jnp.where(strip_one, gather_lanes(medium, index), own_ref[f, MID : MID + 32, :])
        base[f, MID + 24 : MID + 32, :] = value[24:32]
        base[f, MID : MID + 24, :] = jnp.where(
            strip_none[0:24], gather_lanes(coarse, index[0:24]), value[0:24]
        )

    def swapped(value):
        outside = jnp.where(p8 < 48, pltpu.roll(value, 48, 1), pltpu.roll(value, 80, 1))
        return jnp.where((p8 >= 48) & (p8 < 80), value, outside)

    def turn(slot, value):
        value = value.T
        turned[slot, TPAD : TPAD + 128, :] = value
        turned[slot, TPAD - 8 : TPAD, :] = swapped(value[120:128])
        turned[slot, TPAD + 128 : TPAD + 136, :] = swapped(value[0:8])

    chunks = [PAD + 16 * c for c in range(8)]

    def primitives():
        for row in chunks:
            rows = slice(row, row + 16)
            inverse = 1.0 / base[0, rows, :]
            for i in range(3):
                prim[i, rows, :] = base[1 + i, rows, :] * inverse
            prim[3, rows, :] = 0.5 * (base[6, rows, :] + base[6, row + 1 : row + 17, :])
        for rows in row_sets:
            faces = [base[5, row : row + 8, :] for row in rows]
            for row, face, other in zip(rows, faces, beside_cols(faces, False)):
                prim[4, row : row + 8, :] = 0.5 * (face + other)
        sources = [(base, 0), (prim, 0), (prim, 1), (prim, 2), (prim, 3), (base, 4), (base, 5)]
        for slot, (ref, i) in enumerate(sources):
            turn(slot, ref[i, PAD : PAD + 128, :])

    def sweep(items, lefts, row, count, normal):
        def at(item, step):
            ref, i = item
            return ref[i, row + step : row + step + count, :]

        left, right = [], []
        for i, item in enumerate(items):
            value = at(item, 0)
            slope = 0.5 * minmod(value - at(item, -1), at(item, 1) - value)
            lefts[i, row : row + count, :] = value + slope
            if normal is not None:
                left.append(lefts[i, row - 1 : row - 1 + count, :])
                right.append(value - slope)
        if normal is None:
            return None
        return riemann(left, right, at(normal, 0))

    def sweep_x():
        items = [(turned, i) for i in range(6)]
        sweep(items, leftx, TPAD - 8, 8, None)
        for row in [TPAD + 16 * c for c in range(9)]:
            count = 8 if row == TPAD + 128 else 16
            flux = sweep(items, leftx, row, count, (turned, 6))
            for i, value in enumerate(flux):
                fluxx[i, row : row + count, :] = value
        gx[PAD : PAD + 128, :] = fluxx[4, TPAD : TPAD + 128, :].T
        for i, n in enumerate((0, 1, 2, 3, 5)):
            value = fluxx[n, TPAD + 1 : TPAD + 129, :] - fluxx[n, TPAD : TPAD + 128, :]
            diffx[i, PAD : PAD + 128, :] = value.T

    def sweep_y():
        items = [(base, 0), (prim, 1), (prim, 0), (prim, 2), (prim, 4), (base, 4)]
        for row in chunks:
            flux = sweep(items, lefty, row, 16, (base, 6))
            for i, n in enumerate((0, 2, 1, 3, 5, 4)):
                fluxy[i, row : row + 16, :] = flux[n]

    def beside_cols(parts, back):
        parts = [pltpu.roll(part, 1 if back else 127, 1) for part in parts]
        edge_lane = p8 == (0 if back else 127)
        return [
            jnp.where(edge_lane, parts[1], parts[0]),
            jnp.where(edge_lane, parts[0], parts[1]),
        ] + parts[2:]

    row_sets = [
        (PAD + 8 * c, SIDE + 8 * c) + ((MID + 8 * c,) if c < 4 else ()) for c in range(6)
    ]

    def edges():
        for rows in row_sets:
            shifted = beside_cols([fluxy[5, row : row + 8, :] for row in rows], True)
            for row, other in zip(rows, shifted):
                value = (fluxy[5, row : row + 8, :] + other) - (
                    gx[row : row + 8, :] + gx[row - 1 : row + 7, :]
                )
                edge[row : row + 8, :] = 0.125 * value

    def correct():
        value = edge[MID : MID + 32, :]
        values = (value, pltpu.roll(value, 127, 1))
        for step in range(2):
            finest = corner[step]
            coarse = (p32 + step >= 72) & (p32 + step < 120)
            halved_two = down_two(edge, (PAD, SIDE), False, False, step)
            halved_one = down_one(edge, MID, False, False, step)
            value = jnp.where((finest == 2) & ~coarse, halved_two, values[step])
            fixed[step, 0:32, :] = jnp.where((finest >= 1) & coarse, halved_one, value)

    def update_cells(i):
        for rows in row_sets:
            for k, row in enumerate(rows):
                part = slice(row, row + 8)
                change = diffx[i, part, :] + (fluxy[i, row + 1 : row + 9, :] - fluxy[i, part, :])
                win[i, part, :] = base[i, part, :] - 0.5 * ratios[k] * change

    def update_faces():
        for rows in row_sets:
            values = [edge[row : row + 8, :] for row in rows[:2]]
            above = [edge[row + 1 : row + 9, :] for row in rows[:2]]
            others = beside_cols(values, False)
            for row in rows[2:]:
                first = row - MID
                values.append(fixed[0, first : first + 8, :])
                above.append(fixed[0, first + 1 : first + 9, :])
                others.append(fixed[1, first : first + 8, :])
            for row, ratio, value, up, other in zip(rows, ratios, values, above, others):
                part = slice(row, row + 8)
                win[5, part, :] = base[5, part, :] - ratio * (up - value)
                win[6, part, :] = base[6, part, :] + ratio * (other - value)

    ratios = (STEP_SIZE, STEP_SIZE, jnp.where(is_coarse, STEP_SIZE / 4, STEP_SIZE / 2))

    def shared(fields):
        share_levels(win, base, lev, (0, 80), fields)

    def finish(fields):
        zero = jnp.zeros((8, COLS), F32)
        for f in fields:
            for c in range(4):
                value = win[f, PAD + 8 + 8 * c : PAD + 16 + 8 * c, :]
                if c < 2:
                    medium = win[f, MID + 8 + 8 * c : MID + 16 + 8 * c, :]
                    coarse = pltpu.roll(medium, 48, 1) if c == 0 else zero
                    lower = jnp.where(own_level == 1, medium, coarse)
                    value = jnp.where(own_level == 2, value, lower)
                used = p8 < jnp.where(own_level == 2, 128, jnp.where(own_level == 1, 64, 32))
                used = used & (own_level >= (0, 1, 2, 2)[c])
                blend = 0.5 * (fields_ref[f, 8 * c : 8 * c + 8, :] + value)
                result[f, 8 * c : 8 * c + 8, :] = jnp.where(used, blend, 0.0)
            pltpu.make_async_copy(result.at[f], out_ref.at[f], sems.at[f]).start()

    for section in range(2):
        then = (shared, finish)[section]
        primitives()
        sweep_x()
        sweep_y()
        edges()
        update_cells(0)
        then((0,))
        correct()
        for i in range(1, 5):
            update_cells(i)
            then((i,))
            if i == 2:
                update_faces()
        then((5, 6))
    for f in range(7):
        pltpu.make_async_copy(result.at[f], out_ref.at[f], sems.at[f]).wait()


def moved(value, axis, step):
    size = lax.axis_size(axis)
    return lax.ppermute(value, axis, [(i, (i + step) % size) for i in range(size)])


def swapped_pairs(value, axis, first, stop):
    size = lax.axis_size(axis)
    pairs = [(i, (i + 1) % size) for i in range(first, stop, 2)]
    return lax.ppermute(value, axis, pairs + [(j, i) for i, j in pairs])


def on_device(fields, region_levels):
    shape = jax.ShapeDtypeStruct
    params = pltpu.CompilerParams(vmem_limit_bytes=32 * 1024 * 1024)
    size = lax.axis_size("seg")
    close = swapped_pairs(fields, "seg", 2, size)
    far = swapped_pairs(fields, "seg", 1, size)
    first = swapped_pairs(fields, "seg", 0, 2)
    lev, lev_strips, corner, cols = pl.pallas_call(
        own_kernel,
        out_shape=(
            shape((128, COLS), jnp.int32),
            shape((104, COLS), jnp.int32),
            shape((2, 32, COLS), jnp.int32),
            shape((32, COLS), F32),
        ),
        in_specs=[HBM] * 2,
        out_specs=(VMEM,) * 4,
        scratch_shapes=[
            pltpu.VMEM(region_levels.shape[::-1], jnp.int32),
            pltpu.VMEM(fields.shape, F32),
            pltpu.VMEM((24, COLS), jnp.int32),
            pltpu.SemaphoreType.DMA((2,)),
        ],
        compiler_params=params,
    )(*(pltpu.with_memory_space_constraint(x, pltpu.HBM) for x in (region_levels.T, fields)))
    rows = shape((7, 8, COLS), F32)
    packed, below, above = pl.pallas_call(
        cols_kernel,
        out_shape=(shape((48, COLS), F32), rows, rows),
        in_specs=[VMEM] * 5,
        out_specs=(VMEM,) * 3,
        compiler_params=params,
    )(lev, cols, close, far, first)
    right = moved(packed, "sub", -1)
    left = moved(packed, "sub", 1)
    own = pl.pallas_call(
        rows_kernel,
        out_shape=shape((7, PAD + 136, COLS), F32),
        in_specs=[VMEM] * 4,
        out_specs=VMEM,
        scratch_shapes=[pltpu.VMEM((7, PAD + 136, COLS), F32)],
        compiler_params=params,
    )(lev, fields, below, above)

    def window(*lead):
        return pltpu.VMEM((*lead, PAD + 136, COLS), F32)

    def across(*lead):
        return pltpu.VMEM((*lead, TPAD + 144, COLS), F32)

    return pl.pallas_call(
        main_kernel,
        out_shape=shape(fields.shape, F32),
        in_specs=[VMEM] * 7,
        out_specs=HBM,
        scratch_shapes=[
            window(7),
            window(7),
            window(5),
            window(6),
            window(6),
            window(),
            window(5),
            window(),
            pltpu.VMEM((2, 40, COLS), F32),
            across(7),
            across(6),
            across(6),
            pltpu.VMEM((112, COLS), F32),
            pltpu.VMEM(fields.shape, F32),
            pltpu.SemaphoreType.DMA((7,)),
        ],
        compiler_params=params,
    )(lev, lev_strips, corner, fields, own, right, left)


def solution(mesh):
    placed = (P(None, "seg", "sub"), P())
    return jax.shard_map(
        on_device, mesh=mesh, in_specs=placed, out_specs=P(None, "seg", "sub"), check_vma=False
    )
```

```python
from functools import partial

import jax
import jax.numpy as jnp
from jax import lax
from jax.experimental import pallas as pl
from jax.experimental.pallas import tpu as pltpu
from jax.sharding import PartitionSpec as P

STEP_SIZE = 0.08
ROWS, COLS = 32, 128
F32 = jnp.float32
VMEM = pl.BlockSpec(memory_space=pltpu.VMEM)
HBM = pl.BlockSpec(memory_space=pltpu.HBM)

PAD = 8
TPAD = 16
MID, SIDE = PAD + 48, PAD + 80


def lane(rows):
    return lax.broadcasted_iota(jnp.int32, (rows, COLS), 1)


def gather_lanes(value, index):
    return jnp.take_along_axis(value, index, axis=1, mode="promise_in_bounds")


def near_rows(levels_ref, held_ref):
    sub_count, seg_count = levels_ref.shape
    for j in range(3):
        u = lax.rem(lax.axis_index("sub") + (j - 1 + sub_count), sub_count)
        held_ref[8 * j : 8 * j + 1, 0:seg_count] = levels_ref[pl.ds(u, 1), :]
    table = []
    for i in range(3):
        s = lax.rem(lax.axis_index("seg") + (i - 1 + seg_count), seg_count)
        s = jnp.full((8, COLS), s, jnp.int32)
        rows = [jnp.broadcast_to(held_ref[8 * j : 8 * j + 1, :], (8, COLS)) for j in range(3)]
        table.append([gather_lanes(row, s) for row in rows])

    def level_of(i, offset):
        first, middle, last = table[i]
        return jnp.where(offset < 0, first, jnp.where(offset > 0, last, middle))

    return level_of


def last_rows(ref, f, level):
    return jnp.where(
        level == 2, ref[f, 24:32, :], jnp.where(level == 1, ref[f, 8:16, :], ref[f, 0:8, :])
    )


def packed_cols(read, level):
    p = lane(8)
    first = jnp.where(level == 2, 120, jnp.where(level == 1, 56, 24))
    index = (p & 7) + jnp.where((p & 15) < 8, first, 0)
    packed = gather_lanes(read(0), index)
    for f in range(1, 7):
        packed = jnp.where((p >> 4) == f, gather_lanes(read(f), index), packed)
    return packed


def own_kernel(levels_hbm, fields_hbm, lev, lev_strips, corner, cols_ref, levels_ref, fields_ref, held, sems):
    copies = [
        pltpu.make_async_copy(levels_hbm, levels_ref, sems.at[0]),
        pltpu.make_async_copy(fields_hbm, fields_ref, sems.at[1]),
    ]
    for copy in copies:
        copy.start()
    copies[0].wait()
    level_of = near_rows(levels_ref, held)
    p8 = lane(8)
    inner = (p8 < 64) | ((p8 >= 80) & (p8 < 112))
    outer = ((p8 >= 64) & (p8 < 72)) | ((p8 >= 112) & (p8 < 120))
    middle = jnp.zeros((8, COLS), jnp.int32)
    offsets = (middle, jnp.where(inner, 0, jnp.where(outer, 1, -1)), jnp.where(p8 < 64, 1, -1))
    is_coarse = (p8 >= 72) & (p8 < 120)
    for kind, first in enumerate((0, 48, 80)):
        below_row, centre_row, above_row = (level_of(i, offsets[kind]) for i in range(3))
        lev[first : first + 8, :] = below_row
        lev[first + 8 : first + 16, :] = centre_row
        if kind == 1:
            lev[first + 16 : first + 24, :] = jnp.where(is_coarse, above_row, centre_row)
            lev[first + 24 : first + 32, :] = above_row
        else:
            for r in (16, 24, 32):
                lev[first + r : first + r + 8, :] = centre_row
            lev[first + 40 : first + 48, :] = above_row
    offset = jnp.where((p8 & 15) < 8, -1, 1)
    below_row, centre_row, above_row = (level_of(i, offset) for i in range(3))
    for first, count in ((0, 6), (48, 4), (80, 3)):
        for r in range(count):
            row = below_row if r == 0 else above_row if r == count - 1 else centre_row
            lev_strips[first + 8 * r : first + 8 * r + 8, :] = row
    beside = lev[48:80, :]
    beside = jnp.maximum(beside, pltpu.roll(beside, 1, 1))
    corner[0] = jnp.maximum(beside, pltpu.roll(beside, 1, 0))
    corner[1] = pltpu.roll(corner[0], 127, 1)
    own = lev[8:16, :]
    copies[1].wait()
    for r in range(0, 32, 8):
        cols_ref[r : r + 8, :] = packed_cols(lambda f: fields_ref[f, r : r + 8, :], own)


def cols_kernel(lev, cols_ref, close_ref, far_ref, first_ref, out_ref, below_ref, above_ref):
    seg = lax.axis_index("seg")
    even = jnp.full((8, COLS), lax.rem(seg, 2)) == 0
    early = jnp.full((8, COLS), seg) < 2
    below_level, above_level = lev[0:8, :], lev[40:48, :]
    for f in range(7):
        far, close, first = (last_rows(r, f, below_level) for r in (far_ref, close_ref, first_ref))
        below_ref[f] = jnp.where(even, far, jnp.where(early, first, close))
        close = jnp.where(early, first_ref[f, 0:8, :], close_ref[f, 0:8, :])
        above_ref[f] = jnp.where(even, close, far_ref[f, 0:8, :])
    out_ref[0:8, :] = packed_cols(lambda f: below_ref[f], below_level)
    out_ref[8:40, :] = cols_ref[...]
    out_ref[40:48, :] = packed_cols(lambda f: above_ref[f], above_level)


def minmod(a, b):
    return jnp.minimum(jnp.maximum(b, jnp.minimum(a, 0.0)), jnp.maximum(a, 0.0))


def riemann(left, right, normal):
    rho_l, vn_l, vt_l, vz_l, bt_l, bz_l = left
    rho_r, vn_r, vt_r, vz_r, bt_r, bz_r = right
    normal_square = normal * normal

    def signal(density, speed, square):
        total = density + (square + normal_square)
        return jnp.abs(speed) + jnp.abs(total) * lax.rsqrt(density * total)

    square_l = bt_l * bt_l + bz_l * bz_l
    square_r = bt_r * bt_r + bz_r * bz_r
    fastest = jnp.maximum(signal(rho_l, vn_l, square_l), signal(rho_r, vn_r, square_r))
    ahead, back = vn_l + fastest, vn_r - fastest
    mass_l, mass_r = rho_l * ahead, rho_r * back
    pressure = (rho_l + rho_r) + 0.5 * (square_l + square_r)
    return [
        mass_l + mass_r,
        (mass_l * vn_l + mass_r * vn_r) + (pressure - normal_square),
        (mass_l * vt_l + mass_r * vt_r) - normal * (bt_l + bt_r),
        (mass_l * vz_l + mass_r * vz_r) - normal * (bz_l + bz_r),
        (bt_l * ahead + bt_r * back) - normal * (vt_l + vt_r),
        (bz_l * ahead + bz_r * back) - normal * (vz_l + vz_r),
    ]


def doubled(part):
    low = lax.broadcasted_iota(jnp.int32, (8, COLS), 0) >> 1
    rows = []
    for r in range(0, part.shape[0], 8):
        for index in (low, low + 4):
            rows.append(
                jnp.take_along_axis(part[r : r + 8], index, axis=0, mode="promise_in_bounds")
            )
    return jnp.concatenate(rows, axis=0)


def rows_halved(ref, first, by_rows):
    initial = ref[pl.ds(first - 8, 32, stride=2), :]
    if not by_rows:
        return initial
    return 0.5 * (initial + ref[pl.ds(first - 7, 32, stride=2), :])


def paired_lanes(value, index, by_cols):
    initial = gather_lanes(value, index)
    return 0.5 * (initial + gather_lanes(value, index + 1)) if by_cols else initial


def down_two(ref, firsts, by_rows, by_cols, step=0):
    p = lane(32) + step
    index = (2 * p) & 127
    parts = [paired_lanes(rows_halved(ref, first, by_rows), index, by_cols) for first in firsts]
    return parts[0] if len(parts) == 1 else jnp.where((p & 127) < 64, parts[0], parts[1])


def down_one(ref, first, by_rows, by_cols, step=0):
    return paired_lanes(
        rows_halved(ref, first, by_rows), (2 * (lane(32) + step - 80)) & 127, by_cols
    )


def share_levels(win, out, lev, blocks, fields):
    p32, p24, p16 = lane(32), lane(24), lane(16)
    coarse32 = (p32 >= 72) & (p32 < 120)
    level_b = lev[48:80, :]
    up_one = jnp.where(p16 < 72, 80 + (p16 >> 1), jnp.where(p16 >= 120, 16 + (p16 >> 1), p16))
    up_two = (p24 >> 1, 64 + (p24 >> 1))
    for f in fields:
        by_rows, by_cols = f != 6, f != 5
        value = win[f, MID : MID + 32, :]
        up = doubled(gather_lanes(win[f, MID + 4 : MID + 20, :], up_one))
        part = win[f, MID + 4 : MID + 28, :]
        ups = [doubled(gather_lanes(part, up_two[k])) for k in range(len(blocks))]
        down = down_two(win.at[f], [PAD + first for first in blocks], by_rows, by_cols)
        last = down_one(win.at[f], MID, by_rows, by_cols)
        medium = jnp.where(level_b == 0, up, jnp.where(level_b == 2, down, value))
        coarse = jnp.where(level_b >= 1, last, value)
        for first, injected in zip(blocks, ups):
            rows = slice(PAD + first, PAD + first + 48)
            out[f, rows, :] = jnp.where(lev[first : first + 48, :] == 2, win[f, rows, :], injected)
        out[f, MID : MID + 32, :] = jnp.where(coarse32, coarse, medium)


def rows_kernel(lev, fields_ref, below_ref, above_ref, out_ref, win):
    p8 = lane(8)
    is_coarse = (p8 >= 72) & (p8 < 120)

    def joined(fine, coarse):
        return jnp.where(is_coarse, pltpu.roll(coarse, 80, 1), fine)

    for f in range(7):
        below, above = below_ref[f], above_ref[f]
        initial, second = fields_ref[f, 0:8, :], fields_ref[f, 8:16, :]
        win[f, PAD : PAD + 8, :] = below
        win[f, PAD + 8 : PAD + 40, :] = fields_ref[f]
        win[f, PAD + 40 : PAD + 48, :] = above
        win[f, MID : MID + 8, :] = joined(below, below)
        win[f, MID + 8 : MID + 16, :] = joined(initial, initial)
        win[f, MID + 16 : MID + 24, :] = joined(second, above)
        win[f, MID + 24 : MID + 32, :] = above
    share_levels(win, out_ref, lev, (0,), range(7))


def share_strips(strips, lev_strips, held):
    p = lane(32)
    k = p & 15
    up = (p - k) + jnp.where(k < 8, 4 + (k >> 1), 8 + ((k - 8) >> 1))
    down = (p - k) + ((2 * k - 8) & 15)
    held[8:56, :] = strips
    held[56:80, :] = strips[0:24]
    held[80:88, :] = strips[40:48]
    held[88:104, :] = strips[0:16]
    held[104:112, :] = strips[40:48]

    def halved(first, count):
        initial = held[pl.ds(first - 8, count, stride=2), :]
        mean = 0.5 * (initial + held[pl.ds(first - 7, count, stride=2), :])
        f = lane(count) >> 4
        value = jnp.where(f == 6, initial, mean)
        even, odd = (gather_lanes(value, down[0:count] + k) for k in range(2))
        return jnp.where(f == 5, even, 0.5 * (even + odd))

    levels = [lev_strips[first : first + count, :] for first, count in ((0, 48), (48, 32), (80, 24))]
    up_one = doubled(gather_lanes(held[92:108, :], up[0:16]))
    up_two = doubled(gather_lanes(held[60:84, :], up[0:24]))
    down_to_one, down_to_none = halved(8, 32), halved(56, 24)
    fine = jnp.where(levels[0] == 2, held[8:56, :], up_two)
    medium = jnp.where(levels[1] == 2, down_to_one, held[56:88, :])
    medium = jnp.where(levels[1] == 0, up_one, medium)
    coarse = jnp.where(levels[2] >= 1, down_to_none, held[88:112, :])
    return fine, medium, coarse


def main_kernel(
    lev,
    lev_strips,
    corner,
    fields_ref,
    own_ref,
    last_ref,
    far_ref,
    near_ref,
    out_ref,
    win,
    base,
    prim,
    lefty,
    fluxy,
    gx,
    diffx,
    edge,
    fixed,
    turned,
    leftx,
    fluxx,
    held,
    result,
    sems,
):
    p32, p8 = lane(32), lane(8)
    is_coarse = (p8 >= 72) & (p8 < 120)
    own_level = lev[8:16, :]

    p48 = lane(48)
    sub, count = lax.axis_index("sub"), lax.axis_size("sub")
    even = jnp.full((48, COLS), lax.rem(sub, 2)) == 0
    near = jnp.where(jnp.full((48, COLS), sub) >= count - 2, last_ref[...], near_ref[...])
    strips = jnp.where(((p48 & 15) < 8) == even, far_ref[...], near)
    fine, medium, coarse = share_strips(strips, lev_strips, held)
    strip_one = ((p32 >= 64) & (p32 < 72)) | (p32 >= 120)
    strip_none = ((p32 >= 72) & (p32 < 80)) | ((p32 >= 112) & (p32 < 120))
    right_side = ((p32 >= 64) & (p32 < 72)) | ((p32 >= 112) & (p32 < 120))
    strip_index = (p32 & 7) + jnp.where(right_side, 8, 0)
    for f in range(7):
        index = strip_index + 16 * f
        base[f, PAD : PAD + 48, :] = own_ref[f, PAD : PAD + 48, :]
        base[f, SIDE : SIDE + 48, :] = pltpu.roll(fine, (120 - 16 * f) % 128, 1)
        value = jnp.where(strip_one, gather_lanes(medium, index), own_ref[f, MID : MID + 32, :])
        base[f, MID + 24 : MID + 32, :] = value[24:32]
        base[f, MID : MID + 24, :] = jnp.where(
            strip_none[0:24], gather_lanes(coarse, index[0:24]), value[0:24]
        )

    def swapped(value):
        outside = jnp.where(p8 < 48, pltpu.roll(value, 48, 1), pltpu.roll(value, 80, 1))
        return jnp.where((p8 >= 48) & (p8 < 80), value, outside)

    def turn(slot, value):
        value = value.T
        turned[slot, TPAD : TPAD + 128, :] = value
        turned[slot, TPAD - 8 : TPAD, :] = swapped(value[120:128])
        turned[slot, TPAD + 128 : TPAD + 136, :] = swapped(value[0:8])

    chunks = [PAD + 16 * c for c in range(8)]

    def primitives():
        for row in chunks:
            rows = slice(row, row + 16)
            inverse = 1.0 / base[0, rows, :]
            for i in range(3):
                prim[i, rows, :] = base[1 + i, rows, :] * inverse
            prim[3, rows, :] = 0.5 * (base[6, rows, :] + base[6, row + 1 : row + 17, :])
        for rows in row_sets:
            faces = [base[5, row : row + 8, :] for row in rows]
            for row, face, other in zip(rows, faces, beside_cols(faces, False)):
                prim[4, row : row + 8, :] = 0.5 * (face + other)
        sources = [(base, 0), (prim, 0), (prim, 1), (prim, 2), (prim, 3), (base, 4), (base, 5)]
        for slot, (ref, i) in enumerate(sources):
            turn(slot, ref[i, PAD : PAD + 128, :])

    def sweep(items, lefts, row, count, normal):
        def at(item, step):
            ref, i = item
            return ref[i, row + step : row + step + count, :]

        left, right = [], []
        for i, item in enumerate(items):
            value = at(item, 0)
            slope = 0.5 * minmod(value - at(item, -1), at(item, 1) - value)
            lefts[i, row : row + count, :] = value + slope
            if normal is not None:
                left.append(lefts[i, row - 1 : row - 1 + count, :])
                right.append(value - slope)
        if normal is None:
            return None
        return riemann(left, right, at(normal, 0))

    def sweep_x():
        items = [(turned, i) for i in range(6)]
        sweep(items, leftx, TPAD - 8, 8, None)
        for row in [TPAD + 16 * c for c in range(9)]:
            count = 8 if row == TPAD + 128 else 16
            flux = sweep(items, leftx, row, count, (turned, 6))
            for i, value in enumerate(flux):
                fluxx[i, row : row + count, :] = value
        gx[PAD : PAD + 128, :] = fluxx[4, TPAD : TPAD + 128, :].T
        for i, n in enumerate((0, 1, 2, 3, 5)):
            value = fluxx[n, TPAD + 1 : TPAD + 129, :] - fluxx[n, TPAD : TPAD + 128, :]
            diffx[i, PAD : PAD + 128, :] = value.T

    def sweep_y(last):
        items = [(base, 0), (prim, 1), (prim, 0), (prim, 2), (prim, 4), (base, 4)]
        for row in chunks:
            flux = sweep(items, lefty, row, 16, (base, 6))
            for i, n in enumerate((0, 2, 1, 3, 5, 4)):
                if i == 5 or row < SIDE or not last:
                    fluxy[i, row : row + 16, :] = flux[n]

    def beside_cols(parts, back):
        parts = [pltpu.roll(part, 1 if back else 127, 1) for part in parts]
        edge_lane = p8 == (0 if back else 127)
        return [
            jnp.where(edge_lane, parts[1], parts[0]),
            jnp.where(edge_lane, parts[0], parts[1]),
        ] + parts[2:]

    row_sets = [
        (PAD + 8 * c, SIDE + 8 * c) + ((MID + 8 * c,) if c < 4 else ()) for c in range(6)
    ]

    def edges():
        for rows in row_sets:
            shifted = beside_cols([fluxy[5, row : row + 8, :] for row in rows], True)
            for row, other in zip(rows, shifted):
                value = (fluxy[5, row : row + 8, :] + other) - (
                    gx[row : row + 8, :] + gx[row - 1 : row + 7, :]
                )
                edge[row : row + 8, :] = 0.125 * value

    def correct():
        value = edge[MID : MID + 32, :]
        values = (value, pltpu.roll(value, 127, 1))
        for step in range(2):
            finest = corner[step]
            coarse = (p32 + step >= 72) & (p32 + step < 120)
            halved_two = down_two(edge, (PAD, SIDE), False, False, step)
            halved_one = down_one(edge, MID, False, False, step)
            value = jnp.where((finest == 2) & ~coarse, halved_two, values[step])
            fixed[step, 0:32, :] = jnp.where((finest >= 1) & coarse, halved_one, value)

    def is_own(row):
        return PAD + 8 <= row < PAD + 40 or MID + 8 <= row < MID + 24

    def update_cells(i, last):
        for rows in row_sets:
            for k, row in enumerate(rows):
                if last and not is_own(row):
                    continue
                part = slice(row, row + 8)
                change = diffx[i, part, :] + (fluxy[i, row + 1 : row + 9, :] - fluxy[i, part, :])
                win[i, part, :] = base[i, part, :] - 0.5 * ratios[k] * change

    def update_faces(last):
        for rows in row_sets:
            values = [edge[row : row + 8, :] for row in rows[:2]]
            above = [edge[row + 1 : row + 9, :] for row in rows[:2]]
            others = beside_cols(values, False)
            for row in rows[2:]:
                first = row - MID
                values.append(fixed[0, first : first + 8, :])
                above.append(fixed[0, first + 1 : first + 9, :])
                others.append(fixed[1, first : first + 8, :])
            for row, ratio, value, up, other in zip(rows, ratios, values, above, others):
                if last and not is_own(row):
                    continue
                part = slice(row, row + 8)
                win[5, part, :] = base[5, part, :] - ratio * (up - value)
                win[6, part, :] = base[6, part, :] + ratio * (other - value)

    ratios = (STEP_SIZE, STEP_SIZE, jnp.where(is_coarse, STEP_SIZE / 4, STEP_SIZE / 2))

    def shared(fields):
        share_levels(win, base, lev, (0, 80), fields)

    def finish(fields):
        zero = jnp.zeros((8, COLS), F32)
        for f in fields:
            for c in range(4):
                value = win[f, PAD + 8 + 8 * c : PAD + 16 + 8 * c, :]
                if c < 2:
                    medium = win[f, MID + 8 + 8 * c : MID + 16 + 8 * c, :]
                    coarse = pltpu.roll(medium, 48, 1) if c == 0 else zero
                    lower = jnp.where(own_level == 1, medium, coarse)
                    value = jnp.where(own_level == 2, value, lower)
                used = p8 < jnp.where(own_level == 2, 128, jnp.where(own_level == 1, 64, 32))
                used = used & (own_level >= (0, 1, 2, 2)[c])
                blend = 0.5 * (fields_ref[f, 8 * c : 8 * c + 8, :] + value)
                result[f, 8 * c : 8 * c + 8, :] = jnp.where(used, blend, 0.0)
            pltpu.make_async_copy(result.at[f], out_ref.at[f], sems.at[f]).start()

    for section in range(2):
        last = section == 1
        then = (shared, finish)[section]
        primitives()
        sweep_y(last)
        sweep_x()
        edges()
        correct()
        update_cells(0, last)
        then((0,))
        update_faces(last)
        update_cells(1, last)
        then((1,))
        then((5, 6))
        for i in range(2, 5):
            update_cells(i, last)
            then((i,))
    for f in range(7):
        pltpu.make_async_copy(result.at[f], out_ref.at[f], sems.at[f]).wait()


def swapped_pairs(value, axis, first, stop):
    size = lax.axis_size(axis)
    pairs = [(i, (i + 1) % size) for i in range(first, stop, 2)]
    return lax.ppermute(value, axis, pairs + [(j, i) for i, j in pairs])


def on_device(fields, region_levels):
    shape = jax.ShapeDtypeStruct
    params = pltpu.CompilerParams(vmem_limit_bytes=32 * 1024 * 1024)
    size = lax.axis_size("seg")
    close = swapped_pairs(fields, "seg", 2, size)
    far = swapped_pairs(fields, "seg", 1, size)
    first = swapped_pairs(fields, "seg", 0, 2)
    lev, lev_strips, corner, cols = pl.pallas_call(
        own_kernel,
        out_shape=(
            shape((128, COLS), jnp.int32),
            shape((104, COLS), jnp.int32),
            shape((2, 32, COLS), jnp.int32),
            shape((32, COLS), F32),
        ),
        in_specs=[HBM] * 2,
        out_specs=(VMEM,) * 4,
        scratch_shapes=[
            pltpu.VMEM(region_levels.shape[::-1], jnp.int32),
            pltpu.VMEM(fields.shape, F32),
            pltpu.VMEM((24, COLS), jnp.int32),
            pltpu.SemaphoreType.DMA((2,)),
        ],
        compiler_params=params,
    )(*(pltpu.with_memory_space_constraint(x, pltpu.HBM) for x in (region_levels.T, fields)))
    rows = shape((7, 8, COLS), F32)
    packed, below, above = pl.pallas_call(
        cols_kernel,
        out_shape=(shape((48, COLS), F32), rows, rows),
        in_specs=[VMEM] * 5,
        out_specs=(VMEM,) * 3,
        compiler_params=params,
    )(lev, cols, close, far, first)
    count = lax.axis_size("sub")
    end = swapped_pairs(packed, "sub", count - 2, count)
    far = swapped_pairs(packed, "sub", 1, count)
    near = swapped_pairs(packed, "sub", 0, count - 2)
    own = pl.pallas_call(
        rows_kernel,
        out_shape=shape((7, PAD + 136, COLS), F32),
        in_specs=[VMEM] * 4,
        out_specs=VMEM,
        scratch_shapes=[pltpu.VMEM((7, PAD + 136, COLS), F32)],
        compiler_params=params,
    )(lev, fields, below, above)

    def window(*lead):
        return pltpu.VMEM((*lead, PAD + 136, COLS), F32)

    def across(*lead):
        return pltpu.VMEM((*lead, TPAD + 144, COLS), F32)

    return pl.pallas_call(
        main_kernel,
        out_shape=shape(fields.shape, F32),
        in_specs=[VMEM] * 8,
        out_specs=HBM,
        scratch_shapes=[
            window(7),
            window(7),
            window(5),
            window(6),
            window(6),
            window(),
            window(5),
            window(),
            pltpu.VMEM((2, 40, COLS), F32),
            across(7),
            across(6),
            across(6),
            pltpu.VMEM((112, COLS), F32),
            pltpu.VMEM(fields.shape, F32),
            pltpu.SemaphoreType.DMA((7,)),
        ],
        compiler_params=params,
    )(lev, lev_strips, corner, fields, own, end, far, near)


def solution(mesh):
    placed = (P(None, "seg", "sub"), P())
    return jax.shard_map(
        on_device, mesh=mesh, in_specs=placed, out_specs=P(None, "seg", "sub"), check_vma=False
    )
```

```python
from functools import partial

import jax
import jax.numpy as jnp
from jax import lax
from jax.experimental import pallas as pl
from jax.experimental.pallas import tpu as pltpu
from jax.sharding import PartitionSpec as P

STEP_SIZE = 0.08
ROWS, COLS = 32, 128
F32 = jnp.float32
VMEM = pl.BlockSpec(memory_space=pltpu.VMEM)
HBM = pl.BlockSpec(memory_space=pltpu.HBM)

PAD = 8
TPAD = 16
MID, SIDE = PAD + 48, PAD + 80


def lane(rows):
    return lax.broadcasted_iota(jnp.int32, (rows, COLS), 1)


def gather_lanes(value, index):
    return jnp.take_along_axis(value, index, axis=1, mode="promise_in_bounds")


def near_rows(levels_ref, held_ref):
    sub_count, seg_count = levels_ref.shape
    for j in range(3):
        u = lax.rem(lax.axis_index("sub") + (j - 1 + sub_count), sub_count)
        held_ref[8 * j : 8 * j + 1, 0:seg_count] = levels_ref[pl.ds(u, 1), :]
    table = []
    for i in range(3):
        s = lax.rem(lax.axis_index("seg") + (i - 1 + seg_count), seg_count)
        s = jnp.full((8, COLS), s, jnp.int32)
        rows = [jnp.broadcast_to(held_ref[8 * j : 8 * j + 1, :], (8, COLS)) for j in range(3)]
        table.append([gather_lanes(row, s) for row in rows])

    def level_of(i, offset):
        first, middle, last = table[i]
        return jnp.where(offset < 0, first, jnp.where(offset > 0, last, middle))

    return level_of


def last_rows(ref, f, level):
    return jnp.where(
        level == 2, ref[f, 24:32, :], jnp.where(level == 1, ref[f, 8:16, :], ref[f, 0:8, :])
    )


def packed_cols(read, level):
    p = lane(8)
    first = jnp.where(level == 2, 120, jnp.where(level == 1, 56, 24))
    index = (p & 7) + jnp.where((p & 15) < 8, first, 0)
    packed = gather_lanes(read(0), index)
    for f in range(1, 7):
        packed = jnp.where((p >> 4) == f, gather_lanes(read(f), index), packed)
    return packed


def own_kernel(
    levels_hbm,
    fields_hbm,
    lev,
    lev_strips,
    corner,
    cols_ref,
    far_ref,
    close_ref,
    levels_ref,
    fields_ref,
    held,
    sems,
):
    copies = [
        pltpu.make_async_copy(levels_hbm, levels_ref, sems.at[0]),
        pltpu.make_async_copy(fields_hbm, fields_ref, sems.at[1]),
    ]
    for copy in copies:
        copy.start()
    copies[0].wait()
    level_of = near_rows(levels_ref, held)
    p8 = lane(8)
    inner = (p8 < 64) | ((p8 >= 80) & (p8 < 112))
    outer = ((p8 >= 64) & (p8 < 72)) | ((p8 >= 112) & (p8 < 120))
    middle = jnp.zeros((8, COLS), jnp.int32)
    offsets = (middle, jnp.where(inner, 0, jnp.where(outer, 1, -1)), jnp.where(p8 < 64, 1, -1))
    is_coarse = (p8 >= 72) & (p8 < 120)
    for kind, first in enumerate((0, 48, 80)):
        below_row, centre_row, above_row = (level_of(i, offsets[kind]) for i in range(3))
        lev[first : first + 8, :] = below_row
        lev[first + 8 : first + 16, :] = centre_row
        if kind == 1:
            lev[first + 16 : first + 24, :] = jnp.where(is_coarse, above_row, centre_row)
            lev[first + 24 : first + 32, :] = above_row
        else:
            for r in (16, 24, 32):
                lev[first + r : first + r + 8, :] = centre_row
            lev[first + 40 : first + 48, :] = above_row
    offset = jnp.where((p8 & 15) < 8, -1, 1)
    below_row, centre_row, above_row = (level_of(i, offset) for i in range(3))
    for first, count in ((0, 6), (48, 4), (80, 3)):
        for r in range(count):
            row = below_row if r == 0 else above_row if r == count - 1 else centre_row
            lev_strips[first + 8 * r : first + 8 * r + 8, :] = row
    beside = lev[48:80, :]
    beside = jnp.maximum(beside, pltpu.roll(beside, 1, 1))
    corner[0] = jnp.maximum(beside, pltpu.roll(beside, 1, 0))
    corner[1] = pltpu.roll(corner[0], 127, 1)
    own = lev[8:16, :]
    copies[1].wait()
    even = jnp.full((8, COLS), lax.rem(lax.axis_index("seg"), 2)) == 0
    for f in range(7):
        first, last = fields_ref[f, 0:8, :], last_rows(fields_ref, f, own)
        far_ref[f] = jnp.where(even, first, last)
        close_ref[f] = jnp.where(even, last, first)
    for r in range(0, 32, 8):
        cols_ref[r : r + 8, :] = packed_cols(lambda f: fields_ref[f, r : r + 8, :], own)


def cols_kernel(lev, cols_ref, close_ref, far_ref, first_ref, out_ref, below_ref, above_ref):
    seg = lax.axis_index("seg")
    even = jnp.full((8, COLS), lax.rem(seg, 2)) == 0
    early = jnp.full((8, COLS), seg) < 2
    below_level, above_level = lev[0:8, :], lev[40:48, :]
    for f in range(7):
        close = jnp.where(early, first_ref[f], close_ref[f])
        below_ref[f] = jnp.where(even, far_ref[f], close)
        above_ref[f] = jnp.where(even, close, far_ref[f])
    out_ref[0:8, :] = packed_cols(lambda f: below_ref[f], below_level)
    out_ref[8:40, :] = cols_ref[...]
    out_ref[40:48, :] = packed_cols(lambda f: above_ref[f], above_level)


def minmod(a, b):
    return jnp.minimum(jnp.maximum(b, jnp.minimum(a, 0.0)), jnp.maximum(a, 0.0))


def riemann(left, right, normal):
    rho_l, vn_l, vt_l, vz_l, bt_l, bz_l = left
    rho_r, vn_r, vt_r, vz_r, bt_r, bz_r = right
    normal_square = normal * normal

    def signal(density, speed, square):
        total = density + (square + normal_square)
        return jnp.abs(speed) + jnp.abs(total) * lax.rsqrt(density * total)

    square_l = bt_l * bt_l + bz_l * bz_l
    square_r = bt_r * bt_r + bz_r * bz_r
    fastest = jnp.maximum(signal(rho_l, vn_l, square_l), signal(rho_r, vn_r, square_r))
    ahead, back = vn_l + fastest, vn_r - fastest
    mass_l, mass_r = rho_l * ahead, rho_r * back
    pressure = (rho_l + rho_r) + 0.5 * (square_l + square_r)
    return [
        mass_l + mass_r,
        (mass_l * vn_l + mass_r * vn_r) + (pressure - normal_square),
        (mass_l * vt_l + mass_r * vt_r) - normal * (bt_l + bt_r),
        (mass_l * vz_l + mass_r * vz_r) - normal * (bz_l + bz_r),
        (bt_l * ahead + bt_r * back) - normal * (vt_l + vt_r),
        (bz_l * ahead + bz_r * back) - normal * (vz_l + vz_r),
    ]


def doubled(part):
    low = lax.broadcasted_iota(jnp.int32, (8, COLS), 0) >> 1
    rows = []
    for r in range(0, part.shape[0], 8):
        for index in (low, low + 4):
            rows.append(
                jnp.take_along_axis(part[r : r + 8], index, axis=0, mode="promise_in_bounds")
            )
    return jnp.concatenate(rows, axis=0)


def rows_halved(ref, first, by_rows):
    initial = ref[pl.ds(first - 8, 32, stride=2), :]
    if not by_rows:
        return initial
    return 0.5 * (initial + ref[pl.ds(first - 7, 32, stride=2), :])


def paired_lanes(value, index, by_cols):
    initial = gather_lanes(value, index)
    return 0.5 * (initial + gather_lanes(value, index + 1)) if by_cols else initial


def down_two(ref, firsts, by_rows, by_cols, step=0):
    p = lane(32) + step
    index = (2 * p) & 127
    parts = [paired_lanes(rows_halved(ref, first, by_rows), index, by_cols) for first in firsts]
    return parts[0] if len(parts) == 1 else jnp.where((p & 127) < 64, parts[0], parts[1])


def down_one(ref, first, by_rows, by_cols, step=0):
    return paired_lanes(
        rows_halved(ref, first, by_rows), (2 * (lane(32) + step - 80)) & 127, by_cols
    )


def share_levels(win, out, lev, blocks, fields):
    p32, p24, p16 = lane(32), lane(24), lane(16)
    coarse32 = (p32 >= 72) & (p32 < 120)
    level_b = lev[48:80, :]
    up_one = jnp.where(p16 < 72, 80 + (p16 >> 1), jnp.where(p16 >= 120, 16 + (p16 >> 1), p16))
    up_two = (p24 >> 1, 64 + (p24 >> 1))
    for f in fields:
        by_rows, by_cols = f != 6, f != 5
        value = win[f, MID : MID + 32, :]
        up = doubled(gather_lanes(win[f, MID + 4 : MID + 20, :], up_one))
        part = win[f, MID + 4 : MID + 28, :]
        ups = [doubled(gather_lanes(part, up_two[k])) for k in range(len(blocks))]
        down = down_two(win.at[f], [PAD + first for first in blocks], by_rows, by_cols)
        last = down_one(win.at[f], MID, by_rows, by_cols)
        medium = jnp.where(level_b == 0, up, jnp.where(level_b == 2, down, value))
        coarse = jnp.where(level_b >= 1, last, value)
        for first, injected in zip(blocks, ups):
            rows = slice(PAD + first, PAD + first + 48)
            out[f, rows, :] = jnp.where(lev[first : first + 48, :] == 2, win[f, rows, :], injected)
        out[f, MID : MID + 32, :] = jnp.where(coarse32, coarse, medium)


def rows_kernel(lev, fields_ref, below_ref, above_ref, out_ref, win):
    p8 = lane(8)
    is_coarse = (p8 >= 72) & (p8 < 120)

    def joined(fine, coarse):
        return jnp.where(is_coarse, pltpu.roll(coarse, 80, 1), fine)

    for f in range(7):
        below, above = below_ref[f], above_ref[f]
        initial, second = fields_ref[f, 0:8, :], fields_ref[f, 8:16, :]
        win[f, PAD : PAD + 8, :] = below
        win[f, PAD + 8 : PAD + 40, :] = fields_ref[f]
        win[f, PAD + 40 : PAD + 48, :] = above
        win[f, MID : MID + 8, :] = joined(below, below)
        win[f, MID + 8 : MID + 16, :] = joined(initial, initial)
        win[f, MID + 16 : MID + 24, :] = joined(second, above)
        win[f, MID + 24 : MID + 32, :] = above
    share_levels(win, out_ref, lev, (0,), range(7))


def share_strips(strips, lev_strips, held):
    p = lane(32)
    k = p & 15
    up = (p - k) + jnp.where(k < 8, 4 + (k >> 1), 8 + ((k - 8) >> 1))
    down = (p - k) + ((2 * k - 8) & 15)
    held[8:56, :] = strips
    held[56:80, :] = strips[0:24]
    held[80:88, :] = strips[40:48]
    held[88:104, :] = strips[0:16]
    held[104:112, :] = strips[40:48]

    def halved(first, count):
        initial = held[pl.ds(first - 8, count, stride=2), :]
        mean = 0.5 * (initial + held[pl.ds(first - 7, count, stride=2), :])
        f = lane(count) >> 4
        value = jnp.where(f == 6, initial, mean)
        even, odd = (gather_lanes(value, down[0:count] + k) for k in range(2))
        return jnp.where(f == 5, even, 0.5 * (even + odd))

    levels = [lev_strips[first : first + count, :] for first, count in ((0, 48), (48, 32), (80, 24))]
    up_one = doubled(gather_lanes(held[92:108, :], up[0:16]))
    up_two = doubled(gather_lanes(held[60:84, :], up[0:24]))
    down_to_one, down_to_none = halved(8, 32), halved(56, 24)
    fine = jnp.where(levels[0] == 2, held[8:56, :], up_two)
    medium = jnp.where(levels[1] == 2, down_to_one, held[56:88, :])
    medium = jnp.where(levels[1] == 0, up_one, medium)
    coarse = jnp.where(levels[2] >= 1, down_to_none, held[88:112, :])
    return fine, medium, coarse


def main_kernel(
    lev,
    lev_strips,
    corner,
    fields_ref,
    own_ref,
    last_ref,
    far_ref,
    near_ref,
    out_ref,
    win,
    base,
    prim,
    lefty,
    fluxy,
    gx,
    diffx,
    edge,
    fixed,
    turned,
    leftx,
    fluxx,
    held,
    result,
    sems,
):
    p32, p8 = lane(32), lane(8)
    is_coarse = (p8 >= 72) & (p8 < 120)
    own_level = lev[8:16, :]

    p48 = lane(48)
    sub, count = lax.axis_index("sub"), lax.axis_size("sub")
    even = jnp.full((48, COLS), lax.rem(sub, 2)) == 0
    near = jnp.where(jnp.full((48, COLS), sub) >= count - 2, last_ref[...], near_ref[...])
    strips = jnp.where(((p48 & 15) < 8) == even, far_ref[...], near)
    fine, medium, coarse = share_strips(strips, lev_strips, held)
    strip_one = ((p32 >= 64) & (p32 < 72)) | (p32 >= 120)
    strip_none = ((p32 >= 72) & (p32 < 80)) | ((p32 >= 112) & (p32 < 120))
    right_side = ((p32 >= 64) & (p32 < 72)) | ((p32 >= 112) & (p32 < 120))
    strip_index = (p32 & 7) + jnp.where(right_side, 8, 0)
    for f in range(7):
        index = strip_index + 16 * f
        base[f, PAD : PAD + 48, :] = own_ref[f, PAD : PAD + 48, :]
        base[f, SIDE : SIDE + 48, :] = pltpu.roll(fine, (120 - 16 * f) % 128, 1)
        value = jnp.where(strip_one, gather_lanes(medium, index), own_ref[f, MID : MID + 32, :])
        base[f, MID + 24 : MID + 32, :] = value[24:32]
        base[f, MID : MID + 24, :] = jnp.where(
            strip_none[0:24], gather_lanes(coarse, index[0:24]), value[0:24]
        )

    def swapped(value):
        outside = jnp.where(p8 < 48, pltpu.roll(value, 48, 1), pltpu.roll(value, 80, 1))
        return jnp.where((p8 >= 48) & (p8 < 80), value, outside)

    def turn(slot, value):
        value = value.T
        turned[slot, TPAD : TPAD + 128, :] = value
        turned[slot, TPAD - 8 : TPAD, :] = swapped(value[120:128])
        turned[slot, TPAD + 128 : TPAD + 136, :] = swapped(value[0:8])

    chunks = [PAD + 16 * c for c in range(8)]

    def primitives():
        for row in chunks:
            rows = slice(row, row + 16)
            inverse = 1.0 / base[0, rows, :]
            for i in range(3):
                prim[i, rows, :] = base[1 + i, rows, :] * inverse
            prim[3, rows, :] = 0.5 * (base[6, rows, :] + base[6, row + 1 : row + 17, :])
        for rows in row_sets:
            faces = [base[5, row : row + 8, :] for row in rows]
            for row, face, other in zip(rows, faces, beside_cols(faces, False)):
                prim[4, row : row + 8, :] = 0.5 * (face + other)
        sources = [(base, 0), (prim, 0), (prim, 1), (prim, 2), (prim, 3), (base, 4), (base, 5)]
        for slot, (ref, i) in enumerate(sources):
            turn(slot, ref[i, PAD : PAD + 128, :])

    def sweep(items, lefts, row, count, normal):
        def at(item, step):
            ref, i = item
            return ref[i, row + step : row + step + count, :]

        left, right = [], []
        for i, item in enumerate(items):
            value = at(item, 0)
            slope = 0.5 * minmod(value - at(item, -1), at(item, 1) - value)
            lefts[i, row : row + count, :] = value + slope
            if normal is not None:
                left.append(lefts[i, row - 1 : row - 1 + count, :])
                right.append(value - slope)
        if normal is None:
            return None
        return riemann(left, right, at(normal, 0))

    def sweep_x():
        items = [(turned, i) for i in range(6)]
        sweep(items, leftx, TPAD - 8, 8, None)
        for row in [TPAD + 16 * c for c in range(9)]:
            count = 8 if row == TPAD + 128 else 16
            flux = sweep(items, leftx, row, count, (turned, 6))
            for i, value in enumerate(flux):
                fluxx[i, row : row + count, :] = value
        gx[PAD : PAD + 128, :] = fluxx[4, TPAD : TPAD + 128, :].T
        for i, n in enumerate((0, 1, 2, 3, 5)):
            value = fluxx[n, TPAD + 1 : TPAD + 129, :] - fluxx[n, TPAD : TPAD + 128, :]
            diffx[i, PAD : PAD + 128, :] = value.T

    def sweep_y(last):
        items = [(base, 0), (prim, 1), (prim, 0), (prim, 2), (prim, 4), (base, 4)]
        for row in chunks:
            flux = sweep(items, lefty, row, 16, (base, 6))
            for i, n in enumerate((0, 2, 1, 3, 5, 4)):
                if i == 5 or row < SIDE or not last:
                    fluxy[i, row : row + 16, :] = flux[n]

    def beside_cols(parts, back):
        parts = [pltpu.roll(part, 1 if back else 127, 1) for part in parts]
        edge_lane = p8 == (0 if back else 127)
        return [
            jnp.where(edge_lane, parts[1], parts[0]),
            jnp.where(edge_lane, parts[0], parts[1]),
        ] + parts[2:]

    row_sets = [
        (PAD + 8 * c, SIDE + 8 * c) + ((MID + 8 * c,) if c < 4 else ()) for c in range(6)
    ]

    def edges():
        for rows in row_sets:
            shifted = beside_cols([fluxy[5, row : row + 8, :] for row in rows], True)
            for row, other in zip(rows, shifted):
                value = (fluxy[5, row : row + 8, :] + other) - (
                    gx[row : row + 8, :] + gx[row - 1 : row + 7, :]
                )
                edge[row : row + 8, :] = 0.125 * value

    def correct():
        value = edge[MID : MID + 32, :]
        values = (value, pltpu.roll(value, 127, 1))
        for step in range(2):
            finest = corner[step]
            coarse = (p32 + step >= 72) & (p32 + step < 120)
            halved_two = down_two(edge, (PAD, SIDE), False, False, step)
            halved_one = down_one(edge, MID, False, False, step)
            value = jnp.where((finest == 2) & ~coarse, halved_two, values[step])
            fixed[step, 0:32, :] = jnp.where((finest >= 1) & coarse, halved_one, value)

    def is_own(row):
        return PAD + 8 <= row < PAD + 40 or MID + 8 <= row < MID + 24

    def update_cells(i, last):
        for rows in row_sets:
            for k, row in enumerate(rows):
                if last and not is_own(row):
                    continue
                part = slice(row, row + 8)
                change = diffx[i, part, :] + (fluxy[i, row + 1 : row + 9, :] - fluxy[i, part, :])
                win[i, part, :] = base[i, part, :] - 0.5 * ratios[k] * change

    def update_faces(last):
        for rows in row_sets:
            values = [edge[row : row + 8, :] for row in rows[:2]]
            above = [edge[row + 1 : row + 9, :] for row in rows[:2]]
            others = beside_cols(values, False)
            for row in rows[2:]:
                first = row - MID
                values.append(fixed[0, first : first + 8, :])
                above.append(fixed[0, first + 1 : first + 9, :])
                others.append(fixed[1, first : first + 8, :])
            for row, ratio, value, up, other in zip(rows, ratios, values, above, others):
                if last and not is_own(row):
                    continue
                part = slice(row, row + 8)
                win[5, part, :] = base[5, part, :] - ratio * (up - value)
                win[6, part, :] = base[6, part, :] + ratio * (other - value)

    ratios = (STEP_SIZE, STEP_SIZE, jnp.where(is_coarse, STEP_SIZE / 4, STEP_SIZE / 2))

    def shared(fields):
        share_levels(win, base, lev, (0, 80), fields)

    def finish(fields):
        zero = jnp.zeros((8, COLS), F32)
        for f in fields:
            for c in range(4):
                value = win[f, PAD + 8 + 8 * c : PAD + 16 + 8 * c, :]
                if c < 2:
                    medium = win[f, MID + 8 + 8 * c : MID + 16 + 8 * c, :]
                    coarse = pltpu.roll(medium, 48, 1) if c == 0 else zero
                    lower = jnp.where(own_level == 1, medium, coarse)
                    value = jnp.where(own_level == 2, value, lower)
                used = p8 < jnp.where(own_level == 2, 128, jnp.where(own_level == 1, 64, 32))
                used = used & (own_level >= (0, 1, 2, 2)[c])
                blend = 0.5 * (fields_ref[f, 8 * c : 8 * c + 8, :] + value)
                result[f, 8 * c : 8 * c + 8, :] = jnp.where(used, blend, 0.0)
            pltpu.make_async_copy(result.at[f], out_ref.at[f], sems.at[f]).start()

    for section in range(2):
        last = section == 1
        then = (shared, finish)[section]
        primitives()
        sweep_y(last)
        sweep_x()
        edges()
        correct()
        update_cells(0, last)
        then((0,))
        update_faces(last)
        update_cells(1, last)
        then((1,))
        then((5, 6))
        for i in range(2, 5):
            update_cells(i, last)
            then((i,))
    for f in range(7):
        pltpu.make_async_copy(result.at[f], out_ref.at[f], sems.at[f]).wait()


def swapped_pairs(value, axis, first, stop):
    size = lax.axis_size(axis)
    pairs = [(i, (i + 1) % size) for i in range(first, stop, 2)]
    return lax.ppermute(value, axis, pairs + [(j, i) for i, j in pairs])


def on_device(fields, region_levels):
    shape = jax.ShapeDtypeStruct
    params = pltpu.CompilerParams(vmem_limit_bytes=32 * 1024 * 1024)
    rows = shape((7, 8, COLS), F32)
    lev, lev_strips, corner, cols, to_far, to_close = pl.pallas_call(
        own_kernel,
        out_shape=(
            shape((128, COLS), jnp.int32),
            shape((104, COLS), jnp.int32),
            shape((2, 32, COLS), jnp.int32),
            shape((32, COLS), F32),
            rows,
            rows,
        ),
        in_specs=[HBM] * 2,
        out_specs=(VMEM,) * 6,
        scratch_shapes=[
            pltpu.VMEM(region_levels.shape[::-1], jnp.int32),
            pltpu.VMEM(fields.shape, F32),
            pltpu.VMEM((24, COLS), jnp.int32),
            pltpu.SemaphoreType.DMA((2,)),
        ],
        compiler_params=params,
    )(*(pltpu.with_memory_space_constraint(x, pltpu.HBM) for x in (region_levels.T, fields)))
    size = lax.axis_size("seg")
    close = swapped_pairs(to_close, "seg", 2, size)
    far = swapped_pairs(to_far, "seg", 1, size)
    first = swapped_pairs(to_close, "seg", 0, 2)
    packed, below, above = pl.pallas_call(
        cols_kernel,
        out_shape=(shape((48, COLS), F32), rows, rows),
        in_specs=[VMEM] * 5,
        out_specs=(VMEM,) * 3,
        compiler_params=params,
    )(lev, cols, close, far, first)
    count = lax.axis_size("sub")
    end = swapped_pairs(packed, "sub", count - 2, count)
    far = swapped_pairs(packed, "sub", 1, count)
    near = swapped_pairs(packed, "sub", 0, count - 2)
    own = pl.pallas_call(
        rows_kernel,
        out_shape=shape((7, PAD + 136, COLS), F32),
        in_specs=[VMEM] * 4,
        out_specs=VMEM,
        scratch_shapes=[pltpu.VMEM((7, PAD + 136, COLS), F32)],
        compiler_params=params,
    )(lev, fields, below, above)

    def window(*lead):
        return pltpu.VMEM((*lead, PAD + 136, COLS), F32)

    def across(*lead):
        return pltpu.VMEM((*lead, TPAD + 144, COLS), F32)

    return pl.pallas_call(
        main_kernel,
        out_shape=shape(fields.shape, F32),
        in_specs=[VMEM] * 8,
        out_specs=HBM,
        scratch_shapes=[
            window(7),
            window(7),
            window(5),
            window(6),
            window(6),
            window(),
            window(5),
            window(),
            pltpu.VMEM((2, 40, COLS), F32),
            across(7),
            across(6),
            across(6),
            pltpu.VMEM((112, COLS), F32),
            pltpu.VMEM(fields.shape, F32),
            pltpu.SemaphoreType.DMA((7,)),
        ],
        compiler_params=params,
    )(lev, lev_strips, corner, fields, own, end, far, near)


def solution(mesh):
    placed = (P(None, "seg", "sub"), P())
    return jax.shard_map(
        on_device, mesh=mesh, in_specs=placed, out_specs=P(None, "seg", "sub"), check_vma=False
    )
```

```python
from functools import partial

import jax
import jax.numpy as jnp
from jax import lax
from jax.experimental import pallas as pl
from jax.experimental.pallas import tpu as pltpu
from jax.sharding import PartitionSpec as P

STEP_SIZE = 0.08
ROWS, COLS = 32, 128
F32 = jnp.float32
VMEM = pl.BlockSpec(memory_space=pltpu.VMEM)
HBM = pl.BlockSpec(memory_space=pltpu.HBM)

PAD = 8
TPAD = 16
MID, SIDE = PAD + 48, PAD + 80


def lane(rows):
    return lax.broadcasted_iota(jnp.int32, (rows, COLS), 1)


def gather_lanes(value, index):
    return jnp.take_along_axis(value, index, axis=1, mode="promise_in_bounds")


def near_rows(levels_ref, held_ref):
    sub_count, seg_count = levels_ref.shape
    for j in range(3):
        u = lax.rem(lax.axis_index("sub") + (j - 1 + sub_count), sub_count)
        held_ref[8 * j : 8 * j + 1, 0:seg_count] = levels_ref[pl.ds(u, 1), :]
    table = []
    for i in range(3):
        s = lax.rem(lax.axis_index("seg") + (i - 1 + seg_count), seg_count)
        s = jnp.full((8, COLS), s, jnp.int32)
        rows = [jnp.broadcast_to(held_ref[8 * j : 8 * j + 1, :], (8, COLS)) for j in range(3)]
        table.append([gather_lanes(row, s) for row in rows])

    def level_of(i, offset):
        first, middle, last = table[i]
        return jnp.where(offset < 0, first, jnp.where(offset > 0, last, middle))

    return level_of


def last_rows(ref, f, level):
    return jnp.where(
        level == 2, ref[f, 24:32, :], jnp.where(level == 1, ref[f, 8:16, :], ref[f, 0:8, :])
    )


def packed_cols(read, level):
    p = lane(8)
    first = jnp.where(level == 2, 120, jnp.where(level == 1, 56, 24))
    index = (p & 7) + jnp.where((p & 15) < 8, first, 0)
    packed = gather_lanes(read(0), index)
    for f in range(1, 7):
        packed = jnp.where((p >> 4) == f, gather_lanes(read(f), index), packed)
    return packed


def own_kernel(levels_hbm, fields_hbm, lev, lev_strips, corner, cols_ref, levels_ref, fields_ref, held, sems):
    copies = [
        pltpu.make_async_copy(levels_hbm, levels_ref, sems.at[0]),
        pltpu.make_async_copy(fields_hbm, fields_ref, sems.at[1]),
    ]
    for copy in copies:
        copy.start()
    copies[0].wait()
    level_of = near_rows(levels_ref, held)
    p8 = lane(8)
    inner = (p8 < 64) | ((p8 >= 80) & (p8 < 112))
    outer = ((p8 >= 64) & (p8 < 72)) | ((p8 >= 112) & (p8 < 120))
    middle = jnp.zeros((8, COLS), jnp.int32)
    offsets = (middle, jnp.where(inner, 0, jnp.where(outer, 1, -1)), jnp.where(p8 < 64, 1, -1))
    is_coarse = (p8 >= 72) & (p8 < 120)
    for kind, first in enumerate((0, 48, 80)):
        below_row, centre_row, above_row = (level_of(i, offsets[kind]) for i in range(3))
        lev[first : first + 8, :] = below_row
        lev[first + 8 : first + 16, :] = centre_row
        if kind == 1:
            lev[first + 16 : first + 24, :] = jnp.where(is_coarse, above_row, centre_row)
            lev[first + 24 : first + 32, :] = above_row
        else:
            for r in (16, 24, 32):
                lev[first + r : first + r + 8, :] = centre_row
            lev[first + 40 : first + 48, :] = above_row
    offset = jnp.where((p8 & 15) < 8, -1, 1)
    below_row, centre_row, above_row = (level_of(i, offset) for i in range(3))
    for first, count in ((0, 6), (48, 4), (80, 3)):
        for r in range(count):
            row = below_row if r == 0 else above_row if r == count - 1 else centre_row
            lev_strips[first + 8 * r : first + 8 * r + 8, :] = row
    beside = lev[48:80, :]
    beside = jnp.maximum(beside, pltpu.roll(beside, 1, 1))
    corner[0] = jnp.maximum(beside, pltpu.roll(beside, 1, 0))
    corner[1] = pltpu.roll(corner[0], 127, 1)
    own = lev[8:16, :]
    copies[1].wait()
    for r in range(0, 32, 8):
        cols_ref[r : r + 8, :] = packed_cols(lambda f: fields_ref[f, r : r + 8, :], own)


def cols_kernel(lev, cols_ref, close_ref, far_ref, first_ref, out_ref, below_ref, above_ref):
    seg = lax.axis_index("seg")
    even = jnp.full((8, COLS), lax.rem(seg, 2)) == 0
    early = jnp.full((8, COLS), seg) < 2
    below_level, above_level = lev[0:8, :], lev[40:48, :]
    for f in range(7):
        far, close, first = (last_rows(r, f, below_level) for r in (far_ref, close_ref, first_ref))
        below_ref[f] = jnp.where(even, far, jnp.where(early, first, close))
        close = jnp.where(early, first_ref[f, 0:8, :], close_ref[f, 0:8, :])
        above_ref[f] = jnp.where(even, close, far_ref[f, 0:8, :])
    out_ref[0:8, :] = packed_cols(lambda f: below_ref[f], below_level)
    out_ref[8:40, :] = cols_ref[...]
    out_ref[40:48, :] = packed_cols(lambda f: above_ref[f], above_level)


def minmod(a, b):
    return jnp.minimum(jnp.maximum(b, jnp.minimum(a, 0.0)), jnp.maximum(a, 0.0))


def riemann(left, right, normal):
    rho_l, vn_l, vt_l, vz_l, bt_l, bz_l = left
    rho_r, vn_r, vt_r, vz_r, bt_r, bz_r = right
    normal_square = normal * normal

    def signal(density, speed, square):
        total = density + (square + normal_square)
        return jnp.abs(speed) + jnp.abs(total) * lax.rsqrt(density * total)

    square_l = bt_l * bt_l + bz_l * bz_l
    square_r = bt_r * bt_r + bz_r * bz_r
    fastest = jnp.maximum(signal(rho_l, vn_l, square_l), signal(rho_r, vn_r, square_r))
    ahead, back = vn_l + fastest, vn_r - fastest
    mass_l, mass_r = rho_l * ahead, rho_r * back
    pressure = (rho_l + rho_r) + 0.5 * (square_l + square_r)
    return [
        mass_l + mass_r,
        (mass_l * vn_l + mass_r * vn_r) + (pressure - normal_square),
        (mass_l * vt_l + mass_r * vt_r) - normal * (bt_l + bt_r),
        (mass_l * vz_l + mass_r * vz_r) - normal * (bz_l + bz_r),
        (bt_l * ahead + bt_r * back) - normal * (vt_l + vt_r),
        (bz_l * ahead + bz_r * back) - normal * (vz_l + vz_r),
    ]


def doubled(part):
    low = lax.broadcasted_iota(jnp.int32, (8, COLS), 0) >> 1
    rows = []
    for r in range(0, part.shape[0], 8):
        for index in (low, low + 4):
            rows.append(
                jnp.take_along_axis(part[r : r + 8], index, axis=0, mode="promise_in_bounds")
            )
    return jnp.concatenate(rows, axis=0)


def rows_halved(ref, first, by_rows):
    initial = ref[pl.ds(first - 8, 32, stride=2), :]
    if not by_rows:
        return initial
    return 0.5 * (initial + ref[pl.ds(first - 7, 32, stride=2), :])


def paired_lanes(value, index, by_cols):
    initial = gather_lanes(value, index)
    return 0.5 * (initial + gather_lanes(value, index + 1)) if by_cols else initial


def down_two(ref, firsts, by_rows, by_cols, step=0):
    p = lane(32) + step
    index = (2 * p) & 127
    parts = [paired_lanes(rows_halved(ref, first, by_rows), index, by_cols) for first in firsts]
    return parts[0] if len(parts) == 1 else jnp.where((p & 127) < 64, parts[0], parts[1])


def down_one(ref, first, by_rows, by_cols, step=0):
    return paired_lanes(
        rows_halved(ref, first, by_rows), (2 * (lane(32) + step - 80)) & 127, by_cols
    )


def share_levels(win, out, lev, blocks, fields):
    p32, p24, p16 = lane(32), lane(24), lane(16)
    coarse32 = (p32 >= 72) & (p32 < 120)
    level_b = lev[48:80, :]
    up_one = jnp.where(p16 < 72, 80 + (p16 >> 1), jnp.where(p16 >= 120, 16 + (p16 >> 1), p16))
    up_two = (p24 >> 1, 64 + (p24 >> 1))
    for f in fields:
        by_rows, by_cols = f != 6, f != 5
        value = win[f, MID : MID + 32, :]
        up = doubled(gather_lanes(win[f, MID + 4 : MID + 20, :], up_one))
        part = win[f, MID + 4 : MID + 28, :]
        ups = [doubled(gather_lanes(part, up_two[k])) for k in range(len(blocks))]
        down = down_two(win.at[f], [PAD + first for first in blocks], by_rows, by_cols)
        last = down_one(win.at[f], MID, by_rows, by_cols)
        medium = jnp.where(level_b == 0, up, jnp.where(level_b == 2, down, value))
        coarse = jnp.where(level_b >= 1, last, value)
        for first, injected in zip(blocks, ups):
            rows = slice(PAD + first, PAD + first + 48)
            out[f, rows, :] = jnp.where(lev[first : first + 48, :] == 2, win[f, rows, :], injected)
        out[f, MID : MID + 32, :] = jnp.where(coarse32, coarse, medium)


def rows_kernel(lev, fields_ref, below_ref, above_ref, out_ref, win):
    p8 = lane(8)
    is_coarse = (p8 >= 72) & (p8 < 120)

    def joined(fine, coarse):
        return jnp.where(is_coarse, pltpu.roll(coarse, 80, 1), fine)

    for f in range(7):
        below, above = below_ref[f], above_ref[f]
        initial, second = fields_ref[f, 0:8, :], fields_ref[f, 8:16, :]
        win[f, PAD : PAD + 8, :] = below
        win[f, PAD + 8 : PAD + 40, :] = fields_ref[f]
        win[f, PAD + 40 : PAD + 48, :] = above
        win[f, MID : MID + 8, :] = joined(below, below)
        win[f, MID + 8 : MID + 16, :] = joined(initial, initial)
        win[f, MID + 16 : MID + 24, :] = joined(second, above)
        win[f, MID + 24 : MID + 32, :] = above
    share_levels(win, out_ref, lev, (0,), range(7))


def share_strips(strips, lev_strips, held):
    p = lane(32)
    k = p & 15
    up = (p - k) + jnp.where(k < 8, 4 + (k >> 1), 8 + ((k - 8) >> 1))
    down = (p - k) + ((2 * k - 8) & 15)
    held[8:56, :] = strips
    held[56:80, :] = strips[0:24]
    held[80:88, :] = strips[40:48]
    held[88:104, :] = strips[0:16]
    held[104:112, :] = strips[40:48]

    def halved(first, count):
        initial = held[pl.ds(first - 8, count, stride=2), :]
        mean = 0.5 * (initial + held[pl.ds(first - 7, count, stride=2), :])
        f = lane(count) >> 4
        value = jnp.where(f == 6, initial, mean)
        even, odd = (gather_lanes(value, down[0:count] + k) for k in range(2))
        return jnp.where(f == 5, even, 0.5 * (even + odd))

    levels = [lev_strips[first : first + count, :] for first, count in ((0, 48), (48, 32), (80, 24))]
    up_one = doubled(gather_lanes(held[92:108, :], up[0:16]))
    up_two = doubled(gather_lanes(held[60:84, :], up[0:24]))
    down_to_one, down_to_none = halved(8, 32), halved(56, 24)
    fine = jnp.where(levels[0] == 2, held[8:56, :], up_two)
    medium = jnp.where(levels[1] == 2, down_to_one, held[56:88, :])
    medium = jnp.where(levels[1] == 0, up_one, medium)
    coarse = jnp.where(levels[2] >= 1, down_to_none, held[88:112, :])
    return fine, medium, coarse


def main_kernel(
    lev,
    lev_strips,
    corner,
    fields_ref,
    own_ref,
    last_ref,
    far_ref,
    near_ref,
    out_ref,
    win,
    base,
    prim,
    lefty,
    fluxy,
    gx,
    diffx,
    edge,
    fixed,
    turned,
    leftx,
    fluxx,
    held,
    result,
    sems,
):
    p32, p8 = lane(32), lane(8)
    is_coarse = (p8 >= 72) & (p8 < 120)
    own_level = lev[8:16, :]

    p48 = lane(48)
    sub, count = lax.axis_index("sub"), lax.axis_size("sub")
    first_row = lax.axis_index("seg") == 0
    sub = jnp.full((48, COLS), sub)
    even = jnp.where(first_row, 1 - (sub & 1), sub & 1) == 0
    third = jnp.where(first_row, jnp.where(sub == 0, count - 1, sub), sub + 1) >= count - 1
    near = jnp.where(third, last_ref[...], near_ref[...])
    strips = jnp.where(((p48 & 15) < 8) == even, far_ref[...], near)
    fine, medium, coarse = share_strips(strips, lev_strips, held)
    strip_one = ((p32 >= 64) & (p32 < 72)) | (p32 >= 120)
    strip_none = ((p32 >= 72) & (p32 < 80)) | ((p32 >= 112) & (p32 < 120))
    right_side = ((p32 >= 64) & (p32 < 72)) | ((p32 >= 112) & (p32 < 120))
    strip_index = (p32 & 7) + jnp.where(right_side, 8, 0)
    for f in range(7):
        index = strip_index + 16 * f
        base[f, PAD : PAD + 48, :] = own_ref[f, PAD : PAD + 48, :]
        base[f, SIDE : SIDE + 48, :] = pltpu.roll(fine, (120 - 16 * f) % 128, 1)
        value = jnp.where(strip_one, gather_lanes(medium, index), own_ref[f, MID : MID + 32, :])
        base[f, MID + 24 : MID + 32, :] = value[24:32]
        base[f, MID : MID + 24, :] = jnp.where(
            strip_none[0:24], gather_lanes(coarse, index[0:24]), value[0:24]
        )

    def swapped(value):
        outside = jnp.where(p8 < 48, pltpu.roll(value, 48, 1), pltpu.roll(value, 80, 1))
        return jnp.where((p8 >= 48) & (p8 < 80), value, outside)

    def turn(slot, value):
        value = value.T
        turned[slot, TPAD : TPAD + 128, :] = value
        turned[slot, TPAD - 8 : TPAD, :] = swapped(value[120:128])
        turned[slot, TPAD + 128 : TPAD + 136, :] = swapped(value[0:8])

    chunks = [PAD + 16 * c for c in range(8)]

    def primitives():
        for row in chunks:
            rows = slice(row, row + 16)
            inverse = 1.0 / base[0, rows, :]
            for i in range(3):
                prim[i, rows, :] = base[1 + i, rows, :] * inverse
            prim[3, rows, :] = 0.5 * (base[6, rows, :] + base[6, row + 1 : row + 17, :])
        for rows in row_sets:
            faces = [base[5, row : row + 8, :] for row in rows]
            for row, face, other in zip(rows, faces, beside_cols(faces, False)):
                prim[4, row : row + 8, :] = 0.5 * (face + other)
        sources = [(base, 0), (prim, 0), (prim, 1), (prim, 2), (prim, 3), (base, 4), (base, 5)]
        for slot, (ref, i) in enumerate(sources):
            turn(slot, ref[i, PAD : PAD + 128, :])

    def sweep(items, lefts, row, count, normal):
        def at(item, step):
            ref, i = item
            return ref[i, row + step : row + step + count, :]

        left, right = [], []
        for i, item in enumerate(items):
            value = at(item, 0)
            slope = 0.5 * minmod(value - at(item, -1), at(item, 1) - value)
            lefts[i, row : row + count, :] = value + slope
            if normal is not None:
                left.append(lefts[i, row - 1 : row - 1 + count, :])
                right.append(value - slope)
        if normal is None:
            return None
        return riemann(left, right, at(normal, 0))

    def sweep_x():
        items = [(turned, i) for i in range(6)]
        sweep(items, leftx, TPAD - 8, 8, None)
        for row in [TPAD + 16 * c for c in range(9)]:
            count = 8 if row == TPAD + 128 else 16
            flux = sweep(items, leftx, row, count, (turned, 6))
            for i, value in enumerate(flux):
                fluxx[i, row : row + count, :] = value
        gx[PAD : PAD + 128, :] = fluxx[4, TPAD : TPAD + 128, :].T
        for i, n in enumerate((0, 1, 2, 3, 5)):
            value = fluxx[n, TPAD + 1 : TPAD + 129, :] - fluxx[n, TPAD : TPAD + 128, :]
            diffx[i, PAD : PAD + 128, :] = value.T

    def sweep_y(last):
        items = [(base, 0), (prim, 1), (prim, 0), (prim, 2), (prim, 4), (base, 4)]
        for row in chunks:
            flux = sweep(items, lefty, row, 16, (base, 6))
            for i, n in enumerate((0, 2, 1, 3, 5, 4)):
                if i == 5 or row < SIDE or not last:
                    fluxy[i, row : row + 16, :] = flux[n]

    def beside_cols(parts, back):
        parts = [pltpu.roll(part, 1 if back else 127, 1) for part in parts]
        edge_lane = p8 == (0 if back else 127)
        return [
            jnp.where(edge_lane, parts[1], parts[0]),
            jnp.where(edge_lane, parts[0], parts[1]),
        ] + parts[2:]

    row_sets = [
        (PAD + 8 * c, SIDE + 8 * c) + ((MID + 8 * c,) if c < 4 else ()) for c in range(6)
    ]

    def edges():
        for rows in row_sets:
            shifted = beside_cols([fluxy[5, row : row + 8, :] for row in rows], True)
            for row, other in zip(rows, shifted):
                value = (fluxy[5, row : row + 8, :] + other) - (
                    gx[row : row + 8, :] + gx[row - 1 : row + 7, :]
                )
                edge[row : row + 8, :] = 0.125 * value

    def correct():
        value = edge[MID : MID + 32, :]
        values = (value, pltpu.roll(value, 127, 1))
        for step in range(2):
            finest = corner[step]
            coarse = (p32 + step >= 72) & (p32 + step < 120)
            halved_two = down_two(edge, (PAD, SIDE), False, False, step)
            halved_one = down_one(edge, MID, False, False, step)
            value = jnp.where((finest == 2) & ~coarse, halved_two, values[step])
            fixed[step, 0:32, :] = jnp.where((finest >= 1) & coarse, halved_one, value)

    def is_own(row):
        return PAD + 8 <= row < PAD + 40 or MID + 8 <= row < MID + 24

    def update_cells(i, last):
        for rows in row_sets:
            for k, row in enumerate(rows):
                if last and not is_own(row):
                    continue
                part = slice(row, row + 8)
                change = diffx[i, part, :] + (fluxy[i, row + 1 : row + 9, :] - fluxy[i, part, :])
                win[i, part, :] = base[i, part, :] - 0.5 * ratios[k] * change

    def update_faces(last):
        for rows in row_sets:
            values = [edge[row : row + 8, :] for row in rows[:2]]
            above = [edge[row + 1 : row + 9, :] for row in rows[:2]]
            others = beside_cols(values, False)
            for row in rows[2:]:
                first = row - MID
                values.append(fixed[0, first : first + 8, :])
                above.append(fixed[0, first + 1 : first + 9, :])
                others.append(fixed[1, first : first + 8, :])
            for row, ratio, value, up, other in zip(rows, ratios, values, above, others):
                if last and not is_own(row):
                    continue
                part = slice(row, row + 8)
                win[5, part, :] = base[5, part, :] - ratio * (up - value)
                win[6, part, :] = base[6, part, :] + ratio * (other - value)

    ratios = (STEP_SIZE, STEP_SIZE, jnp.where(is_coarse, STEP_SIZE / 4, STEP_SIZE / 2))

    def shared(fields):
        share_levels(win, base, lev, (0, 80), fields)

    def finish(fields):
        zero = jnp.zeros((8, COLS), F32)
        for f in fields:
            for c in range(4):
                value = win[f, PAD + 8 + 8 * c : PAD + 16 + 8 * c, :]
                if c < 2:
                    medium = win[f, MID + 8 + 8 * c : MID + 16 + 8 * c, :]
                    coarse = pltpu.roll(medium, 48, 1) if c == 0 else zero
                    lower = jnp.where(own_level == 1, medium, coarse)
                    value = jnp.where(own_level == 2, value, lower)
                used = p8 < jnp.where(own_level == 2, 128, jnp.where(own_level == 1, 64, 32))
                used = used & (own_level >= (0, 1, 2, 2)[c])
                blend = 0.5 * (fields_ref[f, 8 * c : 8 * c + 8, :] + value)
                result[f, 8 * c : 8 * c + 8, :] = jnp.where(used, blend, 0.0)
            pltpu.make_async_copy(result.at[f], out_ref.at[f], sems.at[f]).start()

    for section in range(2):
        last = section == 1
        then = (shared, finish)[section]
        primitives()
        sweep_y(last)
        sweep_x()
        edges()
        correct()
        update_cells(0, last)
        then((0,))
        update_faces(last)
        update_cells(1, last)
        then((1,))
        then((5, 6))
        for i in range(2, 5):
            update_cells(i, last)
            then((i,))
    for f in range(7):
        pltpu.make_async_copy(result.at[f], out_ref.at[f], sems.at[f]).wait()


def swapped_pairs(value, axis, first, stop):
    size = lax.axis_size(axis)
    pairs = [(i, (i + 1) % size) for i in range(first, stop, 2)]
    return lax.ppermute(value, axis, pairs + [(j, i) for i, j in pairs])


def swapped_subs(value, turn):
    rows, count = lax.axis_size("seg"), lax.axis_size("sub")
    pairs = []
    for s in range(rows):
        first, stop = ((0, count - 2), (1, count), (count - 2, count))[turn]
        if s == 0:
            first, stop = ((1, count - 1), (0, count), (count - 1, count))[turn]
        for u in range(first, stop, 2):
            a, b = s * count + u, s * count + (u + 1) % count
            pairs += [(a, b), (b, a)]
    return lax.ppermute(value, ("seg", "sub"), pairs)


def on_device(fields, region_levels):
    shape = jax.ShapeDtypeStruct
    params = pltpu.CompilerParams(vmem_limit_bytes=32 * 1024 * 1024)
    size = lax.axis_size("seg")
    close = swapped_pairs(fields, "seg", 2, size)
    far = swapped_pairs(fields, "seg", 1, size)
    first = swapped_pairs(fields, "seg", 0, 2)
    lev, lev_strips, corner, cols = pl.pallas_call(
        own_kernel,
        out_shape=(
            shape((128, COLS), jnp.int32),
            shape((104, COLS), jnp.int32),
            shape((2, 32, COLS), jnp.int32),
            shape((32, COLS), F32),
        ),
        in_specs=[HBM] * 2,
        out_specs=(VMEM,) * 4,
        scratch_shapes=[
            pltpu.VMEM(region_levels.shape[::-1], jnp.int32),
            pltpu.VMEM(fields.shape, F32),
            pltpu.VMEM((24, COLS), jnp.int32),
            pltpu.SemaphoreType.DMA((2,)),
        ],
        compiler_params=params,
    )(*(pltpu.with_memory_space_constraint(x, pltpu.HBM) for x in (region_levels.T, fields)))
    rows = shape((7, 8, COLS), F32)
    packed, below, above = pl.pallas_call(
        cols_kernel,
        out_shape=(shape((48, COLS), F32), rows, rows),
        in_specs=[VMEM] * 5,
        out_specs=(VMEM,) * 3,
        compiler_params=params,
    )(lev, cols, close, far, first)
    end, far, near = (swapped_subs(packed, turn) for turn in (2, 1, 0))
    own = pl.pallas_call(
        rows_kernel,
        out_shape=shape((7, PAD + 136, COLS), F32),
        in_specs=[VMEM] * 4,
        out_specs=VMEM,
        scratch_shapes=[pltpu.VMEM((7, PAD + 136, COLS), F32)],
        compiler_params=params,
    )(lev, fields, below, above)

    def window(*lead):
        return pltpu.VMEM((*lead, PAD + 136, COLS), F32)

    def across(*lead):
        return pltpu.VMEM((*lead, TPAD + 144, COLS), F32)

    return pl.pallas_call(
        main_kernel,
        out_shape=shape(fields.shape, F32),
        in_specs=[VMEM] * 8,
        out_specs=HBM,
        scratch_shapes=[
            window(7),
            window(7),
            window(5),
            window(6),
            window(6),
            window(),
            window(5),
            window(),
            pltpu.VMEM((2, 40, COLS), F32),
            across(7),
            across(6),
            across(6),
            pltpu.VMEM((112, COLS), F32),
            pltpu.VMEM(fields.shape, F32),
            pltpu.SemaphoreType.DMA((7,)),
        ],
        compiler_params=params,
    )(lev, lev_strips, corner, fields, own, end, far, near)


def solution(mesh):
    placed = (P(None, "seg", "sub"), P())
    return jax.shard_map(
        on_device, mesh=mesh, in_specs=placed, out_specs=P(None, "seg", "sub"), check_vma=False
    )
```

```python
from functools import partial

import jax
import jax.numpy as jnp
from jax import lax
from jax.experimental import pallas as pl
from jax.experimental.pallas import tpu as pltpu
from jax.sharding import PartitionSpec as P

STEP_SIZE = 0.08
ROWS, COLS = 32, 128
F32 = jnp.float32
VMEM = pl.BlockSpec(memory_space=pltpu.VMEM)
HBM = pl.BlockSpec(memory_space=pltpu.HBM)

PAD = 8
TPAD = 16
MID, SIDE = PAD + 48, PAD + 80


def lane(rows):
    return lax.broadcasted_iota(jnp.int32, (rows, COLS), 1)


def gather_lanes(value, index):
    return jnp.take_along_axis(value, index, axis=1, mode="promise_in_bounds")


def near_rows(levels_ref, held_ref):
    sub_count, seg_count = levels_ref.shape
    for j in range(3):
        u = lax.rem(lax.axis_index("sub") + (j - 1 + sub_count), sub_count)
        held_ref[8 * j : 8 * j + 1, 0:seg_count] = levels_ref[pl.ds(u, 1), :]
    table = []
    for i in range(3):
        s = lax.rem(lax.axis_index("seg") + (i - 1 + seg_count), seg_count)
        s = jnp.full((8, COLS), s, jnp.int32)
        rows = [jnp.broadcast_to(held_ref[8 * j : 8 * j + 1, :], (8, COLS)) for j in range(3)]
        table.append([gather_lanes(row, s) for row in rows])

    def level_of(i, offset):
        first, middle, last = table[i]
        return jnp.where(offset < 0, first, jnp.where(offset > 0, last, middle))

    return level_of


def last_rows(ref, f, level):
    return jnp.where(
        level == 2, ref[f, 24:32, :], jnp.where(level == 1, ref[f, 8:16, :], ref[f, 0:8, :])
    )


def packed_cols(read, level):
    p = lane(8)
    first = jnp.where(level == 2, 120, jnp.where(level == 1, 56, 24))
    index = (p & 7) + jnp.where((p & 15) < 8, first, 0)
    packed = gather_lanes(read(0), index)
    for f in range(1, 7):
        packed = jnp.where((p >> 4) == f, gather_lanes(read(f), index), packed)
    return packed


def own_kernel(levels_hbm, fields_hbm, lev, lev_strips, corner, cols_ref, levels_ref, fields_ref, held, sems):
    copies = [
        pltpu.make_async_copy(levels_hbm, levels_ref, sems.at[0]),
        pltpu.make_async_copy(fields_hbm, fields_ref, sems.at[1]),
    ]
    for copy in copies:
        copy.start()
    copies[0].wait()
    level_of = near_rows(levels_ref, held)
    p8 = lane(8)
    inner = (p8 < 64) | ((p8 >= 80) & (p8 < 112))
    outer = ((p8 >= 64) & (p8 < 72)) | ((p8 >= 112) & (p8 < 120))
    middle = jnp.zeros((8, COLS), jnp.int32)
    offsets = (middle, jnp.where(inner, 0, jnp.where(outer, 1, -1)), jnp.where(p8 < 64, 1, -1))
    is_coarse = (p8 >= 72) & (p8 < 120)
    for kind, first in enumerate((0, 48, 80)):
        below_row, centre_row, above_row = (level_of(i, offsets[kind]) for i in range(3))
        lev[first : first + 8, :] = below_row
        lev[first + 8 : first + 16, :] = centre_row
        if kind == 1:
            lev[first + 16 : first + 24, :] = jnp.where(is_coarse, above_row, centre_row)
            lev[first + 24 : first + 32, :] = above_row
        else:
            for r in (16, 24, 32):
                lev[first + r : first + r + 8, :] = centre_row
            lev[first + 40 : first + 48, :] = above_row
    offset = jnp.where((p8 & 15) < 8, -1, 1)
    below_row, centre_row, above_row = (level_of(i, offset) for i in range(3))
    for first, count in ((0, 6), (48, 4), (80, 3)):
        for r in range(count):
            row = below_row if r == 0 else above_row if r == count - 1 else centre_row
            lev_strips[first + 8 * r : first + 8 * r + 8, :] = row
    beside = lev[48:80, :]
    beside = jnp.maximum(beside, pltpu.roll(beside, 1, 1))
    corner[0] = jnp.maximum(beside, pltpu.roll(beside, 1, 0))
    corner[1] = pltpu.roll(corner[0], 127, 1)
    own = lev[8:16, :]
    copies[1].wait()
    for r in range(0, 32, 8):
        cols_ref[r : r + 8, :] = packed_cols(lambda f: fields_ref[f, r : r + 8, :], own)


def cols_kernel(lev, cols_ref, close_ref, far_ref, first_ref, out_ref, below_ref, above_ref):
    seg = lax.axis_index("seg")
    even = jnp.full((8, COLS), lax.rem(seg, 2)) == 0
    early = jnp.full((8, COLS), seg) < 2
    below_level, above_level = lev[0:8, :], lev[40:48, :]
    for f in range(7):
        far, close, first = (last_rows(r, f, below_level) for r in (far_ref, close_ref, first_ref))
        below_ref[f] = jnp.where(even, far, jnp.where(early, first, close))
        close = jnp.where(early, first_ref[f, 0:8, :], close_ref[f, 0:8, :])
        above_ref[f] = jnp.where(even, close, far_ref[f, 0:8, :])
    out_ref[0:8, :] = packed_cols(lambda f: below_ref[f], below_level)
    out_ref[8:40, :] = cols_ref[...]
    out_ref[40:48, :] = packed_cols(lambda f: above_ref[f], above_level)


def minmod(a, b):
    return jnp.minimum(jnp.maximum(b, jnp.minimum(a, 0.0)), jnp.maximum(a, 0.0))


def riemann(left, right, normal):
    rho_l, vn_l, vt_l, vz_l, bt_l, bz_l = left
    rho_r, vn_r, vt_r, vz_r, bt_r, bz_r = right
    normal_square = normal * normal

    def signal(density, speed, square):
        total = density + (square + normal_square)
        return jnp.abs(speed) + jnp.abs(total) * lax.rsqrt(density * total)

    square_l = bt_l * bt_l + bz_l * bz_l
    square_r = bt_r * bt_r + bz_r * bz_r
    fastest = jnp.maximum(signal(rho_l, vn_l, square_l), signal(rho_r, vn_r, square_r))
    ahead, back = vn_l + fastest, vn_r - fastest
    mass_l, mass_r = rho_l * ahead, rho_r * back
    pressure = (rho_l + rho_r) + 0.5 * (square_l + square_r)
    return [
        mass_l + mass_r,
        (mass_l * vn_l + mass_r * vn_r) + (pressure - normal_square),
        (mass_l * vt_l + mass_r * vt_r) - normal * (bt_l + bt_r),
        (mass_l * vz_l + mass_r * vz_r) - normal * (bz_l + bz_r),
        (bt_l * ahead + bt_r * back) - normal * (vt_l + vt_r),
        (bz_l * ahead + bz_r * back) - normal * (vz_l + vz_r),
    ]


def doubled(part):
    low = lax.broadcasted_iota(jnp.int32, (8, COLS), 0) >> 1
    rows = []
    for r in range(0, part.shape[0], 8):
        for index in (low, low + 4):
            rows.append(
                jnp.take_along_axis(part[r : r + 8], index, axis=0, mode="promise_in_bounds")
            )
    return jnp.concatenate(rows, axis=0)


def rows_halved(ref, first, by_rows):
    initial = ref[pl.ds(first - 8, 32, stride=2), :]
    if not by_rows:
        return initial
    return 0.5 * (initial + ref[pl.ds(first - 7, 32, stride=2), :])


def paired_lanes(value, index, by_cols):
    initial = gather_lanes(value, index)
    return 0.5 * (initial + gather_lanes(value, index + 1)) if by_cols else initial


def down_two(ref, firsts, by_rows, by_cols, step=0):
    p = lane(32) + step
    index = (2 * p) & 127
    parts = [rows_halved(ref, first, by_rows) for first in firsts]
    if len(parts) == 1:
        return paired_lanes(parts[0], index, by_cols)
    inside = (p & 127) < 64
    picks = []
    for k in range(2 if by_cols else 1):
        picks.append(jnp.where(inside, gather_lanes(parts[0], index + k), gather_lanes(parts[1], index + k)))
    return 0.5 * (picks[0] + picks[1]) if by_cols else picks[0]


def down_one(ref, first, by_rows, by_cols, step=0):
    return paired_lanes(
        rows_halved(ref, first, by_rows), (2 * (lane(32) + step - 80)) & 127, by_cols
    )


def share_levels(win, out, lev, blocks, fields):
    p32, p24, p16 = lane(32), lane(24), lane(16)
    coarse32 = (p32 >= 72) & (p32 < 120)
    level_b = lev[48:80, :]
    up_one = jnp.where(p16 < 72, 80 + (p16 >> 1), jnp.where(p16 >= 120, 16 + (p16 >> 1), p16))
    up_two = (p24 >> 1, 64 + (p24 >> 1))
    for f in fields:
        by_rows, by_cols = f != 6, f != 5
        value = win[f, MID : MID + 32, :]
        up = doubled(gather_lanes(win[f, MID + 4 : MID + 20, :], up_one))
        part = win[f, MID + 4 : MID + 28, :]
        ups = [doubled(gather_lanes(part, up_two[k])) for k in range(len(blocks))]
        down = down_two(win.at[f], [PAD + first for first in blocks], by_rows, by_cols)
        last = down_one(win.at[f], MID, by_rows, by_cols)
        medium = jnp.where(level_b == 0, up, jnp.where(level_b == 2, down, value))
        coarse = jnp.where(level_b >= 1, last, value)
        for first, injected in zip(blocks, ups):
            rows = slice(PAD + first, PAD + first + 48)
            out[f, rows, :] = jnp.where(lev[first : first + 48, :] == 2, win[f, rows, :], injected)
        out[f, MID : MID + 32, :] = jnp.where(coarse32, coarse, medium)


def rows_kernel(lev, fields_ref, below_ref, above_ref, out_ref, win):
    p8 = lane(8)
    is_coarse = (p8 >= 72) & (p8 < 120)

    def joined(fine, coarse):
        return jnp.where(is_coarse, pltpu.roll(coarse, 80, 1), fine)

    for f in range(7):
        below, above = below_ref[f], above_ref[f]
        initial, second = fields_ref[f, 0:8, :], fields_ref[f, 8:16, :]
        win[f, PAD : PAD + 8, :] = below
        win[f, PAD + 8 : PAD + 40, :] = fields_ref[f]
        win[f, PAD + 40 : PAD + 48, :] = above
        win[f, MID : MID + 8, :] = joined(below, below)
        win[f, MID + 8 : MID + 16, :] = joined(initial, initial)
        win[f, MID + 16 : MID + 24, :] = joined(second, above)
        win[f, MID + 24 : MID + 32, :] = above
    share_levels(win, out_ref, lev, (0,), range(7))


def share_strips(strips, lev_strips, held):
    p = lane(32)
    k = p & 15
    up = (p - k) + jnp.where(k < 8, 4 + (k >> 1), 8 + ((k - 8) >> 1))
    down = (p - k) + ((2 * k - 8) & 15)
    held[8:56, :] = strips
    held[56:80, :] = strips[0:24]
    held[80:88, :] = strips[40:48]
    held[88:104, :] = strips[0:16]
    held[104:112, :] = strips[40:48]

    def halved(first, count):
        initial = held[pl.ds(first - 8, count, stride=2), :]
        mean = 0.5 * (initial + held[pl.ds(first - 7, count, stride=2), :])
        f = lane(count) >> 4
        value = jnp.where(f == 6, initial, mean)
        even, odd = (gather_lanes(value, down[0:count] + k) for k in range(2))
        return jnp.where(f == 5, even, 0.5 * (even + odd))

    levels = [lev_strips[first : first + count, :] for first, count in ((0, 48), (48, 32), (80, 24))]
    up_one = doubled(gather_lanes(held[92:108, :], up[0:16]))
    up_two = doubled(gather_lanes(held[60:84, :], up[0:24]))
    down_to_one, down_to_none = halved(8, 32), halved(56, 24)
    fine = jnp.where(levels[0] == 2, held[8:56, :], up_two)
    medium = jnp.where(levels[1] == 2, down_to_one, held[56:88, :])
    medium = jnp.where(levels[1] == 0, up_one, medium)
    coarse = jnp.where(levels[2] >= 1, down_to_none, held[88:112, :])
    return fine, medium, coarse


def main_kernel(
    lev,
    lev_strips,
    corner,
    fields_ref,
    own_ref,
    last_ref,
    far_ref,
    near_ref,
    out_ref,
    win,
    base,
    prim,
    lefty,
    fluxy,
    gx,
    diffx,
    edge,
    fixed,
    turned,
    leftx,
    fluxx,
    held,
    result,
    sems,
):
    p32, p8 = lane(32), lane(8)
    is_coarse = (p8 >= 72) & (p8 < 120)
    own_level = lev[8:16, :]

    p48 = lane(48)
    sub, count = lax.axis_index("sub"), lax.axis_size("sub")
    first_row = lax.axis_index("seg") == 0
    sub = jnp.full((48, COLS), sub)
    even = jnp.where(first_row, 1 - (sub & 1), sub & 1) == 0
    third = jnp.where(first_row, jnp.where(sub == 0, count - 1, sub), sub + 1) >= count - 1
    near = jnp.where(third, last_ref[...], near_ref[...])
    strips = jnp.where(((p48 & 15) < 8) == even, far_ref[...], near)
    fine, medium, coarse = share_strips(strips, lev_strips, held)
    strip_one = ((p32 >= 64) & (p32 < 72)) | (p32 >= 120)
    strip_none = ((p32 >= 72) & (p32 < 80)) | ((p32 >= 112) & (p32 < 120))
    right_side = ((p32 >= 64) & (p32 < 72)) | ((p32 >= 112) & (p32 < 120))
    strip_index = (p32 & 7) + jnp.where(right_side, 8, 0)
    for f in range(7):
        index = strip_index + 16 * f
        base[f, PAD : PAD + 48, :] = own_ref[f, PAD : PAD + 48, :]
        base[f, SIDE : SIDE + 48, :] = pltpu.roll(fine, (120 - 16 * f) % 128, 1)
        value = jnp.where(strip_one, gather_lanes(medium, index), own_ref[f, MID : MID + 32, :])
        base[f, MID + 24 : MID + 32, :] = value[24:32]
        base[f, MID : MID + 24, :] = jnp.where(
            strip_none[0:24], gather_lanes(coarse, index[0:24]), value[0:24]
        )

    def swapped(value):
        return gather_lanes(value, jnp.where(p8 < 48, p8 + 80, jnp.where(p8 < 80, p8, p8 - 80)))

    def turn(slot, value):
        value = value.T
        turned[slot, TPAD : TPAD + 128, :] = value
        turned[slot, TPAD - 8 : TPAD, :] = swapped(value[120:128])
        turned[slot, TPAD + 128 : TPAD + 136, :] = swapped(value[0:8])

    chunks = [PAD + 16 * c for c in range(8)]

    def primitives():
        for row in chunks:
            rows = slice(row, row + 16)
            inverse = 1.0 / base[0, rows, :]
            for i in range(3):
                prim[i, rows, :] = base[1 + i, rows, :] * inverse
            prim[3, rows, :] = 0.5 * (base[6, rows, :] + base[6, row + 1 : row + 17, :])
        for rows in row_sets:
            faces = [base[5, row : row + 8, :] for row in rows]
            for row, face, other in zip(rows, faces, beside_cols(faces, False)):
                prim[4, row : row + 8, :] = 0.5 * (face + other)
        sources = [(base, 0), (prim, 0), (prim, 1), (prim, 2), (prim, 3), (base, 4), (base, 5)]
        for slot, (ref, i) in enumerate(sources):
            turn(slot, ref[i, PAD : PAD + 128, :])

    def sweep(items, lefts, row, count, normal):
        def at(item, step):
            ref, i = item
            return ref[i, row + step : row + step + count, :]

        left, right = [], []
        for i, item in enumerate(items):
            value = at(item, 0)
            slope = 0.5 * minmod(value - at(item, -1), at(item, 1) - value)
            lefts[i, row : row + count, :] = value + slope
            if normal is not None:
                left.append(lefts[i, row - 1 : row - 1 + count, :])
                right.append(value - slope)
        if normal is None:
            return None
        return riemann(left, right, at(normal, 0))

    def sweep_x():
        items = [(turned, i) for i in range(6)]
        sweep(items, leftx, TPAD - 8, 8, None)
        for row in range(TPAD, TPAD + 136, 8):
            count = min(8, TPAD + 136 - row)
            flux = sweep(items, leftx, row, count, (turned, 6))
            for i, value in enumerate(flux):
                fluxx[i, row : row + count, :] = value
        gx[PAD : PAD + 128, :] = fluxx[4, TPAD : TPAD + 128, :].T
        for i, n in enumerate((0, 1, 2, 3, 5)):
            value = fluxx[n, TPAD + 1 : TPAD + 129, :] - fluxx[n, TPAD : TPAD + 128, :]
            diffx[i, PAD : PAD + 128, :] = value.T

    def sweep_y(last):
        items = [(base, 0), (prim, 1), (prim, 0), (prim, 2), (prim, 4), (base, 4)]
        for row in range(PAD, PAD + 128, 8):
            flux = sweep(items, lefty, row, 8, (base, 6))
            for i, n in enumerate((0, 2, 1, 3, 5, 4)):
                if i == 5 or row < SIDE or not last:
                    fluxy[i, row : row + 8, :] = flux[n]

    def beside_cols(parts, back):
        parts = [pltpu.roll(part, 1 if back else 127, 1) for part in parts]
        edge_lane = p8 == (0 if back else 127)
        return [
            jnp.where(edge_lane, parts[1], parts[0]),
            jnp.where(edge_lane, parts[0], parts[1]),
        ] + parts[2:]

    row_sets = [
        (PAD + 8 * c, SIDE + 8 * c) + ((MID + 8 * c,) if c < 4 else ()) for c in range(6)
    ]

    def edges():
        for rows in row_sets:
            shifted = beside_cols([fluxy[5, row : row + 8, :] for row in rows], True)
            for row, other in zip(rows, shifted):
                value = (fluxy[5, row : row + 8, :] + other) - (
                    gx[row : row + 8, :] + gx[row - 1 : row + 7, :]
                )
                edge[row : row + 8, :] = 0.125 * value

    def correct():
        value = edge[MID : MID + 32, :]
        values = (value, pltpu.roll(value, 127, 1))
        for step in range(2):
            finest = corner[step]
            coarse = (p32 + step >= 72) & (p32 + step < 120)
            halved_two = down_two(edge, (PAD, SIDE), False, False, step)
            halved_one = down_one(edge, MID, False, False, step)
            value = jnp.where((finest == 2) & ~coarse, halved_two, values[step])
            fixed[step, 0:32, :] = jnp.where((finest >= 1) & coarse, halved_one, value)

    def is_own(row):
        return PAD + 8 <= row < PAD + 40 or MID + 8 <= row < MID + 24

    def update_cells(i, last):
        for rows in row_sets:
            for k, row in enumerate(rows):
                if last and not is_own(row):
                    continue
                part = slice(row, row + 8)
                change = diffx[i, part, :] + (fluxy[i, row + 1 : row + 9, :] - fluxy[i, part, :])
                win[i, part, :] = base[i, part, :] - 0.5 * ratios[k] * change

    def update_faces(last):
        for rows in row_sets:
            values = [edge[row : row + 8, :] for row in rows[:2]]
            above = [edge[row + 1 : row + 9, :] for row in rows[:2]]
            others = beside_cols(values, False)
            for row in rows[2:]:
                first = row - MID
                values.append(fixed[0, first : first + 8, :])
                above.append(fixed[0, first + 1 : first + 9, :])
                others.append(fixed[1, first : first + 8, :])
            for row, ratio, value, up, other in zip(rows, ratios, values, above, others):
                if last and not is_own(row):
                    continue
                part = slice(row, row + 8)
                win[5, part, :] = base[5, part, :] - ratio * (up - value)
                win[6, part, :] = base[6, part, :] + ratio * (other - value)

    ratios = (STEP_SIZE, STEP_SIZE, jnp.where(is_coarse, STEP_SIZE / 4, STEP_SIZE / 2))

    def shared(fields):
        share_levels(win, base, lev, (0, 80), fields)

    def finish(fields):
        zero = jnp.zeros((8, COLS), F32)
        for f in fields:
            for c in range(4):
                value = win[f, PAD + 8 + 8 * c : PAD + 16 + 8 * c, :]
                if c < 2:
                    medium = win[f, MID + 8 + 8 * c : MID + 16 + 8 * c, :]
                    coarse = pltpu.roll(medium, 48, 1) if c == 0 else zero
                    lower = jnp.where(own_level == 1, medium, coarse)
                    value = jnp.where(own_level == 2, value, lower)
                used = p8 < jnp.where(own_level == 2, 128, jnp.where(own_level == 1, 64, 32))
                used = used & (own_level >= (0, 1, 2, 2)[c])
                blend = 0.5 * (fields_ref[f, 8 * c : 8 * c + 8, :] + value)
                result[f, 8 * c : 8 * c + 8, :] = jnp.where(used, blend, 0.0)
            pltpu.make_async_copy(result.at[f], out_ref.at[f], sems.at[f]).start()

    for section in range(2):
        last = section == 1
        then = (shared, finish)[section]
        primitives()
        sweep_y(last)
        sweep_x()
        edges()
        correct()
        update_cells(0, last)
        then((0,))
        update_faces(last)
        update_cells(1, last)
        then((1,))
        then((5, 6))
        for i in range(2, 5):
            update_cells(i, last)
            then((i,))
    for f in range(7):
        pltpu.make_async_copy(result.at[f], out_ref.at[f], sems.at[f]).wait()


def swapped_pairs(value, axis, first, stop):
    size = lax.axis_size(axis)
    pairs = [(i, (i + 1) % size) for i in range(first, stop, 2)]
    return lax.ppermute(value, axis, pairs + [(j, i) for i, j in pairs])


def swapped_subs(value, turn):
    rows, count = lax.axis_size("seg"), lax.axis_size("sub")
    pairs = []
    for s in range(rows):
        first, stop = ((0, count - 2), (1, count), (count - 2, count))[turn]
        if s == 0:
            first, stop = ((1, count - 1), (0, count), (count - 1, count))[turn]
        for u in range(first, stop, 2):
            a, b = s * count + u, s * count + (u + 1) % count
            pairs += [(a, b), (b, a)]
    return lax.ppermute(value, ("seg", "sub"), pairs)


def on_device(fields, region_levels):
    shape = jax.ShapeDtypeStruct
    params = pltpu.CompilerParams(vmem_limit_bytes=32 * 1024 * 1024)
    size = lax.axis_size("seg")
    close = swapped_pairs(fields, "seg", 2, size)
    far = swapped_pairs(fields, "seg", 1, size)
    first = swapped_pairs(fields, "seg", 0, 2)
    lev, lev_strips, corner, cols = pl.pallas_call(
        own_kernel,
        out_shape=(
            shape((128, COLS), jnp.int32),
            shape((104, COLS), jnp.int32),
            shape((2, 32, COLS), jnp.int32),
            shape((32, COLS), F32),
        ),
        in_specs=[HBM] * 2,
        out_specs=(VMEM,) * 4,
        scratch_shapes=[
            pltpu.VMEM(region_levels.shape[::-1], jnp.int32),
            pltpu.VMEM(fields.shape, F32),
            pltpu.VMEM((24, COLS), jnp.int32),
            pltpu.SemaphoreType.DMA((2,)),
        ],
        compiler_params=params,
    )(*(pltpu.with_memory_space_constraint(x, pltpu.HBM) for x in (region_levels.T, fields)))
    rows = shape((7, 8, COLS), F32)
    packed, below, above = pl.pallas_call(
        cols_kernel,
        out_shape=(shape((48, COLS), F32), rows, rows),
        in_specs=[VMEM] * 5,
        out_specs=(VMEM,) * 3,
        compiler_params=params,
    )(lev, cols, close, far, first)
    end, far, near = (swapped_subs(packed, turn) for turn in (2, 1, 0))
    own = pl.pallas_call(
        rows_kernel,
        out_shape=shape((7, PAD + 136, COLS), F32),
        in_specs=[VMEM] * 4,
        out_specs=VMEM,
        scratch_shapes=[pltpu.VMEM((7, PAD + 136, COLS), F32)],
        compiler_params=params,
    )(lev, fields, below, above)

    def window(*lead):
        return pltpu.VMEM((*lead, PAD + 136, COLS), F32)

    def across(*lead):
        return pltpu.VMEM((*lead, TPAD + 144, COLS), F32)

    return pl.pallas_call(
        main_kernel,
        out_shape=shape(fields.shape, F32),
        in_specs=[VMEM] * 8,
        out_specs=HBM,
        scratch_shapes=[
            window(7),
            window(7),
            window(5),
            window(6),
            window(6),
            window(),
            window(5),
            window(),
            pltpu.VMEM((2, 40, COLS), F32),
            across(7),
            across(6),
            across(6),
            pltpu.VMEM((112, COLS), F32),
            pltpu.VMEM(fields.shape, F32),
            pltpu.SemaphoreType.DMA((7,)),
        ],
        compiler_params=params,
    )(lev, lev_strips, corner, fields, own, end, far, near)


def solution(mesh):
    placed = (P(None, "seg", "sub"), P())
    return jax.shard_map(
        on_device, mesh=mesh, in_specs=placed, out_specs=P(None, "seg", "sub"), check_vma=False
    )
```

```python
from functools import partial

import jax
import jax.numpy as jnp
from jax import lax
from jax.experimental import pallas as pl
from jax.experimental.pallas import tpu as pltpu
from jax.sharding import PartitionSpec as P

STEP_SIZE = 0.08
ROWS, COLS = 32, 128
F32 = jnp.float32
VMEM = pl.BlockSpec(memory_space=pltpu.VMEM)
HBM = pl.BlockSpec(memory_space=pltpu.HBM)

PAD = 8
TPAD = 16
MID, SIDE = PAD + 48, PAD + 80


def lane(rows):
    return lax.broadcasted_iota(jnp.int32, (rows, COLS), 1)


def gather_lanes(value, index):
    return jnp.take_along_axis(value, index, axis=1, mode="promise_in_bounds")


def near_rows(levels_ref, held_ref):
    sub_count, seg_count = levels_ref.shape
    for j in range(3):
        u = lax.rem(lax.axis_index("sub") + (j - 1 + sub_count), sub_count)
        held_ref[8 * j : 8 * j + 1, 0:seg_count] = levels_ref[pl.ds(u, 1), :]
    table = []
    for i in range(3):
        s = lax.rem(lax.axis_index("seg") + (i - 1 + seg_count), seg_count)
        s = jnp.full((8, COLS), s, jnp.int32)
        rows = [jnp.broadcast_to(held_ref[8 * j : 8 * j + 1, :], (8, COLS)) for j in range(3)]
        table.append([gather_lanes(row, s) for row in rows])

    def level_of(i, offset):
        first, middle, last = table[i]
        return jnp.where(offset < 0, first, jnp.where(offset > 0, last, middle))

    return level_of


def last_rows(ref, f, level):
    return jnp.where(
        level == 2, ref[f, 24:32, :], jnp.where(level == 1, ref[f, 8:16, :], ref[f, 0:8, :])
    )


def packed_cols(read, level):
    p = lane(8)
    first = jnp.where(level == 2, 120, jnp.where(level == 1, 56, 24))
    index = (p & 7) + jnp.where((p & 15) < 8, first, 0)
    packed = gather_lanes(read(0), index)
    for f in range(1, 7):
        packed = jnp.where((p >> 4) == f, gather_lanes(read(f), index), packed)
    return packed


def own_kernel(levels_hbm, fields_hbm, lev, lev_strips, corner, cols_ref, levels_ref, fields_ref, held, sems):
    copies = [
        pltpu.make_async_copy(levels_hbm, levels_ref, sems.at[0]),
        pltpu.make_async_copy(fields_hbm, fields_ref, sems.at[1]),
    ]
    for copy in copies:
        copy.start()
    copies[0].wait()
    level_of = near_rows(levels_ref, held)
    p8 = lane(8)
    inner = (p8 < 64) | ((p8 >= 80) & (p8 < 112))
    outer = ((p8 >= 64) & (p8 < 72)) | ((p8 >= 112) & (p8 < 120))
    middle = jnp.zeros((8, COLS), jnp.int32)
    offsets = (middle, jnp.where(inner, 0, jnp.where(outer, 1, -1)), jnp.where(p8 < 64, 1, -1))
    is_coarse = (p8 >= 72) & (p8 < 120)
    for kind, first in enumerate((0, 48, 80)):
        below_row, centre_row, above_row = (level_of(i, offsets[kind]) for i in range(3))
        lev[first : first + 8, :] = below_row
        lev[first + 8 : first + 16, :] = centre_row
        if kind == 1:
            lev[first + 16 : first + 24, :] = jnp.where(is_coarse, above_row, centre_row)
            lev[first + 24 : first + 32, :] = above_row
        else:
            for r in (16, 24, 32):
                lev[first + r : first + r + 8, :] = centre_row
            lev[first + 40 : first + 48, :] = above_row
    offset = jnp.where((p8 & 15) < 8, -1, 1)
    below_row, centre_row, above_row = (level_of(i, offset) for i in range(3))
    for first, count in ((0, 6), (48, 4), (80, 3)):
        for r in range(count):
            row = below_row if r == 0 else above_row if r == count - 1 else centre_row
            lev_strips[first + 8 * r : first + 8 * r + 8, :] = row
    beside = lev[48:80, :]
    beside = jnp.maximum(beside, pltpu.roll(beside, 1, 1))
    corner[0] = jnp.maximum(beside, pltpu.roll(beside, 1, 0))
    corner[1] = pltpu.roll(corner[0], 127, 1)
    own = lev[8:16, :]
    copies[1].wait()
    for r in range(0, 32, 8):
        cols_ref[r : r + 8, :] = packed_cols(lambda f: fields_ref[f, r : r + 8, :], own)


def cols_kernel(lev, cols_ref, third_ref, second_ref, first_ref, out_ref, below_ref, above_ref):
    seg, size = lax.axis_index("seg"), lax.axis_size("seg")
    seg = jnp.full((8, COLS), seg)
    even = (seg & 1) == 0
    head, tail = seg < 2, seg >= size - 1
    far_second = head | tail | (seg == 2)
    close_third = (seg == 2) | (seg == 3) | (seg >= size - 2)
    below_level, above_level = lev[0:8, :], lev[40:48, :]

    def picked(values):
        first, second, third = values
        far = jnp.where(far_second, second, first)
        return far, jnp.where(close_third, third, jnp.where(head, first, second))

    for f in range(7):
        refs = (first_ref, second_ref, third_ref)
        far, close = picked([last_rows(ref, f, below_level) for ref in refs])
        below_ref[f] = jnp.where(even, far, close)
        far, close = picked([ref[f, 0:8, :] for ref in refs])
        above_ref[f] = jnp.where(even, close, far)
    out_ref[0:8, :] = packed_cols(lambda f: below_ref[f], below_level)
    out_ref[8:40, :] = cols_ref[...]
    out_ref[40:48, :] = packed_cols(lambda f: above_ref[f], above_level)


def minmod(a, b):
    return jnp.minimum(jnp.maximum(b, jnp.minimum(a, 0.0)), jnp.maximum(a, 0.0))


def riemann(left, right, normal):
    rho_l, vn_l, vt_l, vz_l, bt_l, bz_l = left
    rho_r, vn_r, vt_r, vz_r, bt_r, bz_r = right
    normal_square = normal * normal

    def signal(density, speed, square):
        total = density + (square + normal_square)
        return jnp.abs(speed) + jnp.abs(total) * lax.rsqrt(density * total)

    square_l = bt_l * bt_l + bz_l * bz_l
    square_r = bt_r * bt_r + bz_r * bz_r
    fastest = jnp.maximum(signal(rho_l, vn_l, square_l), signal(rho_r, vn_r, square_r))
    ahead, back = vn_l + fastest, vn_r - fastest
    mass_l, mass_r = rho_l * ahead, rho_r * back
    pressure = (rho_l + rho_r) + 0.5 * (square_l + square_r)
    return [
        mass_l + mass_r,
        (mass_l * vn_l + mass_r * vn_r) + (pressure - normal_square),
        (mass_l * vt_l + mass_r * vt_r) - normal * (bt_l + bt_r),
        (mass_l * vz_l + mass_r * vz_r) - normal * (bz_l + bz_r),
        (bt_l * ahead + bt_r * back) - normal * (vt_l + vt_r),
        (bz_l * ahead + bz_r * back) - normal * (vz_l + vz_r),
    ]


def doubled(part):
    low = lax.broadcasted_iota(jnp.int32, (8, COLS), 0) >> 1
    rows = []
    for r in range(0, part.shape[0], 8):
        for index in (low, low + 4):
            rows.append(
                jnp.take_along_axis(part[r : r + 8], index, axis=0, mode="promise_in_bounds")
            )
    return jnp.concatenate(rows, axis=0)


def rows_halved(ref, first, by_rows):
    initial = ref[pl.ds(first - 8, 32, stride=2), :]
    if not by_rows:
        return initial
    return 0.5 * (initial + ref[pl.ds(first - 7, 32, stride=2), :])


def paired_lanes(value, index, by_cols):
    initial = gather_lanes(value, index)
    return 0.5 * (initial + gather_lanes(value, index + 1)) if by_cols else initial


def down_two(ref, firsts, by_rows, by_cols, step=0):
    p = lane(32) + step
    index = (2 * p) & 127
    parts = [rows_halved(ref, first, by_rows) for first in firsts]
    if len(parts) == 1:
        return paired_lanes(parts[0], index, by_cols)
    inside = (p & 127) < 64
    picks = []
    for k in range(2 if by_cols else 1):
        picks.append(jnp.where(inside, gather_lanes(parts[0], index + k), gather_lanes(parts[1], index + k)))
    return 0.5 * (picks[0] + picks[1]) if by_cols else picks[0]


def down_one(ref, first, by_rows, by_cols, step=0):
    return paired_lanes(
        rows_halved(ref, first, by_rows), (2 * (lane(32) + step - 80)) & 127, by_cols
    )


def share_levels(win, out, lev, blocks, fields):
    p32, p24, p16 = lane(32), lane(24), lane(16)
    coarse32 = (p32 >= 72) & (p32 < 120)
    level_b = lev[48:80, :]
    up_one = jnp.where(p16 < 72, 80 + (p16 >> 1), jnp.where(p16 >= 120, 16 + (p16 >> 1), p16))
    up_two = (p24 >> 1, 64 + (p24 >> 1))
    for f in fields:
        by_rows, by_cols = f != 6, f != 5
        value = win[f, MID : MID + 32, :]
        up = doubled(gather_lanes(win[f, MID + 4 : MID + 20, :], up_one))
        part = win[f, MID + 4 : MID + 28, :]
        ups = [doubled(gather_lanes(part, up_two[k])) for k in range(len(blocks))]
        down = down_two(win.at[f], [PAD + first for first in blocks], by_rows, by_cols)
        last = down_one(win.at[f], MID, by_rows, by_cols)
        medium = jnp.where(level_b == 0, up, jnp.where(level_b == 2, down, value))
        coarse = jnp.where(level_b >= 1, last, value)
        for first, injected in zip(blocks, ups):
            rows = slice(PAD + first, PAD + first + 48)
            out[f, rows, :] = jnp.where(lev[first : first + 48, :] == 2, win[f, rows, :], injected)
        out[f, MID : MID + 32, :] = jnp.where(coarse32, coarse, medium)


def rows_kernel(lev, fields_ref, below_ref, above_ref, out_ref, win):
    p8 = lane(8)
    is_coarse = (p8 >= 72) & (p8 < 120)

    def joined(fine, coarse):
        return jnp.where(is_coarse, pltpu.roll(coarse, 80, 1), fine)

    for f in range(7):
        below, above = below_ref[f], above_ref[f]
        initial, second = fields_ref[f, 0:8, :], fields_ref[f, 8:16, :]
        win[f, PAD : PAD + 8, :] = below
        win[f, PAD + 8 : PAD + 40, :] = fields_ref[f]
        win[f, PAD + 40 : PAD + 48, :] = above
        win[f, MID : MID + 8, :] = joined(below, below)
        win[f, MID + 8 : MID + 16, :] = joined(initial, initial)
        win[f, MID + 16 : MID + 24, :] = joined(second, above)
        win[f, MID + 24 : MID + 32, :] = above
    share_levels(win, out_ref, lev, (0,), range(7))


def share_strips(strips, lev_strips, held):
    p = lane(32)
    k = p & 15
    up = (p - k) + jnp.where(k < 8, 4 + (k >> 1), 8 + ((k - 8) >> 1))
    down = (p - k) + ((2 * k - 8) & 15)
    held[8:56, :] = strips
    held[56:80, :] = strips[0:24]
    held[80:88, :] = strips[40:48]
    held[88:104, :] = strips[0:16]
    held[104:112, :] = strips[40:48]

    def halved(first, count):
        initial = held[pl.ds(first - 8, count, stride=2), :]
        mean = 0.5 * (initial + held[pl.ds(first - 7, count, stride=2), :])
        f = lane(count) >> 4
        value = jnp.where(f == 6, initial, mean)
        even, odd = (gather_lanes(value, down[0:count] + k) for k in range(2))
        return jnp.where(f == 5, even, 0.5 * (even + odd))

    levels = [lev_strips[first : first + count, :] for first, count in ((0, 48), (48, 32), (80, 24))]
    up_one = doubled(gather_lanes(held[92:108, :], up[0:16]))
    up_two = doubled(gather_lanes(held[60:84, :], up[0:24]))
    down_to_one, down_to_none = halved(8, 32), halved(56, 24)
    fine = jnp.where(levels[0] == 2, held[8:56, :], up_two)
    medium = jnp.where(levels[1] == 2, down_to_one, held[56:88, :])
    medium = jnp.where(levels[1] == 0, up_one, medium)
    coarse = jnp.where(levels[2] >= 1, down_to_none, held[88:112, :])
    return fine, medium, coarse


def main_kernel(
    lev,
    lev_strips,
    corner,
    fields_ref,
    own_ref,
    last_ref,
    far_ref,
    near_ref,
    out_ref,
    win,
    base,
    prim,
    lefty,
    fluxy,
    gx,
    diffx,
    edge,
    fixed,
    turned,
    leftx,
    fluxx,
    held,
    result,
    sems,
):
    p32, p8 = lane(32), lane(8)
    is_coarse = (p8 >= 72) & (p8 < 120)
    own_level = lev[8:16, :]

    p48 = lane(48)
    sub, count = lax.axis_index("sub"), lax.axis_size("sub")
    first_row = lax.axis_index("seg") == 0
    sub = jnp.full((48, COLS), sub)
    even = jnp.where(first_row, 1 - (sub & 1), sub & 1) == 0
    third = jnp.where(first_row, jnp.where(sub == 0, count - 1, sub), sub + 1) >= count - 1
    near = jnp.where(third, last_ref[...], near_ref[...])
    strips = jnp.where(((p48 & 15) < 8) == even, far_ref[...], near)
    fine, medium, coarse = share_strips(strips, lev_strips, held)
    strip_one = ((p32 >= 64) & (p32 < 72)) | (p32 >= 120)
    strip_none = ((p32 >= 72) & (p32 < 80)) | ((p32 >= 112) & (p32 < 120))
    right_side = ((p32 >= 64) & (p32 < 72)) | ((p32 >= 112) & (p32 < 120))
    strip_index = (p32 & 7) + jnp.where(right_side, 8, 0)
    for f in range(7):
        index = strip_index + 16 * f
        base[f, PAD : PAD + 48, :] = own_ref[f, PAD : PAD + 48, :]
        base[f, SIDE : SIDE + 48, :] = pltpu.roll(fine, (120 - 16 * f) % 128, 1)
        value = jnp.where(strip_one, gather_lanes(medium, index), own_ref[f, MID : MID + 32, :])
        base[f, MID + 24 : MID + 32, :] = value[24:32]
        base[f, MID : MID + 24, :] = jnp.where(
            strip_none[0:24], gather_lanes(coarse, index[0:24]), value[0:24]
        )

    def swapped(value):
        return gather_lanes(value, jnp.where(p8 < 48, p8 + 80, jnp.where(p8 < 80, p8, p8 - 80)))

    def turn(slot, value):
        value = value.T
        turned[slot, TPAD : TPAD + 128, :] = value
        turned[slot, TPAD - 8 : TPAD, :] = swapped(value[120:128])
        turned[slot, TPAD + 128 : TPAD + 136, :] = swapped(value[0:8])

    chunks = [PAD + 16 * c for c in range(8)]

    def primitives():
        for row in chunks:
            rows = slice(row, row + 16)
            inverse = 1.0 / base[0, rows, :]
            for i in range(3):
                prim[i, rows, :] = base[1 + i, rows, :] * inverse
            prim[3, rows, :] = 0.5 * (base[6, rows, :] + base[6, row + 1 : row + 17, :])
        for rows in row_sets:
            faces = [base[5, row : row + 8, :] for row in rows]
            for row, face, other in zip(rows, faces, beside_cols(faces, False)):
                prim[4, row : row + 8, :] = 0.5 * (face + other)
        sources = [(base, 0), (prim, 0), (prim, 1), (prim, 2), (prim, 3), (base, 4), (base, 5)]
        for slot, (ref, i) in enumerate(sources):
            turn(slot, ref[i, PAD : PAD + 128, :])

    def sweep(items, lefts, row, count, normal):
        def at(item, step):
            ref, i = item
            return ref[i, row + step : row + step + count, :]

        left, right = [], []
        for i, item in enumerate(items):
            value = at(item, 0)
            slope = 0.5 * minmod(value - at(item, -1), at(item, 1) - value)
            lefts[i, row : row + count, :] = value + slope
            if normal is not None:
                left.append(lefts[i, row - 1 : row - 1 + count, :])
                right.append(value - slope)
        if normal is None:
            return None
        return riemann(left, right, at(normal, 0))

    def sweep_x():
        items = [(turned, i) for i in range(6)]
        sweep(items, leftx, TPAD - 8, 8, None)
        for row in range(TPAD, TPAD + 136, 8):
            count = min(8, TPAD + 136 - row)
            flux = sweep(items, leftx, row, count, (turned, 6))
            for i, value in enumerate(flux):
                fluxx[i, row : row + count, :] = value
        gx[PAD : PAD + 128, :] = fluxx[4, TPAD : TPAD + 128, :].T
        for i, n in enumerate((0, 1, 2, 3, 5)):
            value = fluxx[n, TPAD + 1 : TPAD + 129, :] - fluxx[n, TPAD : TPAD + 128, :]
            diffx[i, PAD : PAD + 128, :] = value.T

    def sweep_y(last):
        items = [(base, 0), (prim, 1), (prim, 0), (prim, 2), (prim, 4), (base, 4)]
        for row in range(PAD, PAD + 128, 8):
            flux = sweep(items, lefty, row, 8, (base, 6))
            for i, n in enumerate((0, 2, 1, 3, 5, 4)):
                if i == 5 or row < SIDE or not last:
                    fluxy[i, row : row + 8, :] = flux[n]

    def beside_cols(parts, back):
        parts = [pltpu.roll(part, 1 if back else 127, 1) for part in parts]
        edge_lane = p8 == (0 if back else 127)
        return [
            jnp.where(edge_lane, parts[1], parts[0]),
            jnp.where(edge_lane, parts[0], parts[1]),
        ] + parts[2:]

    row_sets = [
        (PAD + 8 * c, SIDE + 8 * c) + ((MID + 8 * c,) if c < 4 else ()) for c in range(6)
    ]

    def edges():
        for rows in row_sets:
            shifted = beside_cols([fluxy[5, row : row + 8, :] for row in rows], True)
            for row, other in zip(rows, shifted):
                value = (fluxy[5, row : row + 8, :] + other) - (
                    gx[row : row + 8, :] + gx[row - 1 : row + 7, :]
                )
                edge[row : row + 8, :] = 0.125 * value

    def correct():
        value = edge[MID : MID + 32, :]
        values = (value, pltpu.roll(value, 127, 1))
        for step in range(2):
            finest = corner[step]
            coarse = (p32 + step >= 72) & (p32 + step < 120)
            halved_two = down_two(edge, (PAD, SIDE), False, False, step)
            halved_one = down_one(edge, MID, False, False, step)
            value = jnp.where((finest == 2) & ~coarse, halved_two, values[step])
            fixed[step, 0:32, :] = jnp.where((finest >= 1) & coarse, halved_one, value)

    def is_own(row):
        return PAD + 8 <= row < PAD + 40 or MID + 8 <= row < MID + 24

    def update_cells(i, last):
        for rows in row_sets:
            for k, row in enumerate(rows):
                if last and not is_own(row):
                    continue
                part = slice(row, row + 8)
                change = diffx[i, part, :] + (fluxy[i, row + 1 : row + 9, :] - fluxy[i, part, :])
                win[i, part, :] = base[i, part, :] - 0.5 * ratios[k] * change

    def update_faces(last):
        for rows in row_sets:
            values = [edge[row : row + 8, :] for row in rows[:2]]
            above = [edge[row + 1 : row + 9, :] for row in rows[:2]]
            others = beside_cols(values, False)
            for row in rows[2:]:
                first = row - MID
                values.append(fixed[0, first : first + 8, :])
                above.append(fixed[0, first + 1 : first + 9, :])
                others.append(fixed[1, first : first + 8, :])
            for row, ratio, value, up, other in zip(rows, ratios, values, above, others):
                if last and not is_own(row):
                    continue
                part = slice(row, row + 8)
                win[5, part, :] = base[5, part, :] - ratio * (up - value)
                win[6, part, :] = base[6, part, :] + ratio * (other - value)

    ratios = (STEP_SIZE, STEP_SIZE, jnp.where(is_coarse, STEP_SIZE / 4, STEP_SIZE / 2))

    def shared(fields):
        share_levels(win, base, lev, (0, 80), fields)

    def finish(fields):
        zero = jnp.zeros((8, COLS), F32)
        for f in fields:
            for c in range(4):
                value = win[f, PAD + 8 + 8 * c : PAD + 16 + 8 * c, :]
                if c < 2:
                    medium = win[f, MID + 8 + 8 * c : MID + 16 + 8 * c, :]
                    coarse = pltpu.roll(medium, 48, 1) if c == 0 else zero
                    lower = jnp.where(own_level == 1, medium, coarse)
                    value = jnp.where(own_level == 2, value, lower)
                used = p8 < jnp.where(own_level == 2, 128, jnp.where(own_level == 1, 64, 32))
                used = used & (own_level >= (0, 1, 2, 2)[c])
                blend = 0.5 * (fields_ref[f, 8 * c : 8 * c + 8, :] + value)
                result[f, 8 * c : 8 * c + 8, :] = jnp.where(used, blend, 0.0)
            pltpu.make_async_copy(result.at[f], out_ref.at[f], sems.at[f]).start()

    for section in range(2):
        last = section == 1
        then = (shared, finish)[section]
        primitives()
        sweep_y(last)
        sweep_x()
        edges()
        correct()
        update_cells(0, last)
        then((0,))
        update_faces(last)
        update_cells(1, last)
        then((1,))
        then((5, 6))
        for i in range(2, 5):
            update_cells(i, last)
            then((i,))
    for f in range(7):
        pltpu.make_async_copy(result.at[f], out_ref.at[f], sems.at[f]).wait()


def swapped_segs(value, turn):
    size = lax.axis_size("seg")
    starts = (
        [0, *range(3, size - 2, 2)],
        [size - 1, 1, *range(4, size - 2, 2)],
        [2, size - 2] if size > 4 else [2],
    )[turn]
    pairs = [(i, (i + 1) % size) for i in starts]
    return lax.ppermute(value, "seg", pairs + [(j, i) for i, j in pairs])


def swapped_subs(value, turn):
    rows, count = lax.axis_size("seg"), lax.axis_size("sub")
    pairs = []
    for s in range(rows):
        first, stop = ((0, count - 2), (1, count), (count - 2, count))[turn]
        if s == 0:
            first, stop = ((1, count - 1), (0, count), (count - 1, count))[turn]
        for u in range(first, stop, 2):
            a, b = s * count + u, s * count + (u + 1) % count
            pairs += [(a, b), (b, a)]
    return lax.ppermute(value, ("seg", "sub"), pairs)


def on_device(fields, region_levels):
    shape = jax.ShapeDtypeStruct
    params = pltpu.CompilerParams(vmem_limit_bytes=32 * 1024 * 1024)
    third, second, first = (swapped_segs(fields, turn) for turn in (2, 1, 0))
    lev, lev_strips, corner, cols = pl.pallas_call(
        own_kernel,
        out_shape=(
            shape((128, COLS), jnp.int32),
            shape((104, COLS), jnp.int32),
            shape((2, 32, COLS), jnp.int32),
            shape((32, COLS), F32),
        ),
        in_specs=[HBM] * 2,
        out_specs=(VMEM,) * 4,
        scratch_shapes=[
            pltpu.VMEM(region_levels.shape[::-1], jnp.int32),
            pltpu.VMEM(fields.shape, F32),
            pltpu.VMEM((24, COLS), jnp.int32),
            pltpu.SemaphoreType.DMA((2,)),
        ],
        compiler_params=params,
    )(*(pltpu.with_memory_space_constraint(x, pltpu.HBM) for x in (region_levels.T, fields)))
    rows = shape((7, 8, COLS), F32)
    packed, below, above = pl.pallas_call(
        cols_kernel,
        out_shape=(shape((48, COLS), F32), rows, rows),
        in_specs=[VMEM] * 5,
        out_specs=(VMEM,) * 3,
        compiler_params=params,
    )(lev, cols, third, second, first)
    end, far, near = (swapped_subs(packed, turn) for turn in (2, 1, 0))
    own = pl.pallas_call(
        rows_kernel,
        out_shape=shape((7, PAD + 136, COLS), F32),
        in_specs=[VMEM] * 4,
        out_specs=VMEM,
        scratch_shapes=[pltpu.VMEM((7, PAD + 136, COLS), F32)],
        compiler_params=params,
    )(lev, fields, below, above)

    def window(*lead):
        return pltpu.VMEM((*lead, PAD + 136, COLS), F32)

    def across(*lead):
        return pltpu.VMEM((*lead, TPAD + 144, COLS), F32)

    return pl.pallas_call(
        main_kernel,
        out_shape=shape(fields.shape, F32),
        in_specs=[VMEM] * 8,
        out_specs=HBM,
        scratch_shapes=[
            window(7),
            window(7),
            window(5),
            window(6),
            window(6),
            window(),
            window(5),
            window(),
            pltpu.VMEM((2, 40, COLS), F32),
            across(7),
            across(6),
            across(6),
            pltpu.VMEM((112, COLS), F32),
            pltpu.VMEM(fields.shape, F32),
            pltpu.SemaphoreType.DMA((7,)),
        ],
        compiler_params=params,
    )(lev, lev_strips, corner, fields, own, end, far, near)


def solution(mesh):
    placed = (P(None, "seg", "sub"), P())
    return jax.shard_map(
        on_device, mesh=mesh, in_specs=placed, out_specs=P(None, "seg", "sub"), check_vma=False
    )
```

```python
from functools import partial

import jax
import jax.numpy as jnp
from jax import lax
from jax.experimental import pallas as pl
from jax.experimental.pallas import tpu as pltpu
from jax.sharding import PartitionSpec as P

STEP_SIZE = 0.08
ROWS, COLS = 32, 128
F32 = jnp.float32
VMEM = pl.BlockSpec(memory_space=pltpu.VMEM)
HBM = pl.BlockSpec(memory_space=pltpu.HBM)

PAD = 8
TPAD = 16
MID, SIDE = PAD + 48, PAD + 80


def lane(rows):
    return lax.broadcasted_iota(jnp.int32, (rows, COLS), 1)


def gather_lanes(value, index):
    return jnp.take_along_axis(value, index, axis=1, mode="promise_in_bounds")


def near_rows(levels_ref, held_ref):
    sub_count, seg_count = levels_ref.shape
    for j in range(3):
        u = lax.rem(lax.axis_index("sub") + (j - 1 + sub_count), sub_count)
        held_ref[8 * j : 8 * j + 1, 0:seg_count] = levels_ref[pl.ds(u, 1), :]
    table = []
    for i in range(3):
        s = lax.rem(lax.axis_index("seg") + (i - 1 + seg_count), seg_count)
        s = jnp.full((8, COLS), s, jnp.int32)
        rows = [jnp.broadcast_to(held_ref[8 * j : 8 * j + 1, :], (8, COLS)) for j in range(3)]
        table.append([gather_lanes(row, s) for row in rows])

    def level_of(i, offset):
        first, middle, last = table[i]
        return jnp.where(offset < 0, first, jnp.where(offset > 0, last, middle))

    return level_of


def last_rows(ref, f, level):
    return jnp.where(
        level == 2, ref[f, 24:32, :], jnp.where(level == 1, ref[f, 8:16, :], ref[f, 0:8, :])
    )


def packed_cols(read, level):
    p = lane(8)
    first = jnp.where(level == 2, 120, jnp.where(level == 1, 56, 24))
    index = (p & 7) + jnp.where((p & 15) < 8, first, 0)
    packed = gather_lanes(read(0), index)
    for f in range(1, 7):
        packed = jnp.where((p >> 4) == f, gather_lanes(read(f), index), packed)
    return packed


def own_kernel(levels_hbm, fields_hbm, lev, lev_strips, corner, cols_ref, fields_ref, levels_ref, held, sems):
    copies = [
        pltpu.make_async_copy(levels_hbm, levels_ref, sems.at[0]),
        pltpu.make_async_copy(fields_hbm, fields_ref, sems.at[1]),
    ]
    for copy in copies:
        copy.start()
    copies[0].wait()
    level_of = near_rows(levels_ref, held)
    p8 = lane(8)
    inner = (p8 < 64) | ((p8 >= 80) & (p8 < 112))
    outer = ((p8 >= 64) & (p8 < 72)) | ((p8 >= 112) & (p8 < 120))
    middle = jnp.zeros((8, COLS), jnp.int32)
    offsets = (middle, jnp.where(inner, 0, jnp.where(outer, 1, -1)), jnp.where(p8 < 64, 1, -1))
    is_coarse = (p8 >= 72) & (p8 < 120)
    for kind, first in enumerate((0, 48, 80)):
        below_row, centre_row, above_row = (level_of(i, offsets[kind]) for i in range(3))
        lev[first : first + 8, :] = below_row
        lev[first + 8 : first + 16, :] = centre_row
        if kind == 1:
            lev[first + 16 : first + 24, :] = jnp.where(is_coarse, above_row, centre_row)
            lev[first + 24 : first + 32, :] = above_row
        else:
            for r in (16, 24, 32):
                lev[first + r : first + r + 8, :] = centre_row
            lev[first + 40 : first + 48, :] = above_row
    offset = jnp.where((p8 & 15) < 8, -1, 1)
    below_row, centre_row, above_row = (level_of(i, offset) for i in range(3))
    for first, count in ((0, 6), (48, 4), (80, 3)):
        for r in range(count):
            row = below_row if r == 0 else above_row if r == count - 1 else centre_row
            lev_strips[first + 8 * r : first + 8 * r + 8, :] = row
    beside = lev[48:80, :]
    beside = jnp.maximum(beside, pltpu.roll(beside, 1, 1))
    corner[0] = jnp.maximum(beside, pltpu.roll(beside, 1, 0))
    corner[1] = pltpu.roll(corner[0], 127, 1)
    own = lev[8:16, :]
    copies[1].wait()
    for r in range(0, 32, 8):
        cols_ref[r : r + 8, :] = packed_cols(lambda f: fields_ref[f, r : r + 8, :], own)


def cols_kernel(
    lev,
    cols_ref,
    fields_ref,
    first_ref,
    third_ref,
    second_ref,
    out_ref,
    below_ref,
    above_ref,
    own_ref,
    win,
):
    seg, size = lax.axis_index("seg"), lax.axis_size("seg")
    seg = jnp.full((8, COLS), seg)
    even = (seg & 1) == 0
    head, tail = seg < 2, seg >= size - 1
    far_second = head | tail | (seg == 2)
    close_third = (seg == 2) | (seg == 3) | (seg >= size - 2)
    below_level, above_level = lev[0:8, :], lev[40:48, :]

    def picked(values):
        first, second, third = values
        far = jnp.where(far_second, second, first)
        return far, jnp.where(close_third, third, jnp.where(head, first, second))

    for f in range(7):
        refs = (first_ref, second_ref, third_ref)
        far, close = picked([last_rows(ref, f, below_level) for ref in refs])
        below_ref[f] = jnp.where(even, far, close)
        far, close = picked([ref[f, 0:8, :] for ref in refs])
        above_ref[f] = jnp.where(even, close, far)
    out_ref[0:8, :] = packed_cols(lambda f: below_ref[f], below_level)
    out_ref[8:40, :] = cols_ref[...]
    out_ref[40:48, :] = packed_cols(lambda f: above_ref[f], above_level)

    @pl.when(lax.axis_index("sub") == 0)
    def _():
        own_windows(lev, fields_ref, below_ref, above_ref, own_ref, win)


def minmod(a, b):
    return jnp.minimum(jnp.maximum(b, jnp.minimum(a, 0.0)), jnp.maximum(a, 0.0))


def riemann(left, right, normal):
    rho_l, vn_l, vt_l, vz_l, bt_l, bz_l = left
    rho_r, vn_r, vt_r, vz_r, bt_r, bz_r = right
    normal_square = normal * normal

    def signal(density, speed, square):
        total = density + (square + normal_square)
        return jnp.abs(speed) + jnp.abs(total) * lax.rsqrt(density * total)

    square_l = bt_l * bt_l + bz_l * bz_l
    square_r = bt_r * bt_r + bz_r * bz_r
    fastest = jnp.maximum(signal(rho_l, vn_l, square_l), signal(rho_r, vn_r, square_r))
    ahead, back = vn_l + fastest, vn_r - fastest
    mass_l, mass_r = rho_l * ahead, rho_r * back
    pressure = (rho_l + rho_r) + 0.5 * (square_l + square_r)
    return [
        mass_l + mass_r,
        (mass_l * vn_l + mass_r * vn_r) + (pressure - normal_square),
        (mass_l * vt_l + mass_r * vt_r) - normal * (bt_l + bt_r),
        (mass_l * vz_l + mass_r * vz_r) - normal * (bz_l + bz_r),
        (bt_l * ahead + bt_r * back) - normal * (vt_l + vt_r),
        (bz_l * ahead + bz_r * back) - normal * (vz_l + vz_r),
    ]


def doubled(part):
    low = lax.broadcasted_iota(jnp.int32, (8, COLS), 0) >> 1
    rows = []
    for r in range(0, part.shape[0], 8):
        for index in (low, low + 4):
            rows.append(
                jnp.take_along_axis(part[r : r + 8], index, axis=0, mode="promise_in_bounds")
            )
    return jnp.concatenate(rows, axis=0)


def rows_halved(ref, first, by_rows):
    initial = ref[pl.ds(first - 8, 32, stride=2), :]
    if not by_rows:
        return initial
    return 0.5 * (initial + ref[pl.ds(first - 7, 32, stride=2), :])


def paired_lanes(value, index, by_cols):
    initial = gather_lanes(value, index)
    return 0.5 * (initial + gather_lanes(value, index + 1)) if by_cols else initial


def down_two(ref, firsts, by_rows, by_cols, step=0):
    p = lane(32) + step
    index = (2 * p) & 127
    parts = [rows_halved(ref, first, by_rows) for first in firsts]
    if len(parts) == 1:
        return paired_lanes(parts[0], index, by_cols)
    inside = (p & 127) < 64
    picks = []
    for k in range(2 if by_cols else 1):
        picks.append(jnp.where(inside, gather_lanes(parts[0], index + k), gather_lanes(parts[1], index + k)))
    return 0.5 * (picks[0] + picks[1]) if by_cols else picks[0]


def down_one(ref, first, by_rows, by_cols, step=0):
    return paired_lanes(
        rows_halved(ref, first, by_rows), (2 * (lane(32) + step - 80)) & 127, by_cols
    )


def share_levels(win, out, lev, blocks, fields):
    p32, p24, p16 = lane(32), lane(24), lane(16)
    coarse32 = (p32 >= 72) & (p32 < 120)
    level_b = lev[48:80, :]
    up_one = jnp.where(p16 < 72, 80 + (p16 >> 1), jnp.where(p16 >= 120, 16 + (p16 >> 1), p16))
    up_two = (p24 >> 1, 64 + (p24 >> 1))
    for f in fields:
        by_rows, by_cols = f != 6, f != 5
        value = win[f, MID : MID + 32, :]
        up = doubled(gather_lanes(win[f, MID + 4 : MID + 20, :], up_one))
        part = win[f, MID + 4 : MID + 28, :]
        ups = [doubled(gather_lanes(part, up_two[k])) for k in range(len(blocks))]
        down = down_two(win.at[f], [PAD + first for first in blocks], by_rows, by_cols)
        last = down_one(win.at[f], MID, by_rows, by_cols)
        medium = jnp.where(level_b == 0, up, jnp.where(level_b == 2, down, value))
        coarse = jnp.where(level_b >= 1, last, value)
        for first, injected in zip(blocks, ups):
            rows = slice(PAD + first, PAD + first + 48)
            out[f, rows, :] = jnp.where(lev[first : first + 48, :] == 2, win[f, rows, :], injected)
        out[f, MID : MID + 32, :] = jnp.where(coarse32, coarse, medium)


def rows_kernel(lev, fields_ref, below_ref, above_ref, held_ref, out_ref, win):
    @pl.when(lax.axis_index("sub") != 0)
    def _():
        own_windows(lev, fields_ref, below_ref, above_ref, out_ref, win)


def own_windows(lev, fields_ref, below_ref, above_ref, out_ref, win):
    p8 = lane(8)
    is_coarse = (p8 >= 72) & (p8 < 120)

    def joined(fine, coarse):
        return jnp.where(is_coarse, pltpu.roll(coarse, 80, 1), fine)

    for f in range(7):
        below, above = below_ref[f], above_ref[f]
        initial, second = fields_ref[f, 0:8, :], fields_ref[f, 8:16, :]
        win[f, PAD : PAD + 8, :] = below
        win[f, PAD + 8 : PAD + 40, :] = fields_ref[f]
        win[f, PAD + 40 : PAD + 48, :] = above
        win[f, MID : MID + 8, :] = joined(below, below)
        win[f, MID + 8 : MID + 16, :] = joined(initial, initial)
        win[f, MID + 16 : MID + 24, :] = joined(second, above)
        win[f, MID + 24 : MID + 32, :] = above
    share_levels(win, out_ref, lev, (0,), range(7))


def share_strips(strips, lev_strips, held):
    p = lane(32)
    k = p & 15
    up = (p - k) + jnp.where(k < 8, 4 + (k >> 1), 8 + ((k - 8) >> 1))
    down = (p - k) + ((2 * k - 8) & 15)
    held[8:56, :] = strips
    held[56:80, :] = strips[0:24]
    held[80:88, :] = strips[40:48]
    held[88:104, :] = strips[0:16]
    held[104:112, :] = strips[40:48]

    def halved(first, count):
        initial = held[pl.ds(first - 8, count, stride=2), :]
        mean = 0.5 * (initial + held[pl.ds(first - 7, count, stride=2), :])
        f = lane(count) >> 4
        value = jnp.where(f == 6, initial, mean)
        even, odd = (gather_lanes(value, down[0:count] + k) for k in range(2))
        return jnp.where(f == 5, even, 0.5 * (even + odd))

    levels = [lev_strips[first : first + count, :] for first, count in ((0, 48), (48, 32), (80, 24))]
    up_one = doubled(gather_lanes(held[92:108, :], up[0:16]))
    up_two = doubled(gather_lanes(held[60:84, :], up[0:24]))
    down_to_one, down_to_none = halved(8, 32), halved(56, 24)
    fine = jnp.where(levels[0] == 2, held[8:56, :], up_two)
    medium = jnp.where(levels[1] == 2, down_to_one, held[56:88, :])
    medium = jnp.where(levels[1] == 0, up_one, medium)
    coarse = jnp.where(levels[2] >= 1, down_to_none, held[88:112, :])
    return fine, medium, coarse


def main_kernel(
    lev,
    lev_strips,
    corner,
    fields_ref,
    own_ref,
    last_ref,
    far_ref,
    near_ref,
    out_ref,
    win,
    base,
    prim,
    lefty,
    fluxy,
    gx,
    diffx,
    edge,
    fixed,
    turned,
    leftx,
    fluxx,
    held,
    result,
    sems,
):
    p32, p8 = lane(32), lane(8)
    is_coarse = (p8 >= 72) & (p8 < 120)
    own_level = lev[8:16, :]

    p48 = lane(48)
    sub, count = lax.axis_index("sub"), lax.axis_size("sub")
    first_row = lax.axis_index("seg") == 0
    sub = jnp.full((48, COLS), sub)
    even = jnp.where(first_row, 1 - (sub & 1), sub & 1) == 0
    third = jnp.where(first_row, jnp.where(sub == 0, count - 1, sub), sub + 1) >= count - 1
    near = jnp.where(third, last_ref[...], near_ref[...])
    strips = jnp.where(((p48 & 15) < 8) == even, far_ref[...], near)
    fine, medium, coarse = share_strips(strips, lev_strips, held)
    strip_one = ((p32 >= 64) & (p32 < 72)) | (p32 >= 120)
    strip_none = ((p32 >= 72) & (p32 < 80)) | ((p32 >= 112) & (p32 < 120))
    right_side = ((p32 >= 64) & (p32 < 72)) | ((p32 >= 112) & (p32 < 120))
    strip_index = (p32 & 7) + jnp.where(right_side, 8, 0)
    for f in range(7):
        index = strip_index + 16 * f
        base[f, PAD : PAD + 48, :] = own_ref[f, PAD : PAD + 48, :]
        base[f, SIDE : SIDE + 48, :] = pltpu.roll(fine, (120 - 16 * f) % 128, 1)
        value = jnp.where(strip_one, gather_lanes(medium, index), own_ref[f, MID : MID + 32, :])
        base[f, MID + 24 : MID + 32, :] = value[24:32]
        base[f, MID : MID + 24, :] = jnp.where(
            strip_none[0:24], gather_lanes(coarse, index[0:24]), value[0:24]
        )

    def swapped(value):
        return gather_lanes(value, jnp.where(p8 < 48, p8 + 80, jnp.where(p8 < 80, p8, p8 - 80)))

    def turn(slot, value):
        value = value.T
        turned[slot, TPAD : TPAD + 128, :] = value
        turned[slot, TPAD - 8 : TPAD, :] = swapped(value[120:128])
        turned[slot, TPAD + 128 : TPAD + 136, :] = swapped(value[0:8])

    chunks = [PAD + 16 * c for c in range(8)]

    def primitives():
        for row in chunks:
            rows = slice(row, row + 16)
            inverse = 1.0 / base[0, rows, :]
            for i in range(3):
                prim[i, rows, :] = base[1 + i, rows, :] * inverse
            prim[3, rows, :] = 0.5 * (base[6, rows, :] + base[6, row + 1 : row + 17, :])
        for rows in row_sets:
            faces = [base[5, row : row + 8, :] for row in rows]
            for row, face, other in zip(rows, faces, beside_cols(faces, False)):
                prim[4, row : row + 8, :] = 0.5 * (face + other)
        sources = [(base, 0), (prim, 0), (prim, 1), (prim, 2), (prim, 3), (base, 4), (base, 5)]
        for slot, (ref, i) in enumerate(sources):
            turn(slot, ref[i, PAD : PAD + 128, :])

    def sweep(items, lefts, row, count, normal):
        def at(item, step):
            ref, i = item
            return ref[i, row + step : row + step + count, :]

        left, right = [], []
        for i, item in enumerate(items):
            value = at(item, 0)
            slope = 0.5 * minmod(value - at(item, -1), at(item, 1) - value)
            lefts[i, row : row + count, :] = value + slope
            if normal is not None:
                left.append(lefts[i, row - 1 : row - 1 + count, :])
                right.append(value - slope)
        if normal is None:
            return None
        return riemann(left, right, at(normal, 0))

    def sweep_x():
        items = [(turned, i) for i in range(6)]
        sweep(items, leftx, TPAD - 8, 8, None)
        for row in range(TPAD, TPAD + 136, 8):
            count = min(8, TPAD + 136 - row)
            flux = sweep(items, leftx, row, count, (turned, 6))
            for i, value in enumerate(flux):
                fluxx[i, row : row + count, :] = value
        gx[PAD : PAD + 128, :] = fluxx[4, TPAD : TPAD + 128, :].T
        for i, n in enumerate((0, 1, 2, 3, 5)):
            value = fluxx[n, TPAD + 1 : TPAD + 129, :] - fluxx[n, TPAD : TPAD + 128, :]
            diffx[i, PAD : PAD + 128, :] = value.T

    def sweep_y(last):
        items = [(base, 0), (prim, 1), (prim, 0), (prim, 2), (prim, 4), (base, 4)]
        for row in range(PAD, PAD + 128, 8):
            flux = sweep(items, lefty, row, 8, (base, 6))
            for i, n in enumerate((0, 2, 1, 3, 5, 4)):
                if i == 5 or row < SIDE or not last:
                    fluxy[i, row : row + 8, :] = flux[n]

    def beside_cols(parts, back):
        parts = [pltpu.roll(part, 1 if back else 127, 1) for part in parts]
        edge_lane = p8 == (0 if back else 127)
        return [
            jnp.where(edge_lane, parts[1], parts[0]),
            jnp.where(edge_lane, parts[0], parts[1]),
        ] + parts[2:]

    row_sets = [
        (PAD + 8 * c, SIDE + 8 * c) + ((MID + 8 * c,) if c < 4 else ()) for c in range(6)
    ]

    def edges():
        for rows in row_sets:
            shifted = beside_cols([fluxy[5, row : row + 8, :] for row in rows], True)
            for row, other in zip(rows, shifted):
                value = (fluxy[5, row : row + 8, :] + other) - (
                    gx[row : row + 8, :] + gx[row - 1 : row + 7, :]
                )
                edge[row : row + 8, :] = 0.125 * value

    def correct():
        value = edge[MID : MID + 32, :]
        values = (value, pltpu.roll(value, 127, 1))
        for step in range(2):
            finest = corner[step]
            coarse = (p32 + step >= 72) & (p32 + step < 120)
            halved_two = down_two(edge, (PAD, SIDE), False, False, step)
            halved_one = down_one(edge, MID, False, False, step)
            value = jnp.where((finest == 2) & ~coarse, halved_two, values[step])
            fixed[step, 0:32, :] = jnp.where((finest >= 1) & coarse, halved_one, value)

    def is_own(row):
        return PAD + 8 <= row < PAD + 40 or MID + 8 <= row < MID + 24

    def update_cells(i, last):
        for rows in row_sets:
            for k, row in enumerate(rows):
                if last and not is_own(row):
                    continue
                part = slice(row, row + 8)
                change = diffx[i, part, :] + (fluxy[i, row + 1 : row + 9, :] - fluxy[i, part, :])
                win[i, part, :] = base[i, part, :] - 0.5 * ratios[k] * change

    def update_faces(last):
        for rows in row_sets:
            values = [edge[row : row + 8, :] for row in rows[:2]]
            above = [edge[row + 1 : row + 9, :] for row in rows[:2]]
            others = beside_cols(values, False)
            for row in rows[2:]:
                first = row - MID
                values.append(fixed[0, first : first + 8, :])
                above.append(fixed[0, first + 1 : first + 9, :])
                others.append(fixed[1, first : first + 8, :])
            for row, ratio, value, up, other in zip(rows, ratios, values, above, others):
                if last and not is_own(row):
                    continue
                part = slice(row, row + 8)
                win[5, part, :] = base[5, part, :] - ratio * (up - value)
                win[6, part, :] = base[6, part, :] + ratio * (other - value)

    ratios = (STEP_SIZE, STEP_SIZE, jnp.where(is_coarse, STEP_SIZE / 4, STEP_SIZE / 2))

    def shared(fields):
        share_levels(win, base, lev, (0, 80), fields)

    def finish(fields):
        zero = jnp.zeros((8, COLS), F32)
        for f in fields:
            for c in range(4):
                value = win[f, PAD + 8 + 8 * c : PAD + 16 + 8 * c, :]
                if c < 2:
                    medium = win[f, MID + 8 + 8 * c : MID + 16 + 8 * c, :]
                    coarse = pltpu.roll(medium, 48, 1) if c == 0 else zero
                    lower = jnp.where(own_level == 1, medium, coarse)
                    value = jnp.where(own_level == 2, value, lower)
                used = p8 < jnp.where(own_level == 2, 128, jnp.where(own_level == 1, 64, 32))
                used = used & (own_level >= (0, 1, 2, 2)[c])
                blend = 0.5 * (fields_ref[f, 8 * c : 8 * c + 8, :] + value)
                result[f, 8 * c : 8 * c + 8, :] = jnp.where(used, blend, 0.0)
            pltpu.make_async_copy(result.at[f], out_ref.at[f], sems.at[f]).start()

    for section in range(2):
        last = section == 1
        then = (shared, finish)[section]
        primitives()
        sweep_y(last)
        sweep_x()
        edges()
        correct()
        update_cells(0, last)
        then((0,))
        update_faces(last)
        update_cells(1, last)
        then((1,))
        then((5, 6))
        for i in range(2, 5):
            update_cells(i, last)
            then((i,))
    for f in range(7):
        pltpu.make_async_copy(result.at[f], out_ref.at[f], sems.at[f]).wait()


def swapped_segs(value, turn):
    size = lax.axis_size("seg")
    starts = (
        [0, *range(3, size - 2, 2)],
        [size - 1, 1, *range(4, size - 2, 2)],
        [2, size - 2] if size > 4 else [2],
    )[turn]
    pairs = [(i, (i + 1) % size) for i in starts]
    return lax.ppermute(value, "seg", pairs + [(j, i) for i, j in pairs])


def swapped_subs(value, turn):
    rows, count = lax.axis_size("seg"), lax.axis_size("sub")
    pairs = []
    for s in range(rows):
        first, stop = ((0, count - 2), (1, count), (count - 2, count))[turn]
        if s == 0:
            first, stop = ((1, count - 1), (0, count), (count - 1, count))[turn]
        for u in range(first, stop, 2):
            a, b = s * count + u, s * count + (u + 1) % count
            pairs += [(a, b), (b, a)]
    return lax.ppermute(value, ("seg", "sub"), pairs)


def on_device(fields, region_levels):
    shape = jax.ShapeDtypeStruct
    params = pltpu.CompilerParams(vmem_limit_bytes=32 * 1024 * 1024)
    third, second, first = (swapped_segs(fields, turn) for turn in (2, 1, 0))
    lev, lev_strips, corner, cols, tile = pl.pallas_call(
        own_kernel,
        out_shape=(
            shape((128, COLS), jnp.int32),
            shape((104, COLS), jnp.int32),
            shape((2, 32, COLS), jnp.int32),
            shape((32, COLS), F32),
            shape(fields.shape, F32),
        ),
        in_specs=[HBM] * 2,
        out_specs=(VMEM,) * 5,
        scratch_shapes=[
            pltpu.VMEM(region_levels.shape[::-1], jnp.int32),
            pltpu.VMEM((24, COLS), jnp.int32),
            pltpu.SemaphoreType.DMA((2,)),
        ],
        compiler_params=params,
    )(*(pltpu.with_memory_space_constraint(x, pltpu.HBM) for x in (region_levels.T, fields)))
    rows = shape((7, 8, COLS), F32)
    windows = shape((7, PAD + 136, COLS), F32)
    packed, below, above, own = pl.pallas_call(
        cols_kernel,
        out_shape=(shape((48, COLS), F32), rows, rows, windows),
        in_specs=[VMEM] * 6,
        out_specs=(VMEM,) * 4,
        scratch_shapes=[pltpu.VMEM(windows.shape, F32)],
        compiler_params=params,
    )(lev, cols, tile, first, third, second)
    end, far, near = (swapped_subs(packed, turn) for turn in (2, 1, 0))
    own = pl.pallas_call(
        rows_kernel,
        out_shape=windows,
        in_specs=[VMEM] * 5,
        out_specs=VMEM,
        input_output_aliases={4: 0},
        scratch_shapes=[pltpu.VMEM((7, PAD + 136, COLS), F32)],
        compiler_params=params,
    )(lev, tile, below, above, own)

    def window(*lead):
        return pltpu.VMEM((*lead, PAD + 136, COLS), F32)

    def across(*lead):
        return pltpu.VMEM((*lead, TPAD + 144, COLS), F32)

    return pl.pallas_call(
        main_kernel,
        out_shape=shape(fields.shape, F32),
        in_specs=[VMEM] * 8,
        out_specs=HBM,
        scratch_shapes=[
            window(7),
            window(7),
            window(5),
            window(6),
            window(6),
            window(),
            window(5),
            window(),
            pltpu.VMEM((2, 40, COLS), F32),
            across(7),
            across(6),
            across(6),
            pltpu.VMEM((112, COLS), F32),
            pltpu.VMEM(fields.shape, F32),
            pltpu.SemaphoreType.DMA((7,)),
        ],
        compiler_params=params,
    )(lev, lev_strips, corner, tile, own, end, far, near)


def solution(mesh):
    placed = (P(None, "seg", "sub"), P())
    return jax.shard_map(
        on_device, mesh=mesh, in_specs=placed, out_specs=P(None, "seg", "sub"), check_vma=False
    )
```
